128 devices in a mesh: wide: 16 (over x, y_lo, core), narrow: 8 (over z, y_hi).
Axes of the slice: x: 4, y: 4 (y_hi: 2, y_lo: 2; y = y_hi * 2 + y_lo), z: 4, core: 2. Of those that a mesh axis runs over, the one named last changes fastest.
Arguments:
- tokens: bfloat16 [16384, 2048], P(('wide', 'narrow')), may hold values from -6 to 6
- cotangent: bfloat16 [16384, 2048], P(('wide', 'narrow')), may hold values from -6 to 6
- doc_lengths: int32 [16, 3], P('wide'), may hold values from 1 to 1022, as said below
- pre_gain: float32 [2048], replicated, may hold values from 0.1 to 1.9
- mid_gain: float32 [2048], replicated, may hold values from 0.1 to 1.9
- query_gain: float32 [128], replicated, may hold values from 0.1 to 1.9
- key_gain: float32 [128], replicated, may hold values from 0.1 to 1.9
- query_weight: bfloat16 [2048, 2048], P(None, 'narrow'), may hold values from -0.125 to 0.125
- key_matrix: bfloat16 [2048, 1024], P(None, 'narrow'), may hold values from -0.125 to 0.125
- value_matrix: bfloat16 [2048, 1024], P(None, 'narrow'), may hold values from -0.125 to 0.125
- output_weight: bfloat16 [2048, 2048], P('narrow'), may hold values from -1 to 1
- gate_weight: bfloat16 [2048, 6144], P(None, 'narrow'), may hold values from -0.125 to 0.125
- up_weight: bfloat16 [2048, 6144], P(None, 'narrow'), may hold values from -0.125 to 0.125
- down_weight: bfloat16 [6144, 2048], P('narrow'), may hold values from -0.078125 to 0.078125
Outputs:
- block_output: bfloat16 [16384, 2048], P(('wide', 'narrow'))
- tokens_grad: bfloat16 [16384, 2048], P(('wide', 'narrow'))
- pregain_grad: float32 [2048], P('wide')
- midgain_grad: float32 [2048], P('wide')
- querygain_grad: float32 [128], P('wide')
- keygain_grad: float32 [128], P('wide')
- query_grad: float32 [2048, 2048], P('wide', 'narrow')
- key_grad: float32 [2048, 1024], P('wide', 'narrow')
- value_grad: float32 [2048, 1024], P('wide', 'narrow')
- output_grad: float32 [2048, 2048], P('narrow', 'wide')
- gate_grad: float32 [2048, 6144], P('wide', 'narrow')
- up_grad: float32 [2048, 6144], P('wide', 'narrow')
- down_grad: float32 [6144, 2048], P('narrow', 'wide')
The draws below stay inside these ranges and needn't reach their ends.
Inputs may be any that keep to these rules, and one draw needn't show every extreme that they name: `doc_lengths`: each row's 3 lengths sum to 1024; in every row one document starts among its first 128 places and ends among its last 128.
All inputs are finite; a program needn't handle non-finite values.
Results may differ from the reference program's by a relative error of at most 0.04.
Values may be sent and summed in bfloat16 or wider, within the bound.
No kernel may reach another device: no remote copies, remote signals or barrier semaphores. Data moves between devices by JAX's collectives and lax.ppermute only.
A program may use at most 192 MiB of HBM per device.

```python
import math
import jax
import jax.numpy as jnp
from jax import lax

MODEL_WIDTH = 2048
QUERY_HEADS = 16
KEY_VALUE_HEADS = 8
HEAD_SIZE = 128
FF = 6144
DOCS = 3
ROW_TOKENS = 1024
ROW_DEV = 128
TOKENS = 16384
N_WIDE = 16


def draw_doc_lengths(key, part):
    key = jax.random.fold_in(key, 7)
    key_short, key_place, key_row = jax.random.split(key, 3)
    shortmax = (ROW_DEV - 1) // (DOCS - 1)
    shorts = jax.random.randint(key_short, (N_WIDE, DOCS), 1, shortmax + 1)
    packed_row = jax.random.randint(key_row, (1, 1), 0, N_WIDE)
    row_ids = jnp.arange(N_WIDE, dtype=jnp.int32)[:, None]
    shorts = jnp.where(row_ids == packed_row, 1, shorts)
    place = jax.random.randint(key_place, (N_WIDE, 1), 0, DOCS)
    columns = jnp.arange(DOCS, dtype=jnp.int32)[None, :]
    shorts = jnp.where(columns == place, 0, shorts)
    longest = ROW_TOKENS - jnp.sum(shorts, axis=1, keepdims=True)
    return jnp.where(columns == place, longest, shorts).astype(jnp.int32)


def levels(stream_key, shape, cuts, smallest, top_value):
    level = 1.0
    for dim, shards_of in cuts:
        steps = jax.random.uniform(jax.random.fold_in(jax.random.fold_in(stream_key, 6), dim), (shards_of,), jnp.float32, smallest / len(cuts), top_value / len(cuts))
        level = level * jnp.repeat(jnp.exp(steps), shape[dim] // shards_of).reshape((-1,) + (1,) * (len(shape) - 1 - dim))
    return level


def scatter_about(rng, extent, deviation, bound, cuts=(), kind=jnp.bfloat16):
    factor_of = levels(rng, extent, cuts, -0.22, 0.18) if cuts else 1.0
    drawn = jax.random.normal(rng, extent, jnp.float32) * deviation * factor_of
    return jnp.minimum(jnp.maximum(drawn, -bound), bound).astype(kind)


def setup_inputs(seed: int = 0) -> dict:
    arg_keys = jax.random.split(jax.random.key(seed), 15)
    return {
        "tokens": scatter_about(arg_keys[0], (TOKENS, MODEL_WIDTH), 1.0, 6.0, ((0, 128),)),
        "cotangent": scatter_about(arg_keys[1], (TOKENS, MODEL_WIDTH), 1.0, 6.0, ((0, 128),)),
        "doc_lengths": draw_doc_lengths(jax.random.fold_in(arg_keys[14], 71), 0),
        "pre_gain": jnp.clip(1.0 + 0.18 * jax.random.normal(arg_keys[3], (MODEL_WIDTH,), jnp.float32), 0.1, 1.9),
        "mid_gain": jnp.clip(1.0 + 0.18 * jax.random.normal(arg_keys[4], (MODEL_WIDTH,), jnp.float32), 0.1, 1.9),
        "query_gain": jnp.clip(1.0 + 0.18 * jax.random.normal(arg_keys[5], (HEAD_SIZE,), jnp.float32), 0.1, 1.9),
        "key_gain": jnp.clip(1.0 + 0.18 * jax.random.normal(arg_keys[6], (HEAD_SIZE,), jnp.float32), 0.1, 1.9),
        "query_weight": scatter_about(arg_keys[7], (MODEL_WIDTH, QUERY_HEADS * HEAD_SIZE), MODEL_WIDTH ** -0.5, 0.125, ((1, 8),)),
        "key_matrix": scatter_about(arg_keys[8], (MODEL_WIDTH, KEY_VALUE_HEADS * HEAD_SIZE), MODEL_WIDTH ** -0.5, 0.125, ((1, 8),)),
        "value_matrix": scatter_about(arg_keys[9], (MODEL_WIDTH, KEY_VALUE_HEADS * HEAD_SIZE), MODEL_WIDTH ** -0.5, 0.125, ((1, 8),)),
        "output_weight": scatter_about(arg_keys[10], (QUERY_HEADS * HEAD_SIZE, MODEL_WIDTH), (QUERY_HEADS * HEAD_SIZE // 64) ** -0.5, 1.0, ((0, 8),)),
        "gate_weight": scatter_about(arg_keys[11], (MODEL_WIDTH, FF), MODEL_WIDTH ** -0.5, 0.125, ((1, 8),)),
        "up_weight": scatter_about(arg_keys[12], (MODEL_WIDTH, FF), MODEL_WIDTH ** -0.5, 0.125, ((1, 8),)),
        "down_weight": scatter_about(arg_keys[13], (FF, MODEL_WIDTH), FF ** -0.5, 0.078125, ((0, 8),)),
    }


norm_eps = 1e-06
rope_base = 1000000.0

@jax.custom_vjp
def reduced_cast(v):
    return lax.optimization_barrier(v.astype(jnp.bfloat16)).astype(jnp.float32)

@jax.custom_vjp
def reduced_return(v):
    return v

def low_keep(v):
    return (reduced_cast(v), None)

def low_pass(kept, grad):
    return (grad,)

def back_keep(v):
    return (v, None)

def back_low(kept, grad):
    return (reduced_cast(grad),)
reduced_cast.defvjp(low_keep, low_pass)
reduced_return.defvjp(back_keep, back_low)

def matrix_product(left, right):
    return jnp.dot(left, right, precision=lax.Precision.HIGHEST, preferred_element_type=jnp.float32)

def rms_apply(values, gain):
    inverse = lax.rsqrt(lax.optimization_barrier(jnp.mean(values * values, axis=-1, keepdims=True)) + norm_eps)
    return values * inverse * gain

def rotary(values, cosine, sine):
    half = values.shape[-1] // 2
    first = values[..., :half]
    second = values[..., half:]
    cos_part = cosine[..., None, :]
    sin_part = sine[..., None, :]
    return jnp.concatenate([first * cos_part - second * sin_part, second * cos_part + first * sin_part], axis=-1)

def row_tables(lengths, row_len, head_dim):
    ends = jnp.cumsum(lengths).astype(jnp.int32)
    starts = (ends - lengths).astype(jnp.int32)
    places = jnp.arange(row_len, dtype=jnp.int32)
    begin = lax.optimization_barrier(jnp.max(jnp.where(starts[None, :] <= places[:, None], starts[None, :], 0), axis=1)).astype(jnp.int32)
    offset = (places - begin).astype(jnp.float32)
    half = head_dim // 2
    freq = jnp.exp(jnp.arange(half, dtype=jnp.float32) * (-2.0 * math.log(rope_base) / head_dim))
    angle = offset[:, None] * freq[None, :]
    return (begin, jnp.cos(angle), jnp.sin(angle))

def attend_row(inputs):
    query_rows, keys, values, begin = inputs
    scale = HEAD_SIZE ** (-0.5)
    grouped_heads = query_rows.reshape(ROW_TOKENS, KEY_VALUE_HEADS, QUERY_HEADS // KEY_VALUE_HEADS, HEAD_SIZE)
    scores = reduced_return(jnp.einsum('sagd,tad->agst', grouped_heads, keys, precision=lax.Precision.HIGHEST)) * scale
    places = jnp.arange(ROW_TOKENS, dtype=jnp.int32)
    visible = (places[None, :] <= places[:, None]) & (places[None, :] >= begin[:, None])
    scores = jnp.where(visible, scores, -1e+30)
    peak = lax.optimization_barrier(jnp.max(scores, axis=-1, keepdims=True))
    expo = jnp.exp(scores - peak)
    weights = reduced_cast(expo / lax.optimization_barrier(jnp.sum(expo, axis=-1, keepdims=True)))
    context = jnp.einsum('agst,tad->sagd', weights, values, precision=lax.Precision.HIGHEST)
    return context.reshape(ROW_TOKENS, QUERY_HEADS * HEAD_SIZE)

def layer(x, pre_gain, mid_gain, query_gain, key_gain, query_weight, key_matrix, value_matrix, output_weight, gate_weight, up_weight, down_weight, begin, cosine, sine):
    normed_before = reduced_cast(rms_apply(x, pre_gain))
    query_raw = reduced_return(matrix_product(normed_before, query_weight)).reshape(N_WIDE, ROW_TOKENS, QUERY_HEADS, HEAD_SIZE)
    unrotated_key = reduced_return(matrix_product(normed_before, key_matrix)).reshape(N_WIDE, ROW_TOKENS, KEY_VALUE_HEADS, HEAD_SIZE)
    value_reduced = reduced_cast(reduced_return(matrix_product(normed_before, value_matrix))).reshape(N_WIDE, ROW_TOKENS, KEY_VALUE_HEADS, HEAD_SIZE)
    query_rot = reduced_cast(rotary(rms_apply(query_raw, query_gain), cosine, sine))
    key_rot = reduced_cast(rotary(rms_apply(unrotated_key, key_gain), cosine, sine))
    context = lax.map(jax.checkpoint(attend_row), (query_rot, key_rot, value_reduced, begin))
    context = reduced_cast(reduced_return(context.reshape(TOKENS, QUERY_HEADS * HEAD_SIZE)))
    hidden = x + reduced_return(matrix_product(context, output_weight))
    mid_normed = reduced_cast(rms_apply(hidden, mid_gain))
    gate = reduced_return(matrix_product(mid_normed, gate_weight))
    upper = reduced_return(matrix_product(mid_normed, up_weight))
    product = reduced_cast(jax.nn.silu(gate) * upper)
    return hidden + reduced_return(matrix_product(product, down_weight))

def reference(tokens, cotangent, doc_lengths, pre_gain, mid_gain, query_gain, key_gain, query_weight, key_matrix, value_matrix, output_weight, gate_weight, up_weight, down_weight):
    begin, cosine, sine = jax.vmap(lambda lengths: row_tables(lengths, ROW_TOKENS, HEAD_SIZE))(doc_lengths)
    floats = [item.astype(jnp.float32) for item in (tokens, pre_gain, mid_gain, query_gain, key_gain, query_weight, key_matrix, value_matrix, output_weight, gate_weight, up_weight, down_weight)]

    def forward(*params):
        return layer(*params, begin, cosine, sine)
    output, pull = jax.vjp(forward, *floats)
    grads = pull(cotangent.astype(jnp.float32))
    return (output.astype(jnp.bfloat16), grads[0].astype(jnp.bfloat16), grads[1], grads[2], grads[3], grads[4], grads[5], grads[6], grads[7], grads[8], grads[9], grads[10], grads[11])
```

```python
import math

import jax
import jax.numpy as jnp
from jax import lax
from jax.experimental import pallas as pl
from jax.experimental.pallas import tpu as pltpu
from jax.sharding import Mesh
from jax.sharding import PartitionSpec as P

NARROW = ("z", "yhi")
WIDE = ("x", "ylo", "core")
ALL = WIDE + NARROW

EPS = 1e-06
ROPE_BASE = 1000000.0
LOG2E = math.log2(math.e)
F32 = jnp.float32
BF16 = jnp.bfloat16


def dot(a, b, ca, cb):
    return lax.dot_general(a, b, (((ca,), (cb,)), ((), ())), preferred_element_type=F32)


def gather_z(piece):
    copies = jnp.broadcast_to(piece, (4, *piece.shape))
    out = lax.all_to_all(copies, "z", split_axis=0, concat_axis=0, tiled=True)
    return out.reshape(-1, piece.shape[-1])


def scatter_z(partial):
    pieces = partial.reshape(4, -1, partial.shape[-1])
    out = lax.all_to_all(pieces, "z", split_axis=0, concat_axis=0, tiled=True)
    return out.astype(F32).sum(axis=0)


def swap(v, axis):
    return lax.ppermute(v, axis, [(0, 1), (1, 0)])


def cross(v):
    return lax.ppermute(v, ("ylo", "yhi"), [(0, 3), (3, 0), (1, 2), (2, 1)])


def partner_weights(ordered):
    x = lax.axis_index("x")
    piece = lax.dynamic_slice_in_dim(ordered[:1024], x * 256, 256, 0)
    first = lax.all_gather(cross(piece), "x", axis=0, tiled=True)
    second = swap(first, "core")
    return jnp.concatenate([first, second], axis=0)


def wide_sum(keep, send):
    c = keep.shape[1] // 2
    got = swap(send, "core")
    half = (keep.astype(F32) + got.astype(F32)).astype(BF16)
    quarter = lax.psum_scatter(half, "x", scatter_dimension=0, tiled=True).reshape(2, 128, 2 * c)
    ylo = lax.axis_index("ylo")
    mine = lax.dynamic_index_in_dim(quarter, ylo, 0, keepdims=False)
    other = lax.dynamic_index_in_dim(quarter, 1 - ylo, 0, keepdims=False)
    total = mine[:, :c].astype(F32) + swap(other[:, :c], "ylo").astype(F32)
    total = total + swap(mine[:, c:], "yhi").astype(F32)
    return total + cross(other[:, c:]).astype(F32)


def rope(v, cosine, sine):
    return v * cosine + pltpu.roll(v, 64, 1) * sine


def rope_back(v, cosine, sine):
    return v * cosine - pltpu.roll(v, 64, 1) * sine


def vmem_spec():
    return pl.BlockSpec(memory_space=pltpu.VMEM)


def smem_spec():
    return pl.BlockSpec(memory_space=pltpu.SMEM)


def prep_kernel(raw_ref, cos_ref, sin_ref, qgain_ref, kgain_ref, q_ref, kv_ref):
    cosine, sine = cos_ref[...], sin_ref[...]

    def prep(raw, gain):
        inverse = lax.rsqrt(jnp.mean(raw * raw, axis=1, keepdims=True) + EPS)
        return rope(raw * inverse * gain, cosine, sine).astype(BF16)

    for g in range(2):
        at = 512 * g
        for h in range(2):
            q_ref[:, 256 * g + 128 * h : 256 * g + 128 * (h + 1)] = prep(
                raw_ref[:, at + 128 * h : at + 128 * (h + 1)], qgain_ref[...]
            )
        kv_ref[:, 256 * g : 256 * g + 128] = prep(raw_ref[:, at + 256 : at + 384], kgain_ref[...])
        kv_ref[:, 256 * g + 128 : 256 * g + 256] = raw_ref[:, at + 384 : at + 512].astype(BF16)


def prepare(raw, cosine, sine, qgain, kgain):
    return pl.pallas_call(
        prep_kernel,
        out_shape=(
            jax.ShapeDtypeStruct((512, 512), BF16),
            jax.ShapeDtypeStruct((512, 512), BF16),
        ),
        in_specs=[vmem_spec()] * 5,
        out_specs=[vmem_spec()] * 2,
        compiler_params=pltpu.CompilerParams(vmem_limit_bytes=40 * 2**20),
        cost_estimate=pl.CostEstimate(
            flops=10_000_000, bytes_accessed=4_000_000, transcendentals=10_000
        ),
        name="prepare",
    )(raw, cosine, sine, qgain, kgain)


def place_keys(y, kv_ref, other_ref, k_all, v_all):
    for g in range(2):
        for z in range(4):
            rows = slice(128 * z, 128 * (z + 1))
            at = pl.ds(pl.multiple_of(256 * z + 128 * y, 128), 128)
            bt = pl.ds(pl.multiple_of(256 * z + 128 * (1 - y), 128), 128)
            k_all[g, at, :] = kv_ref[rows, 256 * g : 256 * g + 128]
            v_all[g, at, :] = kv_ref[rows, 256 * g + 128 : 256 * g + 256]
            og = 256 * (1 - g)
            k_all[g, bt, :] = other_ref[rows, og : og + 128]
            v_all[g, bt, :] = other_ref[rows, og + 128 : og + 256]


def seen_by(y, z, begin):
    rows = 256 * (z + 1)
    key = lax.broadcasted_iota(jnp.int32, (rows, 256), 0)
    query = (lax.broadcasted_iota(jnp.int32, (rows, 256), 1) & 127) + (256 * z + 128 * y)
    return (key <= query) & (key >= begin)


def stacked(ref, z, g):
    rows = slice(128 * z, 128 * (z + 1))
    return jnp.concatenate(
        [ref[rows, 256 * g : 256 * g + 128], ref[rows, 256 * g + 128 : 256 * g + 256]], axis=0
    )


def attention_kernel(y_ref, q_ref, kv_ref, other_ref, begin_ref, ctx_ref, lse_ref, k_all, v_all):
    scale2 = 128**-0.5 * LOG2E
    y = y_ref[0]
    place_keys(y, kv_ref, other_ref, k_all, v_all)
    for g in range(2):
        v_t = v_all[g].T
        for z in range(4):
            rows = 256 * (z + 1)
            begin = begin_ref[:, 128 * z : 128 * (z + 1)]
            begin = jnp.concatenate([begin, begin], axis=1)
            s = dot(k_all[g, :rows, :], stacked(q_ref, z, g), 1, 1) * scale2
            s = jnp.where(seen_by(y, z, begin), s, -1e30)
            peak = jnp.max(s, axis=0, keepdims=True)
            expo = jnp.exp2(s - peak)
            total = jnp.sum(expo, axis=0, keepdims=True)
            weights = (expo * (1.0 / total)).astype(BF16)
            ctx = dot(v_t[:, :rows], weights, 1, 0).T.astype(BF16)
            for h in range(2):
                ctx_ref[
                    128 * z : 128 * (z + 1), 256 * g + 128 * h : 256 * g + 128 * (h + 1)
                ] = ctx[128 * h : 128 * (h + 1), :]
            lse_ref[4 * g + z : 4 * g + z + 1, :] = peak + jnp.log2(total)


def attention(y, q, kv, other, begin_row):
    return pl.pallas_call(
        attention_kernel,
        out_shape=(
            jax.ShapeDtypeStruct((512, 512), BF16),
            jax.ShapeDtypeStruct((8, 256), F32),
        ),
        in_specs=[smem_spec()] + [vmem_spec()] * 4,
        out_specs=[vmem_spec()] * 2,
        scratch_shapes=[pltpu.VMEM((2, 1024, 128), BF16), pltpu.VMEM((2, 1024, 128), BF16)],
        compiler_params=pltpu.CompilerParams(vmem_limit_bytes=40 * 2**20),
        cost_estimate=pl.CostEstimate(
            flops=900_000_000, bytes_accessed=3_000_000, transcendentals=1_400_000
        ),
        name="attention",
    )(y, q, kv, other, begin_row)


def head_back(d, raw, gain, cosine, sine):
    dn = rope_back(d, cosine, sine)
    inverse = lax.rsqrt(jnp.mean(raw * raw, axis=1, keepdims=True) + EPS)
    n = raw * inverse
    dgain = jnp.sum(dn * n, axis=0, keepdims=True)
    dn = dn * gain
    draw = inverse * (dn - n * jnp.mean(dn * n, axis=1, keepdims=True))
    return draw.astype(BF16), dgain


def attention_back_kernel(
    y_ref, q_ref, kv_ref, other_ref, begin_ref, lse_ref, dctx_ref, raw_ref, cos_ref, sin_ref,
    qgain_ref, dq_ref, mine_ref, send_ref, dqgain_ref, k_all, v_all, dk_acc, dv_acc, dq_acc,
):
    scale = 128**-0.5
    scale2 = scale * LOG2E
    y = y_ref[0]
    place_keys(y, kv_ref, other_ref, k_all, v_all)
    dk_acc[...] = jnp.zeros_like(dk_acc)
    dv_acc[...] = jnp.zeros_like(dv_acc)
    for g in range(2):
        k_t = k_all[g].T
        for z in range(4):
            rows = 256 * (z + 1)
            begin = begin_ref[:, 128 * z : 128 * (z + 1)]
            begin = jnp.concatenate([begin, begin], axis=1)
            q = stacked(q_ref, z, g)
            dctx = stacked(dctx_ref, z, g)
            s = dot(k_all[g, :rows, :], q, 1, 1) * scale2
            s = s - lse_ref[4 * g + z : 4 * g + z + 1, :]
            probs = jnp.where(seen_by(y, z, begin), jnp.exp2(s), 0.0)
            dprobs = dot(v_all[g, :rows, :], dctx, 1, 1)
            inner = jnp.sum(probs * dprobs, axis=0, keepdims=True)
            dscores = (probs * (dprobs - inner) * scale).astype(BF16)
            dv_acc[g, :rows, :] += dot(probs.astype(BF16), dctx, 1, 0)
            dk_acc[g, :rows, :] += dot(dscores, q, 1, 0)
            dq = dot(k_t[:, :rows], dscores, 1, 0).T
            for h in range(2):
                dq_acc[
                    128 * z : 128 * (z + 1), 256 * g + 128 * h : 256 * g + 128 * (h + 1)
                ] = dq[128 * h : 128 * (h + 1), :]
    dgain = jnp.zeros((1, 128), F32)
    for g in range(2):
        for h in range(2):
            lanes = slice(256 * g + 128 * h, 256 * g + 128 * (h + 1))
            raws = slice(512 * g + 128 * h, 512 * g + 128 * (h + 1))
            d, part = head_back(
                dq_acc[:, lanes], raw_ref[:, raws], qgain_ref[...], cos_ref[...], sin_ref[...]
            )
            dq_ref[:, lanes] = d
            dgain = dgain + part
        for z in range(4):
            rows = slice(128 * z, 128 * (z + 1))
            at = pl.ds(pl.multiple_of(256 * z + 128 * y, 128), 128)
            bt = pl.ds(pl.multiple_of(256 * z + 128 * (1 - y), 128), 128)
            mine_ref[rows, 256 * g : 256 * g + 128] = dk_acc[g, at, :]
            mine_ref[rows, 256 * g + 128 : 256 * g + 256] = dv_acc[g, at, :]
            send_ref[rows, 256 * g : 256 * g + 128] = dk_acc[g, bt, :].astype(BF16)
            send_ref[rows, 256 * g + 128 : 256 * g + 256] = dv_acc[g, bt, :].astype(BF16)
    dqgain_ref[...] = dgain


def attention_back(y, q, kv, other, begin_row, lse, dctx, raw, cosine, sine, qgain):
    return pl.pallas_call(
        attention_back_kernel,
        out_shape=(
            jax.ShapeDtypeStruct((512, 512), BF16),
            jax.ShapeDtypeStruct((512, 512), F32),
            jax.ShapeDtypeStruct((512, 512), BF16),
            jax.ShapeDtypeStruct((1, 128), F32),
        ),
        in_specs=[smem_spec()] + [vmem_spec()] * 10,
        out_specs=[vmem_spec()] * 4,
        scratch_shapes=[
            pltpu.VMEM((2, 1024, 128), BF16),
            pltpu.VMEM((2, 1024, 128), BF16),
            pltpu.VMEM((2, 1024, 128), F32),
            pltpu.VMEM((2, 1024, 128), F32),
            pltpu.VMEM((512, 512), F32),
        ],
        compiler_params=pltpu.CompilerParams(vmem_limit_bytes=40 * 2**20),
        cost_estimate=pl.CostEstimate(
            flops=2_200_000_000, bytes_accessed=7_000_000, transcendentals=1_400_000
        ),
        name="attention_back",
    )(y, q, kv, other, begin_row, lse, dctx, raw, cosine, sine, qgain)


def key_back_kernel(
    mine_ref, got_ref, dq_ref, raw_ref, cos_ref, sin_ref, kgain_ref, draw_ref, dkgain_ref
):
    dgain = jnp.zeros((1, 128), F32)
    for g in range(2):
        at, og = 512 * g, 256 * (1 - g)
        draw_ref[:, at : at + 256] = dq_ref[:, 256 * g : 256 * g + 256]
        dk = mine_ref[:, 256 * g : 256 * g + 128] + got_ref[:, og : og + 128].astype(F32)
        d, part = head_back(
            dk, raw_ref[:, at + 256 : at + 384], kgain_ref[...], cos_ref[...], sin_ref[...]
        )
        draw_ref[:, at + 256 : at + 384] = d
        dgain = dgain + part
        dv = mine_ref[:, 256 * g + 128 : 256 * g + 256] + got_ref[:, og + 128 : og + 256].astype(
            F32
        )
        draw_ref[:, at + 384 : at + 512] = dv.astype(BF16)
    dkgain_ref[...] = dgain


def key_back(mine, got, dq, raw, cosine, sine, kgain):
    return pl.pallas_call(
        key_back_kernel,
        out_shape=(
            jax.ShapeDtypeStruct((512, 1024), BF16),
            jax.ShapeDtypeStruct((1, 128), F32),
        ),
        in_specs=[vmem_spec()] * 7,
        out_specs=[vmem_spec()] * 2,
        compiler_params=pltpu.CompilerParams(vmem_limit_bytes=40 * 2**20),
        cost_estimate=pl.CostEstimate(
            flops=10_000_000, bytes_accessed=6_000_000, transcendentals=10_000
        ),
        name="key_back",
    )(mine, got, dq, raw, cosine, sine, kgain)


def row_tables(lengths):
    ends = jnp.cumsum(lengths)
    starts = ends - lengths
    at = jnp.arange(512, dtype=jnp.int32)
    places = (at // 128) * 256 + at % 128 + lax.axis_index("yhi") * 128
    begin = jnp.max(jnp.where(starts[None, :] <= places[:, None], starts[None, :], 0), axis=1)
    offset = (places - begin).astype(F32)
    freq = jnp.exp(jnp.arange(64, dtype=F32) * (-2.0 * math.log(ROPE_BASE) / 128))
    angle = offset[:, None] * freq[None, :]
    cosine, sine = jnp.cos(angle), jnp.sin(angle)
    return (
        begin,
        jnp.concatenate([cosine, cosine], axis=1),
        jnp.concatenate([-sine, sine], axis=1),
    )


def inverse_rms(v):
    return lax.rsqrt(jnp.mean(v * v, axis=-1, keepdims=True) + EPS)


def norm_back(d, v, inverse, gain):
    n = v * inverse
    dn = d * gain
    return inverse * (dn - n * jnp.mean(dn * n, axis=-1, keepdims=True))


def body(
    tokens, cotangent, doc_lengths, pre_gain, mid_gain, query_gain, key_gain,
    query_weight, key_matrix, value_matrix, output_weight, gate_weight, up_weight, down_weight,
):
    core = lax.axis_index("core")

    def order(v, axis):
        shape = v.shape
        parts = v.reshape(*shape[:axis], 8, 2, 128, *shape[axis + 1 :])
        even = lax.index_in_dim(parts, 0, axis + 1, keepdims=False)
        odd = lax.index_in_dim(parts, 1, axis + 1, keepdims=False)
        first = jnp.where(core == 0, even, odd)
        second = jnp.where(core == 0, odd, even)
        return jnp.concatenate([first, second], axis=axis).reshape(shape)

    def unorder(v):
        parts = v.reshape(v.shape[0], 2, 8, 128)
        first, second = parts[:, 0], parts[:, 1]
        even = jnp.where(core == 0, first, second)
        odd = jnp.where(core == 0, second, first)
        return jnp.stack([even, odd], axis=2).reshape(v.shape)

    x = order(tokens, 1).astype(F32)
    cot_low = order(cotangent, 1)
    cot = cot_low.astype(F32)
    pre_gain_o = order(pre_gain, 0)
    mid_gain_o = order(mid_gain, 0)

    r1 = inverse_rms(x)
    normed = (x * r1 * pre_gain_o).astype(BF16)
    normed_half = gather_z(normed)

    def both(own):
        ordered = order(own, 0)
        return jnp.concatenate([ordered, partner_weights(ordered)], axis=1)

    qkv_weight = both(jnp.concatenate([query_weight, key_matrix, value_matrix], axis=1))
    out = both(output_weight.T)
    gu_weight = both(jnp.concatenate([gate_weight, up_weight], axis=1))
    down = both(down_weight.T)
    begin, cosine, sine = row_tables(doc_lengths[0])
    begin_row = begin[None, :]
    qg, kg = query_gain[None, :], key_gain[None, :]
    y = lax.axis_index("yhi").reshape(1).astype(jnp.int32)

    raw = jnp.dot(normed_half, qkv_weight, preferred_element_type=F32)
    q, kv = prepare(raw, cosine, sine, qg, kg)
    kv_other = swap(kv, "yhi")
    ctx, lse = attention(y, q, kv, kv_other, begin_row)
    cot_half = gather_z(cot_low)
    attended = scatter_z(dot(ctx, out, 1, 1).astype(BF16))
    hidden = x + attended
    r2 = inverse_rms(hidden)
    mid = (hidden * r2 * mid_gain_o).astype(BF16)
    mid_half = gather_z(mid)

    gu = jnp.dot(mid_half, gu_weight, preferred_element_type=F32)
    gate = jnp.concatenate([gu[:, :768], gu[:, 1536:2304]], axis=1)
    up = jnp.concatenate([gu[:, 768:1536], gu[:, 2304:]], axis=1)
    sig = jax.nn.sigmoid(gate)
    silu = gate * sig
    product = (silu * up).astype(BF16)
    dproduct = dot(cot_half, down, 1, 0)
    dgate = (dproduct * up * sig * (1.0 + gate * (1.0 - sig))).astype(BF16)
    dup = (dproduct * silu).astype(BF16)
    dgu = jnp.concatenate([dgate[:, :768], dup[:, :768], dgate[:, 768:], dup[:, 768:]], axis=1)
    dmid = scatter_z(dot(dgu, gu_weight, 1, 1).astype(BF16))
    mixed = scatter_z(dot(product, down, 1, 1).astype(BF16))
    block_output = unorder((hidden + mixed).astype(BF16))

    def weight_grad(a, b):
        send = dot(a[:, 1024:], b, 0, 0).astype(BF16)
        keep = dot(a[:, :1024], b, 0, 0).astype(BF16)
        return wide_sum(keep, send)

    down_grad = weight_grad(cot_half, product).T
    gu_grad = weight_grad(mid_half, dgu)

    dhidden = cot + norm_back(dmid, hidden, r2, mid_gain_o)
    datt_half = gather_z(dhidden.astype(BF16))
    dctx = dot(datt_half, out, 1, 0).astype(BF16)
    dq, dkv_mine, dkv_send, dqgain = attention_back(
        y, q, kv, kv_other, begin_row, lse, dctx, raw, cosine, sine, qg
    )
    draw, dkgain = key_back(dkv_mine, swap(dkv_send, "yhi"), dq, raw, cosine, sine, kg)
    dpre = scatter_z(dot(draw, qkv_weight, 1, 1).astype(BF16))
    out_grad = weight_grad(datt_half, ctx).T
    qkv_grad = weight_grad(normed_half, draw)
    tokens_grad = unorder((dhidden + norm_back(dpre, x, r1, pre_gain_o)).astype(BF16))

    w = (lax.axis_index("x") * 2 + lax.axis_index("ylo")) * 2 + core

    def gain_part(grad, weights, gain):
        total = 0.0
        at = 0
        for weight in weights:
            c = weight.shape[1]
            block = lax.dynamic_slice_in_dim(weight, w * 128, 128, 0).astype(F32)
            total = total + jnp.sum(block * grad[:, at : at + c], axis=1)
            at += c
        return total / lax.dynamic_slice_in_dim(gain, w * 128, 128, 0)

    pre_part = gain_part(qkv_grad, (query_weight, key_matrix, value_matrix), pre_gain)
    mid_part = gain_part(gu_grad, (gate_weight, up_weight), mid_gain)
    heads = jnp.concatenate([dqgain.reshape(16, 8), dkgain.reshape(16, 8)], axis=1)
    heads = lax.all_to_all(heads, WIDE, split_axis=0, concat_axis=0, tiled=True).sum(axis=0)
    line = jnp.concatenate([pre_part, mid_part, heads])
    lines = jnp.broadcast_to(line, (8, line.shape[0]))
    line = lax.all_to_all(lines, NARROW, split_axis=0, concat_axis=0, tiled=True).sum(axis=0)

    return (
        block_output,
        tokens_grad,
        line[:128],
        line[128:256],
        line[256:264],
        line[264:272],
        qkv_grad[:, :256],
        qkv_grad[:, 256:384],
        qkv_grad[:, 384:],
        out_grad,
        gu_grad[:, :768],
        gu_grad[:, 768:],
        down_grad,
    )


def solution(mesh):
    torus = Mesh(mesh.devices.reshape(4, 2, 2, 4, 2), ("x", "ylo", "core", "z", "yhi"))
    return jax.shard_map(
        body,
        mesh=torus,
        in_specs=(
            P(ALL, None),
            P(ALL, None),
            P(WIDE, None),
            P(),
            P(),
            P(),
            P(),
            P(None, NARROW),
            P(None, NARROW),
            P(None, NARROW),
            P(NARROW, None),
            P(None, NARROW),
            P(None, NARROW),
            P(NARROW, None),
        ),
        out_specs=(
            P(ALL, None),
            P(ALL, None),
            P(WIDE),
            P(WIDE),
            P(WIDE),
            P(WIDE),
            P(WIDE, NARROW),
            P(WIDE, NARROW),
            P(WIDE, NARROW),
            P(NARROW, WIDE),
            P(WIDE, NARROW),
            P(WIDE, NARROW),
            P(NARROW, WIDE),
        ),
        check_vma=False,
    )
```

```python
import functools
import math

import jax
import jax.numpy as jnp
from jax import lax
from jax.experimental import pallas as pl
from jax.experimental.pallas import tpu as pltpu
from jax.sharding import Mesh
from jax.sharding import PartitionSpec as P

NARROW = ("z", "yhi")
WIDE = ("x", "ylo", "core")
ALL = WIDE + NARROW
CHIPS = ("x", "ylo", "yhi")

EPS = 1e-06
ROPE_BASE = 1000000.0
LOG2E = math.log2(math.e)
F32 = jnp.float32
BF16 = jnp.bfloat16


def dot(a, b, ca, cb):
    return lax.dot_general(a, b, (((ca,), (cb,)), ((), ())), preferred_element_type=F32)


def swap(v, axis):
    return lax.ppermute(v, axis, [(0, 1), (1, 0)])


def cross(v):
    return lax.ppermute(v, ("ylo", "yhi"), [(0, 3), (3, 0), (1, 2), (2, 1)])


def shift(v, axis, by):
    return lax.ppermute(v, axis, [(i, (i + by) % 4) for i in range(4)])


def shift_x(v, by):
    return shift(v, "x", by)


def neighbours_z(piece):
    return shift(piece, "z", 1), shift(piece, "z", -1)


def far_z(left, right):
    return shift(left[:64], "z", 1), shift(right[64:], "z", -1)


def gather_z(piece):
    left, right = neighbours_z(piece)
    return piece, left, right, *far_z(left, right)


def gather_z_directly(piece):
    far = shift(piece, "z", 2)
    return piece, shift(piece, "z", 1), shift(piece, "z", -1), far


def scatter_far(terms):
    return shift(terms[3], "z", 1), shift(terms[4], "z", -1)


def scatter_near(info, terms, far):
    to_right, to_left = relay(info, terms, far)
    return terms[0], shift(to_right, "z", 1), shift(to_left, "z", -1)


def together(*values):
    return lax.optimization_barrier(values)


def vmem_spec():
    return pl.BlockSpec()


def smem_spec():
    return pl.BlockSpec(memory_space=pltpu.SMEM)


def params():
    return pltpu.CompilerParams(vmem_limit_bytes=58 * 2**20)


def shape(*dims, kind=BF16):
    return jax.ShapeDtypeStruct(dims, kind)


def lanes_of(info, c, t, ylo, turned):
    core = info[0] if c == 0 else 1 - info[0]
    tile = (info[1] + t) & 3 if turned else t
    return pl.ds(pl.multiple_of(((tile * 2 + ylo) * 2 + core) * 128, 128), 128)


def place(info, pieces, dst):
    z = info[3]

    def rows(by, first, count):
        return pl.ds(pl.multiple_of(((z + by) & 3) * 128 + first, 64), count)

    own, left, right, far_0, far_1 = pieces
    dst[rows(0, 0, 128), :] = own[...]
    dst[rows(3, 0, 128), :] = left[...]
    dst[rows(1, 0, 128), :] = right[...]
    dst[rows(2, 0, 64), :] = far_0[...]
    dst[rows(2, 64, 64), :] = far_1[...]


def block_of(info, j, how):
    if how != "s":
        return j
    return j - j % 2 + (info[4] if j % 2 == 0 else 1 - info[4])


def turned_rows(info, pieces, core, how, dst):
    own, left, right, far_0, far_1 = pieces
    z = info[3]
    for j in range(8):
        block = 2 * block_of(info, j, how) + core
        lanes = pl.ds(pl.multiple_of(block * 128, 128), 128)
        far = jnp.concatenate([far_0[:, lanes], far_1[:, lanes]], axis=0)
        for by, block in ((0, own[:, lanes]), (3, left[:, lanes]), (1, right[:, lanes]), (2, far)):
            at = pl.ds(pl.multiple_of(((z + by) & 3) * 128, 128), 128)
            dst[128 * j : 128 * (j + 1), at] = block.T


def take_tiles(info, src, dst, turned):
    for c in range(2):
        for t in range(4):
            for ylo in range(2):
                at = (c * 4 + t) * 256 + ylo * 128
                dst[:, at : at + 128] = src[:, lanes_of(info, c, t, ylo, turned)]


def add_rows(info, acc, c, t, value, turned):
    for ylo in range(2):
        acc[lanes_of(info, c, t, ylo, turned), :] += value[ylo * 128 : (ylo + 1) * 128, :]


def add_tile(info, acc, c, t, value, turned):
    for ylo in range(2):
        acc[:, lanes_of(info, c, t, ylo, turned)] += value[:, ylo * 128 : (ylo + 1) * 128]


def inverse_rms(v):
    return lax.rsqrt(jnp.mean(v * v, axis=1, keepdims=True) + EPS)


def norm_back(d, v, inverse, gain):
    n = v * inverse
    dn = d * gain
    return inverse * (dn - n * jnp.mean(dn * n, axis=1, keepdims=True))


def add_up(refs):
    total = refs[0][...].astype(F32)
    for ref in refs[1:]:
        total = total + ref[...].astype(F32)
    return total


def write_terms(info, value, outs):
    for by, out in ((0, outs[0]), (1, outs[1]), (3, outs[2])):
        out[...] = value(at_z(info, by))
    far = value(at_z(info, 2))
    outs[3][...] = far[:64, :]
    outs[4][...] = far[64:, :]


def terms_shape():
    return [shape(128, 2048)] * 3 + [shape(64, 2048)] * 2


def relay_kernel(right_ref, left_ref, far_0, far_1, to_right, to_left):
    to_right[:64, :] = (right_ref[:64, :].astype(F32) + far_0[...].astype(F32)).astype(BF16)
    to_right[64:, :] = right_ref[64:, :]
    to_left[:64, :] = left_ref[:64, :]
    to_left[64:, :] = (left_ref[64:, :].astype(F32) + far_1[...].astype(F32)).astype(BF16)


def relay(info, terms, far):
    return pl.pallas_call(
        relay_kernel,
        out_shape=[shape(128, 2048)] * 2,
        in_specs=[vmem_spec()] * 4,
        out_specs=[vmem_spec()] * 2,
        compiler_params=params(),
        name="relay",
    )(terms[1], terms[2], *far)


def at_z(info, by):
    return pl.ds(pl.multiple_of(((info[3] + by) & 3) * 128, 128), 128)


def small_pieces_kernel(info, q_ref, k_ref, v_ref, o_ref, qkv_ref, out_ref):
    qkv_ref[:, :256] = q_ref[...]
    qkv_ref[:, 256:384] = k_ref[...]
    qkv_ref[:, 384:] = v_ref[...]
    out_ref[...] = o_ref[...].T


def large_pieces_kernel(info, g_ref, u_ref, d_ref, gu_ref, down_ref):
    for i in range(3):
        gu_ref[:, 512 * i : 512 * i + 256] = g_ref[:, 256 * i : 256 * (i + 1)]
        gu_ref[:, 512 * i + 256 : 512 * (i + 1)] = u_ref[:, 256 * i : 256 * (i + 1)]
    down_ref[...] = d_ref[...].T


def pieces_of(kernel, name, info, weights, turned, widths):
    def at(i, info):
        return (2 * info[1] + i) * 2 + info[0]

    def rows(i, info):
        return at(i, info), 0

    def columns(i, info):
        return 0, at(i, info)

    def out(i, info):
        return i, 0

    return pl.pallas_call(
        kernel,
        grid_spec=pltpu.PrefetchScalarGridSpec(
            num_scalar_prefetch=1,
            grid=(2,),
            in_specs=[pl.BlockSpec((128, w.shape[1]), rows) for w in weights]
            + [pl.BlockSpec((turned.shape[0], 128), columns)],
            out_specs=[pl.BlockSpec((128, w), out) for w in widths],
        ),
        out_shape=[shape(256, w) for w in widths],
        compiler_params=params(),
        name=name,
    )(info, *weights, turned)


def first_norm_kernel(tokens_ref, gain_ref, out_ref):
    x = tokens_ref[...].astype(F32)
    normed = (x * inverse_rms(x) * gain_ref[...]).astype(BF16)
    out_ref[...] = normed


def first_norm(tokens, gain):
    return pl.pallas_call(
        first_norm_kernel,
        out_shape=shape(128, 2048),
        in_specs=[vmem_spec()] * 2,
        out_specs=vmem_spec(),
        compiler_params=params(),
        name="first_norm",
    )(tokens, gain)


def mid_norm_kernel(g0, g1, g2, tokens_ref, gain_ref, hidden_ref, out_ref):
    hidden = tokens_ref[...].astype(F32) + add_up((g0, g1, g2))
    hidden_ref[...] = hidden
    normed = (hidden * inverse_rms(hidden) * gain_ref[...]).astype(BF16)
    out_ref[...] = normed


def mid_norm(got, tokens, gain):
    return pl.pallas_call(
        mid_norm_kernel,
        out_shape=(shape(128, 2048, kind=F32), shape(128, 2048)),
        in_specs=[vmem_spec()] * 5,
        out_specs=[vmem_spec()] * 2,
        compiler_params=params(),
        name="mid_norm",
    )(*got, tokens, gain)


def mid_norm_back_kernel(g0, g1, g2, cot_ref, hidden_ref, gain_ref, dhidden_ref, out_ref, dgain_ref):
    hidden = hidden_ref[...]
    inverse = inverse_rms(hidden)
    dmid = add_up((g0, g1, g2))
    dgain_ref[...] = jnp.sum(dmid * (hidden * inverse), axis=0, keepdims=True)
    dhidden = cot_ref[...].astype(F32) + norm_back(dmid, hidden, inverse, gain_ref[...])
    dhidden_ref[...] = dhidden
    out_ref[...] = dhidden.astype(BF16)


def mid_norm_back(got, cot, hidden, gain):
    return pl.pallas_call(
        mid_norm_back_kernel,
        out_shape=(
            shape(128, 2048, kind=F32),
            shape(128, 2048),
            shape(1, 2048, kind=F32),
        ),
        in_specs=[vmem_spec()] * 6,
        out_specs=[vmem_spec()] * 3,
        compiler_params=params(),
        name="mid_norm_back",
    )(*got, cot, hidden, gain)


def first_norm_back_kernel(g0, g1, g2, tokens_ref, dhidden_ref, gain_ref, out_ref):
    x = tokens_ref[...].astype(F32)
    d = norm_back(add_up((g0, g1, g2)), x, inverse_rms(x), gain_ref[...])
    out_ref[...] = (dhidden_ref[...] + d).astype(BF16)


def project_kernel(
    info, a0, a1, a2, a3, a4, wq_ref, wk_ref, wv_ref, p0_ref, p1_ref, cos_ref, sin_ref, qgain_ref,
    kgain_ref, rawq_ref, rawk_ref, q_ref, kv_ref, normed, tiles, raw,
):
    place(info, (a0, a1, a2, a3, a4), normed)
    take_tiles(info, normed, tiles, True)
    raw[:, :256] = dot(normed[...], wq_ref[...], 1, 0)
    raw[:, 256:384] = dot(normed[...], wk_ref[...], 1, 0)
    raw[:, 384:512] = dot(normed[...], wv_ref[...], 1, 0)
    par = None
    for c, p in enumerate((p0_ref, p1_ref)):
        for t in range(4):
            at = (c * 4 + t) * 256
            part = dot(tiles[:, at : at + 256], p[t], 1, 0)
            par = part if par is None else par + part
    raw[:, 512:] = par
    cosine, sine = cos_ref[...], sin_ref[...]

    def prep(v, gain):
        return rope(v * inverse_rms(v) * gain, cosine, sine).astype(BF16)

    for g in range(2):
        at, bt = 512 * g, 256 * g
        for h in range(2):
            v = raw[:, at + 128 * h : at + 128 * (h + 1)]
            rawq_ref[:, bt + 128 * h : bt + 128 * (h + 1)] = v.astype(BF16)
            q_ref[:, bt + 128 * h : bt + 128 * (h + 1)] = prep(v, qgain_ref[...])
        v = raw[:, at + 256 : at + 384]
        rawk_ref[:, 128 * g : 128 * (g + 1)] = v.astype(BF16)
        kv_ref[:, bt : bt + 128] = prep(v, kgain_ref[...])
        kv_ref[:, bt + 128 : bt + 256] = raw[:, at + 384 : at + 512].astype(BF16)


def project(info, pieces, wq, wk, wv, p0, p1, cosine, sine, qgain, kgain):
    return pl.pallas_call(
        project_kernel,
        out_shape=(shape(512, 512), shape(512, 256), shape(512, 512), shape(512, 512)),
        in_specs=[smem_spec()] + [vmem_spec()] * 14,
        out_specs=[vmem_spec()] * 4,
        scratch_shapes=[
            pltpu.VMEM((512, 2048), BF16),
            pltpu.VMEM((512, 2048), BF16),
            pltpu.VMEM((512, 1024), F32),
        ],
        compiler_params=params(),
        name="project",
    )(info, *pieces, wq, wk, wv, p0, p1, cosine, sine, qgain, kgain)


def attended_kernel(info, ctx_ref, own_ref, p0_ref, p1_ref, o0, o1, o2, o3, o4, acc):
    acc[...] = dot(ctx_ref[:, :256], own_ref[...], 1, 0)
    par = ctx_ref[:, 256:]
    for c, p in enumerate((p0_ref, p1_ref)):
        for t in range(4):
            add_tile(info, acc, c, t, dot(par, p[t], 1, 1), True)
    write_terms(info, lambda rows: acc[rows, :].astype(BF16), (o0, o1, o2, o3, o4))


def attended_partial(info, ctx, own, p0, p1):
    return pl.pallas_call(
        attended_kernel,
        out_shape=terms_shape(),
        in_specs=[smem_spec()] + [vmem_spec()] * 4,
        out_specs=[vmem_spec()] * 5,
        scratch_shapes=[pltpu.VMEM((512, 2048), F32)],
        compiler_params=params(),
        name="attended",
    )(info, ctx, own, p0, p1)


def dcontext_kernel(info, d0, d1, d2, d3, d4, own_ref, p0_ref, p1_ref, out_ref, datt, tiles):
    place(info, (d0, d1, d2, d3, d4), datt)
    take_tiles(info, datt, tiles, True)
    out_ref[:, :256] = dot(datt[...], own_ref[...], 1, 1).astype(BF16)
    par = None
    for c, p in enumerate((p0_ref, p1_ref)):
        for t in range(4):
            at = (c * 4 + t) * 256
            part = dot(tiles[:, at : at + 256], p[t], 1, 0)
            par = part if par is None else par + part
    out_ref[:, 256:] = par.astype(BF16)


def dcontext(info, pieces, own, p0, p1):
    return pl.pallas_call(
        dcontext_kernel,
        out_shape=shape(512, 512),
        in_specs=[smem_spec()] + [vmem_spec()] * 8,
        out_specs=vmem_spec(),
        scratch_shapes=[pltpu.VMEM((512, 2048), BF16), pltpu.VMEM((512, 2048), BF16)],
        compiler_params=params(),
        name="dcontext",
    )(info, *pieces, own, p0, p1)


def mlp_kernel(
    info, m0, m1, m2, m3, m4, c0, c1, c2, c3, c4, g_ref, u_ref, d_ref, p0_ref, p1_ref, pd0_ref,
    pd1_ref, product_ref, dgu_ref, o0, o1, o2, o3, o4, mid, cot, mid_t, cot_t, acc, acc_t, w,
):
    step = pl.program_id(0)

    @pl.when(step == 0)
    def start():
        acc[...] = jnp.zeros_like(acc)
        acc_t[...] = jnp.zeros_like(acc_t)
        place(info, (m0, m1, m2, m3, m4), mid)
        place(info, (c0, c1, c2, c3, c4), cot)
        take_tiles(info, mid, mid_t, False)
        take_tiles(info, cot, cot_t, False)

    def middle(gu, dproduct):
        gate, up = gu[:, :256], gu[:, 256:]
        sig = jax.nn.sigmoid(gate)
        silu = gate * sig
        product_ref[...] = (silu * up).astype(BF16)
        dgu_ref[:, :256] = (dproduct * up * sig * (1.0 + gate * (1.0 - sig))).astype(BF16)
        dgu_ref[:, 256:] = (dproduct * silu).astype(BF16)

    @pl.when(step < 3)
    def own_part():
        w[:, :256] = g_ref[...]
        w[:, 256:] = u_ref[...]
        middle(dot(mid[...], w[...], 1, 0), dot(cot[...], d_ref[...], 1, 1))
        acc[...] += dot(w[...], dgu_ref[...], 1, 1)

    @pl.when(step >= 3)
    def par_part():
        w0, w1 = p0_ref[...].reshape(1024, 512), p1_ref[...].reshape(1024, 512)
        gu = dot(mid_t[:, :1024], w0, 1, 0) + dot(mid_t[:, 1024:], w1, 1, 0)
        dproduct = None
        for c, p in enumerate((pd0_ref, pd1_ref)):
            for t in range(4):
                at = (c * 4 + t) * 256
                part = dot(cot_t[:, at : at + 256], p[t], 1, 0)
                dproduct = part if dproduct is None else dproduct + part
        middle(gu, dproduct)
        acc_t[:1024, :] += dot(w0, dgu_ref[...], 1, 1)
        acc_t[1024:, :] += dot(w1, dgu_ref[...], 1, 1)

    @pl.when(step == 5)
    def last():
        for c in range(2):
            for t in range(4):
                at = (c * 4 + t) * 256
                add_rows(info, acc, c, t, acc_t[at : at + 256, :], False)
        write_terms(
            info, lambda rows: acc[:, rows].astype(BF16).T, (o0, o1, o2, o3, o4)
        )


def mlp(info, mid, cot, gate, up, down, p0, p1):
    def own(i):
        return jnp.minimum(i, 2)

    def par(i):
        return jnp.maximum(i - 3, 0)

    def whole(rows):
        return pl.BlockSpec((rows, 2048), lambda i: (0, 0))

    pieces = [whole(128)] * 3 + [whole(64)] * 2
    return pl.pallas_call(
        mlp_kernel,
        grid=(6,),
        out_shape=[shape(512, 1536), shape(512, 3072)] + terms_shape(),
        in_specs=[
            smem_spec(),
            *pieces,
            *pieces,
            pl.BlockSpec((2048, 256), lambda i: (0, own(i))),
            pl.BlockSpec((2048, 256), lambda i: (0, own(i))),
            pl.BlockSpec((256, 2048), lambda i: (own(i), 0)),
            *[pl.BlockSpec((4, 256, 512), lambda i: (0, 0, par(i)))] * 2,
            *[pl.BlockSpec((4, 256, 256), lambda i: (0, 0, 6 + par(i)))] * 2,
        ],
        out_specs=[
            pl.BlockSpec((512, 256), lambda i: (0, i)),
            pl.BlockSpec((512, 512), lambda i: (0, i)),
            *pieces,
        ],
        scratch_shapes=[
            pltpu.VMEM((512, 2048), BF16),
            pltpu.VMEM((512, 2048), BF16),
            pltpu.VMEM((512, 2048), BF16),
            pltpu.VMEM((512, 2048), BF16),
            pltpu.VMEM((2048, 512), F32),
            pltpu.VMEM((2048, 512), F32),
            pltpu.VMEM((2048, 512), BF16),
        ],
        compiler_params=params(),
        name="mlp",
    )(info, *mid, *cot, gate, up, down, p0, p1, p0, p1)


def mixed_kernel(info, product_ref, own_ref, p0_ref, p1_ref, o0, o1, o2, o3, o4, acc):
    t = pl.program_id(0)
    acc[:, pl.ds(pl.multiple_of(t * 512, 512), 512)] = dot(
        product_ref[:, :768], own_ref[...], 1, 0
    )
    par = product_ref[:, 768:]
    for c, p in enumerate((p0_ref, p1_ref)):
        add_tile(info, acc, c, t, dot(par, p[0], 1, 1), False)

    @pl.when(t == 3)
    def write():
        write_terms(info, lambda rows: acc[rows, :].astype(BF16), (o0, o1, o2, o3, o4))


def mixed_partial(info, product, own, p0, p1):
    tile = pl.BlockSpec((1, 256, 768), lambda t: (t, 0, 2))
    return pl.pallas_call(
        mixed_kernel,
        grid=(4,),
        out_shape=terms_shape(),
        in_specs=[
            smem_spec(),
            pl.BlockSpec((512, 1536), lambda t: (0, 0)),
            pl.BlockSpec((768, 512), lambda t: (0, t)),
            tile,
            tile,
        ],
        out_specs=[pl.BlockSpec((n, 2048), lambda t: (0, 0)) for n in (128, 128, 128, 64, 64)],
        scratch_shapes=[pltpu.VMEM((512, 2048), F32)],
        compiler_params=params(),
        name="mixed",
    )(info, product, own, p0, p1)


def dpre_kernel(
    info, mine_ref, got_ref, dq_ref, rawk_ref, cos_ref, sin_ref, kgain_ref, wq_ref, wk_ref, wv_ref,
    p0_ref, p1_ref, a0, a1, a2, a3, a4, gain_ref, mid_ref, dqgain_ref, dkv_ref, gains_ref, o0, o1, o2, o3, o4, acc, normed, low,
):
    place(info, (a0, a1, a2, a3, a4), normed)
    dgain = jnp.zeros((1, 128), F32)
    for g in range(2):
        at, bt, og = 256 * g, 256 * g + 128, 256 * (1 - g)
        dk = mine_ref[:, at:bt] + got_ref[:, og : og + 128].astype(F32)
        raw = rawk_ref[:, 128 * g : 128 * (g + 1)].astype(F32)
        d, part = head_back(dk, raw, kgain_ref[...], cos_ref[...], sin_ref[...])
        dkv_ref[:, at:bt] = d
        dgain = dgain + part
        dv = mine_ref[:, bt : bt + 128] + got_ref[:, og + 128 : og + 256].astype(F32)
        dkv_ref[:, bt : bt + 128] = dv.astype(BF16)
    acc[...] = dot(wq_ref[...], dq_ref[:, :256], 1, 1)
    acc[...] += dot(wk_ref[...], dkv_ref[:, :128], 1, 1) + dot(
        wv_ref[...], dkv_ref[:, 128:256], 1, 1
    )
    par = jnp.concatenate([dq_ref[:, 256:], dkv_ref[:, 256:]], axis=1).T
    for c, p in enumerate((p0_ref, p1_ref)):
        for t in range(4):
            add_rows(info, acc, c, t, dot(p[t], par, 1, 0), True)
    total = jnp.zeros((1, 2048), F32)
    for i in range(4):
        turned = acc[:, 128 * i : 128 * (i + 1)].astype(BF16).T
        part = turned.astype(F32) * normed[128 * i : 128 * (i + 1), :].astype(F32)
        total = total + jnp.sum(part, axis=0, keepdims=True)
        low[128 * i : 128 * (i + 1), :] = turned
    total = total / gain_ref[...]
    for i in range(16):
        row, lanes = slice(i // 2, i // 2 + 1), slice(128 * i, 128 * (i + 1))
        ref = gains_ref.at[jnp.where(info[0] == i % 2, 0, 1)]
        ref[row, :128] = total[:, lanes]
        ref[row, 128:256] = mid_ref[:, lanes]
        ref[row, 256:384] = dqgain_ref[...]
        ref[row, 384:] = dgain
    write_terms(info, lambda rows: low[rows, :], (o0, o1, o2, o3, o4))


def dpre_partial(
    info, mine, got, dq, rawk, cosine, sine, kgain, wq, wk, wv, p0, p1, pieces, *gains
):
    return pl.pallas_call(
        dpre_kernel,
        out_shape=(
            shape(512, 512),
            shape(2, 8, 512, kind=F32),
            *terms_shape(),
        ),
        in_specs=[smem_spec()] + [vmem_spec()] * 20,
        out_specs=[vmem_spec()] * 7,
        scratch_shapes=[
            pltpu.VMEM((2048, 512), F32),
            pltpu.VMEM((512, 2048), BF16),
            pltpu.VMEM((512, 2048), BF16),
        ],
        compiler_params=params(),
        name="dpre",
    )(info, mine, got, dq, rawk, cosine, sine, kgain, wq, wk, wv, p0, p1, *pieces, *gains)


def grad_kernel(info, *refs, plan):
    step = pl.program_id(0)
    turned = refs[-1]
    at_in, at_out = 0, sum(p[3] for p in plan)
    for n, (keep, how, starts, count_in, count_out) in enumerate(plan):
        ins = refs[at_in : at_in + count_in]
        outs = refs[at_out : at_out + count_out]
        at_in, at_out = at_in + count_in, at_out + count_out
        core = info[0] if keep else 1 - info[0]
        ends = starts[1:] + ((plan[n + 1][2][0],) if n + 1 < len(plan) else (None,))
        for job, (start, end) in enumerate(zip(starts, ends)):
            pieces, b = ins[6 * job : 6 * job + 5], ins[6 * job + 5]

            @pl.when(step == start)
            def turn(pieces=pieces, core=core, how=how):
                turned_rows(info, pieces, core, how, turned)

            inside = step >= start if end is None else (step >= start) & (step < end)

            @pl.when(inside)
            def multiply(b=b, keep=keep, how=how, ins=ins, outs=outs, starts=starts, job=job):
                total = dot(turned[...], b[...], 1, 0)
                if not keep:
                    outs[0][...] = total.astype(BF16)
                    return
                got = ins[6 * len(starts)]
                if how == "a":
                    got = ins[6 * len(starts) + (1 if job == len(starts) - 1 else 0)]
                    total = (total + got[...].astype(F32)).astype(BF16)
                    out, yhi = outs[0], info[2]
                    for j in range(8):
                        rows = slice(128 * j, 128 * (j + 1))
                        out[2 * j + yhi, :128, :] = total[rows, :256]
                        out[2 * j + 1 - yhi, :128, :] = total[rows, 256:]
                    if job == 0:
                        gains = (ins[-2][...] + ins[-1][...]).astype(BF16)
                        low = jnp.zeros((14, 256), BF16)
                        for j in range(8):
                            row = gains[j : j + 1, :]
                            row = jnp.concatenate([row[:, :256], row[:, 256:], low], axis=0)
                            out[2 * j, 128:, :] = row
                            out[2 * j + 1, 128:, :] = row
                    else:
                        out[:, 128:, :] = jnp.zeros((16, 16, 256), BF16)
                    return
                for j in range(8):
                    rows = pl.ds(pl.multiple_of(block_of(info, j, how) * 128, 128), 128)
                    block = total[128 * j : 128 * (j + 1), :] + got[rows, :].astype(F32)
                    outs[0][128 * j : 128 * (j + 1), :] = block.astype(BF16)


def grads(info, *bundles):
    plan, in_specs, out_specs, out_shape, args, at = [], [], [], [], [], 0

    def whole(rows):
        return pl.BlockSpec((rows, 2048), lambda i: (0, 0))

    for how, got, jobs, *gains in bundles:
        keep = got is not None
        width = 768 if jobs[0][1].shape[1] % 768 == 0 else 512
        first, starts, before = at, [], len(in_specs)

        def tile_of(start, count):
            return lambda i: (0, jnp.clip(i - start, 0, count - 1))

        for pieces, b in jobs:
            count = b.shape[1] // width
            starts.append(at)
            in_specs += [whole(128)] * 3 + [whole(64)] * 2
            in_specs.append(pl.BlockSpec((512, width), tile_of(at, count)))
            args += [*pieces, b]
            at += count
        tile, columns = tile_of(first, at - first), (at - first) * width
        if keep:
            for part in got if isinstance(got, tuple) else (got,):
                count = part.shape[1] // width
                in_specs.append(pl.BlockSpec((1024, width), tile_of(first, count)))
                args.append(part)
                first += count
            in_specs += [pl.BlockSpec(v.shape, lambda i: (0, 0)) for v in gains]
            args += gains
            first = starts[0]
        if how == "a":
            rows = 144 if gains else 128
            out_shape.append(shape(16, rows, 256 * len(jobs)))
            out_specs.append(
                pl.BlockSpec((16, rows, 256), lambda i, tile=tile: (0, 0, tile(i)[1]))
            )
        else:
            out_shape.append(shape(1024, columns))
            out_specs.append(pl.BlockSpec((1024, width), tile))
        count_out = 1
        plan.append((keep, how, tuple(starts), len(in_specs) - before, count_out))
    out = pl.pallas_call(
        functools.partial(grad_kernel, plan=tuple(plan)),
        grid=(at,),
        out_shape=out_shape,
        in_specs=[smem_spec()] + in_specs,
        out_specs=out_specs,
        scratch_shapes=[pltpu.VMEM((1024, 512), BF16)],
        compiler_params=params(),
        name="grads",
    )(info, *args)
    results, at = [], 0
    for *_, count_out in plan:
        results.append(out[at] if count_out == 1 else list(out[at : at + count_out]))
        at += count_out
    return results[0] if len(results) == 1 else results


def y_parts(quarter):
    c = quarter.shape[1] // 2
    return (
        quarter[:128, :c],
        swap(quarter[128:, :c], "ylo"),
        swap(quarter[:128, c:], "yhi"),
        cross(quarter[128:, c:]),
    )


def to_chips(blocks):
    return lax.all_to_all(blocks, CHIPS, split_axis=0, concat_axis=0, tiled=True)


def last_sum_kernel(*refs):
    out, q, k, v, gate, up, down, block, line = refs[13:]
    blocks = refs[0]
    total = blocks[0].astype(F32)
    for i in range(1, 16):
        total = total + blocks[i].astype(F32)
    out[...] = total[:128, :256].T
    q[...] = total[:128, 256:512]
    k[...] = total[:128, 512:640]
    v[...] = total[:128, 640:]
    line[...] = total[128:136, :256]
    total = add_up(refs[1:5])
    for i in range(3):
        gate[:, 256 * i : 256 * (i + 1)] = total[:, 512 * i : 512 * i + 256]
        up[:, 256 * i : 256 * (i + 1)] = total[:, 512 * i + 256 : 512 * (i + 1)]
    down[...] = add_up(refs[5:9]).T
    block[...] = add_up(refs[9:13]).astype(BF16)


def last_sum(blocks, gu_parts, down_parts, mixed, hidden):
    dims = ((256, 128), (128, 256), (128, 128), (128, 128), (128, 768), (128, 768), (768, 128))
    return pl.pallas_call(
        last_sum_kernel,
        out_shape=[shape(*d, kind=F32) for d in dims]
        + [shape(128, 2048), shape(8, 256, kind=F32)],
        in_specs=[vmem_spec()] * 13,
        out_specs=[vmem_spec()] * 9,
        compiler_params=params(),
        name="last_sum",
    )(blocks, *gu_parts, *down_parts, hidden, *mixed)


def inner_kernel(
    g0, g1, g2, tokens_ref, dhidden_ref, gain_ref, right_ref, left_ref, far_0, far_1,
    grad_ref, to_right, to_left,
):
    first_norm_back_kernel(g0, g1, g2, tokens_ref, dhidden_ref, gain_ref, grad_ref)
    relay_kernel(right_ref, left_ref, far_0, far_1, to_right, to_left)


def inner(got, tokens, dhidden, gain, terms, far):
    return pl.pallas_call(
        inner_kernel,
        out_shape=[shape(128, 2048)] * 3,
        in_specs=[vmem_spec()] * 10,
        out_specs=[vmem_spec()] * 3,
        compiler_params=params(),
        name="inner",
    )(*got, tokens, dhidden, gain, terms[1], terms[2], *far)


def rope(v, cosine, sine):
    return v * cosine + pltpu.roll(v, 64, 1) * sine


def rope_back(v, cosine, sine):
    return v * cosine - pltpu.roll(v, 64, 1) * sine


def place_keys(y, kv_ref, other_ref, k_all, v_all):
    for g in range(2):
        for z in range(4):
            rows = slice(128 * z, 128 * (z + 1))
            at = pl.ds(pl.multiple_of(256 * z + 128 * y, 128), 128)
            bt = pl.ds(pl.multiple_of(256 * z + 128 * (1 - y), 128), 128)
            k_all[g, at, :] = kv_ref[rows, 256 * g : 256 * g + 128]
            v_all[g, at, :] = kv_ref[rows, 256 * g + 128 : 256 * g + 256]
            og = 256 * (1 - g)
            k_all[g, bt, :] = other_ref[rows, og : og + 128]
            v_all[g, bt, :] = other_ref[rows, og + 128 : og + 256]


def seen_by(y, z, begin):
    rows = 256 * (z + 1)
    key = lax.broadcasted_iota(jnp.int32, (rows, 256), 0)
    query = (lax.broadcasted_iota(jnp.int32, (rows, 256), 1) & 127) + (256 * z + 128 * y)
    return (key <= query) & (key >= begin)


def stacked(ref, z, g):
    rows = slice(128 * z, 128 * (z + 1))
    return jnp.concatenate(
        [ref[rows, 256 * g : 256 * g + 128], ref[rows, 256 * g + 128 : 256 * g + 256]], axis=0
    )


def attention_kernel(y_ref, q_ref, kv_ref, other_ref, begin_ref, ctx_ref, lse_ref, k_all, v_all):
    scale2 = 128**-0.5 * LOG2E
    y = y_ref[0]
    place_keys(y, kv_ref, other_ref, k_all, v_all)
    for g in range(2):
        v_t = v_all[g].T
        for z in range(4):
            rows = 256 * (z + 1)
            begin = begin_ref[:, 128 * z : 128 * (z + 1)]
            begin = jnp.concatenate([begin, begin], axis=1)
            s = dot(k_all[g, :rows, :], stacked(q_ref, z, g), 1, 1) * scale2
            s = jnp.where(seen_by(y, z, begin), s, -1e30)
            peak = jnp.max(s, axis=0, keepdims=True)
            expo = jnp.exp2(s - peak)
            total = jnp.sum(expo, axis=0, keepdims=True)
            weights = (expo * (1.0 / total)).astype(BF16)
            ctx = dot(v_t[:, :rows], weights, 1, 0).T.astype(BF16)
            for h in range(2):
                ctx_ref[
                    128 * z : 128 * (z + 1), 256 * g + 128 * h : 256 * g + 128 * (h + 1)
                ] = ctx[128 * h : 128 * (h + 1), :]
            lse_ref[4 * g + z : 4 * g + z + 1, :] = peak + jnp.log2(total)


def attention(y, q, kv, other, begin_row):
    return pl.pallas_call(
        attention_kernel,
        out_shape=(
            jax.ShapeDtypeStruct((512, 512), BF16),
            jax.ShapeDtypeStruct((8, 256), F32),
        ),
        in_specs=[smem_spec()] + [vmem_spec()] * 4,
        out_specs=[vmem_spec()] * 2,
        scratch_shapes=[pltpu.VMEM((2, 1024, 128), BF16), pltpu.VMEM((2, 1024, 128), BF16)],
        compiler_params=params(),
        name="attention",
    )(y, q, kv, other, begin_row)


def head_back(d, raw, gain, cosine, sine):
    dn = rope_back(d, cosine, sine)
    inverse = lax.rsqrt(jnp.mean(raw * raw, axis=1, keepdims=True) + EPS)
    n = raw * inverse
    dgain = jnp.sum(dn * n, axis=0, keepdims=True)
    dn = dn * gain
    draw = inverse * (dn - n * jnp.mean(dn * n, axis=1, keepdims=True))
    return draw.astype(BF16), dgain


def attention_back_kernel(
    y_ref, q_ref, kv_ref, other_ref, begin_ref, lse_ref, dctx_ref, raw_ref, cos_ref, sin_ref,
    qgain_ref, dq_ref, mine_ref, send_ref, dqgain_ref, k_all, v_all, dk_acc, dv_acc, dq_acc,
):
    scale = 128**-0.5
    scale2 = scale * LOG2E
    y = y_ref[0]
    place_keys(y, kv_ref, other_ref, k_all, v_all)
    dk_acc[...] = jnp.zeros_like(dk_acc)
    dv_acc[...] = jnp.zeros_like(dv_acc)
    for g in range(2):
        k_t = k_all[g].T
        for z in range(4):
            rows = 256 * (z + 1)
            begin = begin_ref[:, 128 * z : 128 * (z + 1)]
            begin = jnp.concatenate([begin, begin], axis=1)
            q = stacked(q_ref, z, g)
            dctx = stacked(dctx_ref, z, g)
            s = dot(k_all[g, :rows, :], q, 1, 1) * scale2
            s = s - lse_ref[4 * g + z : 4 * g + z + 1, :]
            probs = jnp.where(seen_by(y, z, begin), jnp.exp2(s), 0.0)
            dprobs = dot(v_all[g, :rows, :], dctx, 1, 1)
            inner = jnp.sum(probs * dprobs, axis=0, keepdims=True)
            dscores = (probs * (dprobs - inner) * scale).astype(BF16)
            dv_acc[g, :rows, :] += dot(probs.astype(BF16), dctx, 1, 0)
            dk_acc[g, :rows, :] += dot(dscores, q, 1, 0)
            dq = dot(k_t[:, :rows], dscores, 1, 0).T
            for h in range(2):
                dq_acc[
                    128 * z : 128 * (z + 1), 256 * g + 128 * h : 256 * g + 128 * (h + 1)
                ] = dq[128 * h : 128 * (h + 1), :]
    dgain = jnp.zeros((1, 128), F32)
    for g in range(2):
        for h in range(2):
            lanes = slice(256 * g + 128 * h, 256 * g + 128 * (h + 1))
            raw = raw_ref[:, lanes].astype(F32)
            d, part = head_back(
                dq_acc[:, lanes], raw, qgain_ref[...], cos_ref[...], sin_ref[...]
            )
            dq_ref[:, lanes] = d
            dgain = dgain + part
        for z in range(4):
            rows = slice(128 * z, 128 * (z + 1))
            at = pl.ds(pl.multiple_of(256 * z + 128 * y, 128), 128)
            bt = pl.ds(pl.multiple_of(256 * z + 128 * (1 - y), 128), 128)
            mine_ref[rows, 256 * g : 256 * g + 128] = dk_acc[g, at, :]
            mine_ref[rows, 256 * g + 128 : 256 * g + 256] = dv_acc[g, at, :]
            send_ref[rows, 256 * g : 256 * g + 128] = dk_acc[g, bt, :].astype(BF16)
            send_ref[rows, 256 * g + 128 : 256 * g + 256] = dv_acc[g, bt, :].astype(BF16)
    dqgain_ref[...] = dgain


def attention_back(y, q, kv, other, begin_row, lse, dctx, raw, cosine, sine, qgain):
    return pl.pallas_call(
        attention_back_kernel,
        out_shape=(
            jax.ShapeDtypeStruct((512, 512), BF16),
            jax.ShapeDtypeStruct((512, 512), F32),
            jax.ShapeDtypeStruct((512, 512), BF16),
            jax.ShapeDtypeStruct((1, 128), F32),
        ),
        in_specs=[smem_spec()] + [vmem_spec()] * 10,
        out_specs=[vmem_spec()] * 4,
        scratch_shapes=[
            pltpu.VMEM((2, 1024, 128), BF16),
            pltpu.VMEM((2, 1024, 128), BF16),
            pltpu.VMEM((2, 1024, 128), F32),
            pltpu.VMEM((2, 1024, 128), F32),
            pltpu.VMEM((512, 512), F32),
        ],
        compiler_params=params(),
        name="attention_back",
    )(y, q, kv, other, begin_row, lse, dctx, raw, cosine, sine, qgain)


def row_tables(lengths):
    ends = jnp.cumsum(lengths)
    starts = ends - lengths
    at = jnp.arange(512, dtype=jnp.int32)
    places = (at // 128) * 256 + at % 128 + lax.axis_index("yhi") * 128
    begin = jnp.max(jnp.where(starts[None, :] <= places[:, None], starts[None, :], 0), axis=1)
    offset = (places - begin).astype(F32)
    freq = jnp.exp(jnp.arange(64, dtype=F32) * (-2.0 * math.log(ROPE_BASE) / 128))
    angle = offset[:, None] * freq[None, :]
    cosine, sine = jnp.cos(angle), jnp.sin(angle)
    return (
        begin,
        jnp.concatenate([cosine, cosine], axis=1),
        jnp.concatenate([-sine, sine], axis=1),
    )


def body(
    tokens, cotangent, doc_lengths, pre_gain, mid_gain, query_gain, key_gain,
    query_weight, key_matrix, value_matrix, output_weight, gate_weight, up_weight, down_weight,
):
    info = jnp.stack([lax.axis_index(name) for name in ("core", "x", "yhi", "z", "ylo")])
    info = info.astype(jnp.int32)
    y = info[2:3]
    pre_row, mid_row = pre_gain[None, :], mid_gain[None, :]
    qg, kg = query_gain[None, :], key_gain[None, :]

    qkv_piece, out_piece = pieces_of(
        small_pieces_kernel,
        "small_pieces",
        info,
        (query_weight, key_matrix, value_matrix),
        output_weight,
        (512, 256),
    )
    normed = first_norm(tokens, pre_row)
    normed, qkv_piece, out_piece = together(normed, qkv_piece, out_piece)
    gu_piece, down_piece = pieces_of(
        large_pieces_kernel, "large_pieces", info, (gate_weight, up_weight), down_weight, (1536, 768)
    )
    normed = gather_z_directly(normed)
    tile, out_tile, gu_piece, down_piece = together(
        cross(qkv_piece), cross(out_piece), gu_piece, down_piece
    )

    def x_tiles(tile):
        return [tile, shift_x(tile, -1), shift_x(tile, -2), shift_x(tile, 1)]

    begin, cosine, sine = row_tables(doc_lengths[0])
    begin_row = begin[None, :]
    *parts, cosine, sine, gu_piece, down_piece = together(
        *x_tiles(tile), *normed, cosine, sine, cross(gu_piece), down_piece
    )
    tiles, (normed, left, right, far) = parts[:4], parts[4:]
    normed = (normed, left, right, far[:64], far[64:])
    qkv_0 = jnp.stack(tiles)
    qkv_0, qkv_1, out_tile = together(qkv_0, swap(qkv_0, "core"), out_tile)

    qkv = (query_weight, key_matrix, value_matrix, qkv_0, qkv_1)
    rawq, rawk, q, kv = project(info, normed, *qkv, cosine, sine, qg, kg)
    kv, down_piece, out_tile, left, right = together(
        kv, cross(down_piece), out_tile, *neighbours_z(cotangent)
    )
    mlp_0 = lax.all_gather(
        jnp.concatenate([gu_piece, down_piece], axis=1), "x", axis=0, tiled=False
    )
    kv_other, far, *tiles = together(
        swap(kv, "yhi"), shift(cotangent, "z", 2), *x_tiles(out_tile)
    )
    cot = (cotangent, left, right, far[:64], far[64:])
    out_0 = jnp.stack(tiles)
    out_1 = swap(out_0, "core")
    ctx, lse = attention(y, q, kv, kv_other, begin_row)
    terms = attended_partial(info, ctx, output_weight, out_0, out_1)
    got = scatter_near(info, terms, together(*scatter_far(terms)))
    g0, g1, g2, mlp_0 = together(*got, mlp_0)
    hidden, mid = mid_norm((g0, g1, g2), tokens, mid_row)
    left, right, mlp_1 = together(*neighbours_z(mid), swap(mlp_0, "core"))
    mid = (mid, left, right, *far_z(left, right))
    product, dgu, *terms = mlp(info, mid, cot, gate_weight, up_weight, down_weight, mlp_0, mlp_1)
    product, dgu, *terms = together(product, dgu, *terms)
    gu_jobs, down_jobs = [(mid, dgu)], [(cot, product)]
    far_0, far_1, gu_send = together(*scatter_far(terms), grads(info, (None, None, gu_jobs)))
    gu_got = swap(gu_send, "core")
    got = scatter_near(info, terms, (far_0, far_1))
    gu_half = grads(info, ("s", gu_got, gu_jobs))
    g0, g1, g2, gu_half = together(*got, gu_half)
    gu_quarter = lax.psum_scatter(gu_half, "x", scatter_dimension=0, tiled=True)
    dhidden, datt, mid_part = mid_norm_back((g0, g1, g2), cotangent, hidden, mid_row)
    mixed = mixed_partial(info, product, down_weight, mlp_0, mlp_1)
    left, right, *mixed = together(*neighbours_z(datt), *mixed)
    far_0, far_1, down_send = together(
        *far_z(left, right), grads(info, (None, None, down_jobs))
    )
    datt = (datt, left, right, far_0, far_1)
    dctx = dcontext(info, datt, output_weight, out_0, out_1)
    down_got = swap(down_send, "core")
    dq, dkv_mine, dkv_send, dqgain = attention_back(
        y, q, kv, kv_other, begin_row, lse, dctx, rawq, cosine, sine, qg
    )
    dq, dkv_mine, dkv_send, down_got = together(dq, dkv_mine, dkv_send, down_got)
    oq_jobs = [(datt, ctx), (normed, dq)]
    down_half, oq_send = grads(info, ("s", down_got, down_jobs), (None, None, oq_jobs))
    dkv_got, mixed_far_0, mixed_far_1, oq_send, down_half = together(
        swap(dkv_send, "yhi"), *scatter_far(mixed), oq_send, down_half
    )
    down_quarter = lax.psum_scatter(down_half, "x", scatter_dimension=0, tiled=True)
    dkv, gains, *terms = dpre_partial(
        info, dkv_mine, dkv_got, dq, rawk, cosine, sine, kg, *qkv, normed, pre_row, mid_part, dqgain
    )
    dkv, gains, oq_got, gu_quarter, *terms = together(
        dkv, gains, swap(oq_send, "core"), gu_quarter, *terms
    )
    kv_jobs = [(normed, dkv)]
    kv_send = grads(info, (None, None, kv_jobs))
    far_0, far_1, kv_send, oq_got, gains_got = together(
        *scatter_far(terms), kv_send, oq_got, swap(gains[1], "core")
    )
    kv_got = swap(kv_send, "core")
    got = scatter_near(info, terms, (far_0, far_1))
    blocks = grads(info, ("a", (oq_got, kv_got), oq_jobs + kv_jobs, gains[0], gains_got))
    g0, g1, g2, blocks, *gu_parts = together(*got, blocks, *y_parts(gu_quarter))
    tokens_grad, to_right, to_left = inner(
        (g0, g1, g2), tokens, dhidden, pre_row, mixed, (mixed_far_0, mixed_far_1)
    )
    mixed = (mixed[0], shift(to_right, "z", 1), shift(to_left, "z", -1))
    out_grad, q_grad, k_grad, v_grad, gate_grad, up_grad, down_grad, block_output, line = last_sum(
        to_chips(blocks), gu_parts, y_parts(down_quarter), mixed, hidden
    )
    line = line + shift(line, "z", 1) + shift(line, "z", -1) + shift(line, "z", 2)
    w = (info[1] * 2 + info[4]) * 2 + info[0]
    heads = lax.dynamic_slice_in_dim(line[1].reshape(2, 128), w * 8, 8, 1)
    return (
        block_output,
        tokens_grad,
        line[0, :128],
        line[0, 128:],
        heads[0],
        heads[1],
        q_grad,
        k_grad,
        v_grad,
        out_grad,
        gate_grad,
        up_grad,
        down_grad,
    )


def solution(mesh):
    torus = Mesh(mesh.devices.reshape(4, 2, 2, 4, 2), ("x", "ylo", "core", "z", "yhi"))
    return jax.shard_map(
        body,
        mesh=torus,
        in_specs=(
            P(ALL, None),
            P(ALL, None),
            P(WIDE, None),
            P(),
            P(),
            P(),
            P(),
            P(None, NARROW),
            P(None, NARROW),
            P(None, NARROW),
            P(NARROW, None),
            P(None, NARROW),
            P(None, NARROW),
            P(NARROW, None),
        ),
        out_specs=(
            P(ALL, None),
            P(ALL, None),
            P(WIDE),
            P(WIDE),
            P(WIDE),
            P(WIDE),
            P(WIDE, NARROW),
            P(WIDE, NARROW),
            P(WIDE, NARROW),
            P(NARROW, WIDE),
            P(WIDE, NARROW),
            P(WIDE, NARROW),
            P(NARROW, WIDE),
        ),
        check_vma=False,
    )
```

```python
import functools
import math

import jax
import jax.numpy as jnp
from jax import lax
from jax.experimental import pallas as pl
from jax.experimental.pallas import tpu as pltpu
from jax.sharding import Mesh
from jax.sharding import PartitionSpec as P

NARROW = ("z", "yhi")
WIDE = ("x", "ylo", "core")
ALL = WIDE + NARROW

EPS = 1e-06
ROPE_BASE = 1000000.0
LOG2E = math.log2(math.e)
F32 = jnp.float32
BF16 = jnp.bfloat16


def dot(a, b, ca, cb):
    return lax.dot_general(a, b, (((ca,), (cb,)), ((), ())), preferred_element_type=F32)


def swap(v, axis):
    return lax.ppermute(v, axis, [(0, 1), (1, 0)])


def cross(v):
    return lax.ppermute(v, ("ylo", "yhi"), [(0, 3), (3, 0), (1, 2), (2, 1)])


def shift(v, axis, by):
    return lax.ppermute(v, axis, [(i, (i + by) % 4) for i in range(4)])


def shift_x(v, by):
    return shift(v, "x", by)


def neighbours_z(piece):
    return shift(piece, "z", 1), shift(piece, "z", -1)


def far_z(left, right):
    return shift(left[:64], "z", 1), shift(right[64:], "z", -1)


def gather_z(piece):
    left, right = neighbours_z(piece)
    return piece, left, right, *far_z(left, right)


def gather_z_directly(piece):
    far = shift(piece, "z", 2)
    return piece, shift(piece, "z", 1), shift(piece, "z", -1), far


def scatter_far(terms):
    return shift(terms[3], "z", 1), shift(terms[4], "z", -1)


def scatter_near(info, terms, far):
    to_right, to_left = relay(info, terms, far)
    return terms[0], shift(to_right, "z", 1), shift(to_left, "z", -1)


def together(*values):
    return lax.optimization_barrier(values)


def vmem_spec():
    return pl.BlockSpec()


def smem_spec():
    return pl.BlockSpec(memory_space=pltpu.SMEM)


def params():
    return pltpu.CompilerParams(vmem_limit_bytes=58 * 2**20)


def shape(*dims, kind=BF16):
    return jax.ShapeDtypeStruct(dims, kind)


def features_of(info, c, t, ylo, turned):
    core = info[0] if c == 0 else 1 - info[0]
    tile = (info[1] + t) & 3 if turned else t
    return pl.ds(pl.multiple_of(((tile * 2 + ylo) * 2 + core) * 128, 128), 128)


def piece_moves(info, pieces, dst):
    own, left, right, far_0, far_1 = pieces
    far = ((info[3] + 2) & 3) * 128
    return [
        (own, dst.at[at_z(info, 0)]),
        (left, dst.at[at_z(info, 3)]),
        (right, dst.at[at_z(info, 1)]),
        (far_0, dst.at[pl.ds(pl.multiple_of(far, 64), 64)]),
        (far_1, dst.at[pl.ds(pl.multiple_of(far + 64, 64), 64)]),
    ]


def tile_moves(info, tiles, lanes, dst, turned):
    moves = []
    for c, tile in enumerate(tiles):
        for t in range(4):
            for ylo in range(2):
                rows = slice(128 * ylo, 128 * (ylo + 1))
                moves.append((tile.at[t, rows, lanes], dst.at[features_of(info, c, t, ylo, turned)]))
    return moves


def start(moves, sems, first):
    copies = [
        pltpu.make_async_copy(a, b, sems.at[first + i]) for i, (a, b) in enumerate(moves)
    ]
    for copy in copies:
        copy.start()
    return copies


def wait(copies):
    for copy in copies:
        copy.wait()


def any_spec():
    return pl.BlockSpec(memory_space=pl.ANY)


def place(info, pieces, dst):
    z = info[3]

    def rows(by, first, count):
        return pl.ds(pl.multiple_of(((z + by) & 3) * 128 + first, 64), count)

    own, left, right, far_0, far_1 = pieces
    dst[rows(0, 0, 128), :] = own[...]
    dst[rows(3, 0, 128), :] = left[...]
    dst[rows(1, 0, 128), :] = right[...]
    dst[rows(2, 0, 64), :] = far_0[...]
    dst[rows(2, 64, 64), :] = far_1[...]


def block_of(info, j, how):
    if how != "s" and how != "x":
        return j
    x = (info[1] + j // 2) & 3 if how == "x" else j // 2
    return x * 2 + (info[4] if j % 2 == 0 else 1 - info[4])


def turned_rows(info, pieces, core, how, dst):
    own, left, right, far_0, far_1 = pieces
    z = info[3]
    for j in range(8):
        block = 2 * block_of(info, j, how) + core
        lanes = pl.ds(pl.multiple_of(block * 128, 128), 128)
        far = jnp.concatenate([far_0[:, lanes], far_1[:, lanes]], axis=0)
        for by, block in ((0, own[:, lanes]), (3, left[:, lanes]), (1, right[:, lanes]), (2, far)):
            at = pl.ds(pl.multiple_of(((z + by) & 3) * 128, 128), 128)
            dst[128 * j : 128 * (j + 1), at] = block.T


def take_tiles(info, src, dst, turned):
    for c in range(2):
        for t in range(4):
            for ylo in range(2):
                at = (c * 4 + t) * 256 + ylo * 128
                dst[:, at : at + 128] = src[:, features_of(info, c, t, ylo, turned)]


def add_tile(info, acc, c, t, value, turned):
    for ylo in range(2):
        acc[:, features_of(info, c, t, ylo, turned)] += value[:, ylo * 128 : (ylo + 1) * 128]


def inverse_rms(v):
    return lax.rsqrt(jnp.mean(v * v, axis=1, keepdims=True) + EPS)


def norm_back(d, v, inverse, gain):
    n = v * inverse
    dn = d * gain
    return inverse * (dn - n * jnp.mean(dn * n, axis=1, keepdims=True))


def add_up(refs):
    total = refs[0][...].astype(F32)
    for ref in refs[1:]:
        total = total + ref[...].astype(F32)
    return total


def write_terms(info, value, outs):
    for by, out in ((0, outs[0]), (1, outs[1]), (3, outs[2])):
        out[...] = value(at_z(info, by))
    far = value(at_z(info, 2))
    outs[3][...] = far[:64, :]
    outs[4][...] = far[64:, :]


def terms_shape():
    return [shape(128, 2048)] * 3 + [shape(64, 2048)] * 2


def relay_kernel(right_ref, left_ref, far_0, far_1, to_right, to_left):
    to_right[:64, :] = (right_ref[:64, :].astype(F32) + far_0[...].astype(F32)).astype(BF16)
    to_right[64:, :] = right_ref[64:, :]
    to_left[:64, :] = left_ref[:64, :]
    to_left[64:, :] = (left_ref[64:, :].astype(F32) + far_1[...].astype(F32)).astype(BF16)


def relay(info, terms, far):
    return pl.pallas_call(
        relay_kernel,
        out_shape=[shape(128, 2048)] * 2,
        in_specs=[vmem_spec()] * 4,
        out_specs=[vmem_spec()] * 2,
        compiler_params=params(),
        name="relay",
    )(terms[1], terms[2], *far)


def at_z(info, by):
    return pl.ds(pl.multiple_of(((info[3] + by) & 3) * 128, 128), 128)


def small_pieces_kernel(info, q_ref, k_ref, v_ref, o_ref, qkv_ref, out_ref):
    qkv_ref[:, :256] = q_ref[...]
    qkv_ref[:, 256:384] = k_ref[...]
    qkv_ref[:, 384:] = v_ref[...]
    out_ref[...] = o_ref[...].T


def large_pieces_kernel(info, g_ref, u_ref, d_ref, gu_ref, down_ref):
    gu_ref[:, :768] = g_ref[...]
    gu_ref[:, 768:] = u_ref[...]
    down_ref[...] = d_ref[...].T


def pieces_of(kernel, name, info, weights, turned, widths):
    def at(i, info):
        return (2 * info[1] + i) * 2 + info[0]

    def rows(i, info):
        return at(i, info), 0

    def columns(i, info):
        return 0, at(i, info)

    def out(i, info):
        return i, 0

    return pl.pallas_call(
        kernel,
        grid_spec=pltpu.PrefetchScalarGridSpec(
            num_scalar_prefetch=1,
            grid=(2,),
            in_specs=[pl.BlockSpec((128, w.shape[1]), rows) for w in weights]
            + [pl.BlockSpec((turned.shape[0], 128), columns)],
            out_specs=[pl.BlockSpec((128, w), out) for w in widths],
        ),
        out_shape=[shape(256, w) for w in widths],
        compiler_params=params(),
        name=name,
    )(info, *weights, turned)


def first_norm_kernel(tokens_ref, gain_ref, out_ref):
    x = tokens_ref[...].astype(F32)
    normed = (x * inverse_rms(x) * gain_ref[...]).astype(BF16)
    out_ref[...] = normed


def first_norm(tokens, gain):
    return pl.pallas_call(
        first_norm_kernel,
        out_shape=shape(128, 2048),
        in_specs=[vmem_spec()] * 2,
        out_specs=vmem_spec(),
        compiler_params=params(),
        name="first_norm",
    )(tokens, gain)


def mid_norm_kernel(g0, g1, g2, tokens_ref, gain_ref, hidden_ref, out_ref):
    hidden = tokens_ref[...].astype(F32) + add_up((g0, g1, g2))
    hidden_ref[...] = hidden
    normed = (hidden * inverse_rms(hidden) * gain_ref[...]).astype(BF16)
    out_ref[...] = normed


def mid_norm(got, tokens, gain):
    return pl.pallas_call(
        mid_norm_kernel,
        out_shape=(shape(128, 2048, kind=F32), shape(128, 2048)),
        in_specs=[vmem_spec()] * 5,
        out_specs=[vmem_spec()] * 2,
        compiler_params=params(),
        name="mid_norm",
    )(*got, tokens, gain)


def mid_norm_back_kernel(g0, g1, g2, cot_ref, hidden_ref, gain_ref, dhidden_ref, out_ref, dgain_ref):
    hidden = hidden_ref[...]
    inverse = inverse_rms(hidden)
    dmid = add_up((g0, g1, g2))
    dgain_ref[...] = jnp.sum(dmid * (hidden * inverse), axis=0, keepdims=True)
    dhidden = cot_ref[...].astype(F32) + norm_back(dmid, hidden, inverse, gain_ref[...])
    dhidden_ref[...] = dhidden
    out_ref[...] = dhidden.astype(BF16)


def mid_norm_back(got, cot, hidden, gain):
    return pl.pallas_call(
        mid_norm_back_kernel,
        out_shape=(
            shape(128, 2048, kind=F32),
            shape(128, 2048),
            shape(1, 2048, kind=F32),
        ),
        in_specs=[vmem_spec()] * 6,
        out_specs=[vmem_spec()] * 3,
        compiler_params=params(),
        name="mid_norm_back",
    )(*got, cot, hidden, gain)


def first_norm_back_kernel(g0, g1, g2, tokens_ref, dhidden_ref, gain_ref, out_ref):
    x = tokens_ref[...].astype(F32)
    d = norm_back(add_up((g0, g1, g2)), x, inverse_rms(x), gain_ref[...])
    out_ref[...] = (dhidden_ref[...] + d).astype(BF16)


def project_kernel(
    info, a0, a1, a2, a3, a4, wq, wk, wv, p0, p1, cos_ref, sin_ref, qgain_ref, kgain_ref,
    rawq_ref, rawk_ref, q_ref, kv_ref, normed, w, raw, sems,
):
    moves = piece_moves(info, (a0, a1, a2, a3, a4), normed)
    moves += [(wq, w.at[:, :256]), (wk, w.at[:, 256:384]), (wv, w.at[:, 384:512])]
    copies = start(moves, sems, 0)
    more = start(tile_moves(info, (p0, p1), slice(None), w.at[:, 512:], True), sems, 8)
    wait(copies)
    raw[:, :512] = dot(normed[...], w[:, :512], 1, 0)
    wait(more)
    raw[:, 512:] = dot(normed[...], w[:, 512:], 1, 0)
    cosine, sine = cos_ref[...], sin_ref[...]

    def prep(v, gain):
        return rope(v * inverse_rms(v) * gain, cosine, sine).astype(BF16)

    for g in range(2):
        at, bt = 512 * g, 256 * g
        for h in range(2):
            v = raw[:, at + 128 * h : at + 128 * (h + 1)]
            rawq_ref[:, bt + 128 * h : bt + 128 * (h + 1)] = v.astype(BF16)
            q_ref[:, bt + 128 * h : bt + 128 * (h + 1)] = prep(v, qgain_ref[...])
        v = raw[:, at + 256 : at + 384]
        rawk_ref[:, 128 * g : 128 * (g + 1)] = v.astype(BF16)
        kv_ref[:, bt : bt + 128] = prep(v, kgain_ref[...])
        kv_ref[:, bt + 128 : bt + 256] = raw[:, at + 384 : at + 512].astype(BF16)


def project(info, pieces, wq, wk, wv, p0, p1, cosine, sine, qgain, kgain):
    return pl.pallas_call(
        project_kernel,
        out_shape=(shape(512, 512), shape(512, 256), shape(512, 512), shape(512, 512)),
        in_specs=[smem_spec()] + [any_spec()] * 10 + [vmem_spec()] * 4,
        out_specs=[vmem_spec()] * 4,
        scratch_shapes=[
            pltpu.VMEM((512, 2048), BF16),
            pltpu.VMEM((2048, 1024), BF16),
            pltpu.VMEM((512, 1024), F32),
            pltpu.SemaphoreType.DMA((24,)),
        ],
        compiler_params=params(),
        name="project",
    )(info, *pieces, wq, wk, wv, p0, p1, cosine, sine, qgain, kgain)


def attended_kernel(info, ctx_ref, own_ref, p0_ref, p1_ref, o0, o1, o2, o3, o4, acc):
    acc[...] = dot(ctx_ref[:, :256], own_ref[...], 1, 0)
    par = ctx_ref[:, 256:]
    for c, p in enumerate((p0_ref, p1_ref)):
        for t in range(4):
            add_tile(info, acc, c, t, dot(par, p[t], 1, 1), True)
    write_terms(info, lambda rows: acc[rows, :].astype(BF16), (o0, o1, o2, o3, o4))


def attended_partial(info, ctx, own, p0, p1):
    return pl.pallas_call(
        attended_kernel,
        out_shape=terms_shape(),
        in_specs=[smem_spec()] + [vmem_spec()] * 4,
        out_specs=[vmem_spec()] * 5,
        scratch_shapes=[pltpu.VMEM((512, 2048), F32)],
        compiler_params=params(),
        name="attended",
    )(info, ctx, own, p0, p1)


def dcontext_kernel(info, d0, d1, d2, d3, d4, own_ref, p0_ref, p1_ref, out_ref, datt, tiles):
    place(info, (d0, d1, d2, d3, d4), datt)
    take_tiles(info, datt, tiles, True)
    out_ref[:, :256] = dot(datt[...], own_ref[...], 1, 1).astype(BF16)
    par = None
    for c, p in enumerate((p0_ref, p1_ref)):
        for t in range(4):
            at = (c * 4 + t) * 256
            part = dot(tiles[:, at : at + 256], p[t], 1, 0)
            par = part if par is None else par + part
    out_ref[:, 256:] = par.astype(BF16)


def dcontext(info, pieces, own, p0, p1):
    return pl.pallas_call(
        dcontext_kernel,
        out_shape=shape(512, 512),
        in_specs=[smem_spec()] + [vmem_spec()] * 8,
        out_specs=vmem_spec(),
        scratch_shapes=[pltpu.VMEM((512, 2048), BF16), pltpu.VMEM((512, 2048), BF16)],
        compiler_params=params(),
        name="dcontext",
    )(info, *pieces, own, p0, p1)


def mlp_kernel(
    info, m0, m1, m2, m3, m4, c0, c1, c2, c3, c4, gate_any, up_any, down_any, p0, p1,
    product_ref, dgu_ref, o0, o1, o2, o3, o4, mid, cot, acc, w, d, par, sems,
):
    moves = piece_moves(info, (m0, m1, m2, m3, m4), mid)
    moves += [(gate_any, w.at[:, :768]), (up_any, w.at[:, 768:])]
    first = start(moves, sems, 0)
    moves = piece_moves(info, (c0, c1, c2, c3, c4), cot) + [(down_any, d)]
    second = start(moves, sems, 7)
    third = start(tile_moves(info, (p0, p1), slice(None), par, False), sems, 13)

    def middle(gu, dproduct, at):
        gate, up = gu[:, :768], gu[:, 768:]
        sig = jax.nn.sigmoid(gate)
        silu = gate * sig
        product_ref[:, at : at + 768] = (silu * up).astype(BF16)
        dgate = (dproduct * up * sig * (1.0 + gate * (1.0 - sig))).astype(BF16)
        dgu_ref[:, 2 * at : 2 * at + 768] = dgate
        dgu_ref[:, 2 * at + 768 : 2 * at + 1536] = (dproduct * silu).astype(BF16)

    wait(first)
    gu = dot(mid[...], w[...], 1, 0)
    wait(second)
    middle(gu, dot(cot[...], d[...], 1, 1), 0)
    acc[...] = dot(w[...], dgu_ref[:, :1536], 1, 1)
    wait(third)
    gu = dot(mid[...], par[:, :1536], 1, 0)
    middle(gu, dot(cot[...], par[:, 1536:], 1, 0), 768)
    acc[...] += dot(par[:, :1536], dgu_ref[:, 1536:], 1, 1)
    write_terms(info, lambda rows: acc[:, rows].astype(BF16).T, (o0, o1, o2, o3, o4))


def mlp(info, mid, cot, gate, up, down, p0, p1):
    return pl.pallas_call(
        mlp_kernel,
        out_shape=[shape(512, 1536), shape(512, 3072)] + terms_shape(),
        in_specs=[smem_spec()] + [any_spec()] * 15,
        out_specs=[vmem_spec()] * 7,
        scratch_shapes=[
            pltpu.VMEM((512, 2048), BF16),
            pltpu.VMEM((512, 2048), BF16),
            pltpu.VMEM((2048, 512), F32),
            pltpu.VMEM((2048, 1536), BF16),
            pltpu.VMEM((768, 2048), BF16),
            pltpu.VMEM((2048, 2304), BF16),
            pltpu.SemaphoreType.DMA((29,)),
        ],
        compiler_params=params(),
        name="mlp",
    )(info, *mid, *cot, gate, up, down, p0, p1)


def mixed_kernel(info, own, p0, p1, product_ref, o0, o1, o2, o3, o4, acc, w, par, sems):
    copies = start([(own, w)], sems, 0)
    lanes = slice(1536, 2304)
    more = start(tile_moves(info, (p0, p1), lanes, par, False), sems, 1)
    wait(copies)
    acc[...] = dot(product_ref[:, :768], w[...], 1, 0)
    wait(more)
    acc[...] += dot(product_ref[:, 768:], par[...], 1, 1)
    write_terms(info, lambda rows: acc[rows, :].astype(BF16), (o0, o1, o2, o3, o4))


def mixed_partial(info, product, own, p0, p1):
    return pl.pallas_call(
        mixed_kernel,
        out_shape=terms_shape(),
        in_specs=[smem_spec()] + [any_spec()] * 3 + [vmem_spec()],
        out_specs=[vmem_spec()] * 5,
        scratch_shapes=[
            pltpu.VMEM((512, 2048), F32),
            pltpu.VMEM((768, 2048), BF16),
            pltpu.VMEM((2048, 768), BF16),
            pltpu.SemaphoreType.DMA((17,)),
        ],
        compiler_params=params(),
        name="mixed",
    )(info, own, p0, p1, product)


def dpre_kernel(
    info, wq, wk, wv, p0, p1, a0, a1, a2, a3, a4, mine_ref, got_ref, dq_ref, rawk_ref, cos_ref,
    sin_ref, kgain_ref, gain_ref, mid_ref, dqgain_ref, dkv_ref, gains_ref, o0, o1, o2, o3, o4,
    acc, normed, low, w, d_all, sems,
):
    copies = start([(wq, w.at[:, :256]), (wk, w.at[:, 256:384]), (wv, w.at[:, 384:512])], sems, 0)
    copies += start(tile_moves(info, (p0, p1), slice(None), w.at[:, 512:], True), sems, 3)
    more = start(piece_moves(info, (a0, a1, a2, a3, a4), normed), sems, 19)
    dgain = jnp.zeros((1, 128), F32)
    for g in range(2):
        at, bt, og = 256 * g, 256 * g + 128, 256 * (1 - g)
        dk = mine_ref[:, at:bt] + got_ref[:, og : og + 128].astype(F32)
        raw = rawk_ref[:, 128 * g : 128 * (g + 1)].astype(F32)
        d, part = head_back(dk, raw, kgain_ref[...], cos_ref[...], sin_ref[...])
        dkv_ref[:, at:bt] = d
        dgain = dgain + part
        dv = mine_ref[:, bt : bt + 128] + got_ref[:, og + 128 : og + 256].astype(F32)
        dkv_ref[:, bt : bt + 128] = dv.astype(BF16)
        d_all[:, 512 * g : 512 * g + 256] = dq_ref[:, at : at + 256]
        d_all[:, 512 * g + 256 : 512 * g + 512] = dkv_ref[:, at : at + 256]
    wait(copies)
    acc[...] = dot(w[...], d_all[...], 1, 1)
    wait(more)
    total = jnp.zeros((1, 2048), F32)
    for i in range(4):
        turned = acc[:, 128 * i : 128 * (i + 1)].astype(BF16).T
        part = turned.astype(F32) * normed[128 * i : 128 * (i + 1), :].astype(F32)
        total = total + jnp.sum(part, axis=0, keepdims=True)
        low[128 * i : 128 * (i + 1), :] = turned
    total = total / gain_ref[...]
    for i in range(16):
        row, lanes = slice(i // 2, i // 2 + 1), slice(128 * i, 128 * (i + 1))
        ref = gains_ref.at[jnp.where(info[0] == i % 2, 0, 1)]
        ref[row, :128] = total[:, lanes]
        ref[row, 128:256] = mid_ref[:, lanes]
        ref[row, 256:384] = dqgain_ref[...]
        ref[row, 384:] = dgain
    write_terms(info, lambda rows: low[rows, :], (o0, o1, o2, o3, o4))


def dpre_partial(
    info, mine, got, dq, rawk, cosine, sine, kgain, wq, wk, wv, p0, p1, pieces, *gains
):
    return pl.pallas_call(
        dpre_kernel,
        out_shape=(shape(512, 512), shape(2, 8, 512, kind=F32), *terms_shape()),
        in_specs=[smem_spec()] + [any_spec()] * 10 + [vmem_spec()] * 10,
        out_specs=[vmem_spec()] * 7,
        scratch_shapes=[
            pltpu.VMEM((2048, 512), F32),
            pltpu.VMEM((512, 2048), BF16),
            pltpu.VMEM((512, 2048), BF16),
            pltpu.VMEM((2048, 1024), BF16),
            pltpu.VMEM((512, 1024), BF16),
            pltpu.SemaphoreType.DMA((24,)),
        ],
        compiler_params=params(),
        name="dpre",
    )(info, wq, wk, wv, p0, p1, *pieces, mine, got, dq, rawk, cosine, sine, kgain, *gains)


def grad_kernel(info, *refs, plan):
    step = pl.program_id(0)
    turned = refs[-1]
    at_in, at_out = 0, sum(p[3] for p in plan)
    for n, (keep, how, starts, count_in, count_out) in enumerate(plan):
        ins = refs[at_in : at_in + count_in]
        outs = refs[at_out : at_out + count_out]
        at_in, at_out = at_in + count_in, at_out + count_out
        core = info[0] if keep else 1 - info[0]
        ends = starts[1:] + ((plan[n + 1][2][0],) if n + 1 < len(plan) else (None,))
        for job, (start, end) in enumerate(zip(starts, ends)):
            pieces, b = ins[6 * job : 6 * job + 5], ins[6 * job + 5]

            @pl.when(step == start)
            def turn(pieces=pieces, core=core, how=how):
                turned_rows(info, pieces, core, how, turned)

            inside = step >= start if end is None else (step >= start) & (step < end)

            @pl.when(inside)
            def multiply(b=b, keep=keep, how=how, ins=ins, outs=outs, starts=starts):
                total = dot(turned[...], b[...], 1, 0)
                if not keep:
                    outs[0][...] = total.astype(BF16)
                    return
                got = ins[6 * len(starts)]
                if how == "y":
                    total = (total + got[...].astype(F32)).astype(BF16)
                    for par in range(2):

                        @pl.when(step == starts[0] + par)
                        def write(par=par):
                            yhi = info[2] if par == 0 else 1 - info[2]
                            for j in range(8):
                                rows = slice(128 * (j // 2), 128 * (j // 2 + 1))
                                out = outs[0].at[2 * (j % 2) + yhi]
                                out[rows, :] = total[128 * j : 128 * (j + 1), :]

                    return
                for j in range(8):
                    block = block_of(info, j, how)
                    rows = pl.ds(pl.multiple_of(block * 128, 128), 128)
                    part = total[128 * j : 128 * (j + 1), :] + got[rows, :].astype(F32)
                    if how == "s":
                        outs[0][128 * j : 128 * (j + 1), :] = part.astype(BF16)
                        continue
                    out, i = outs[j // 2], j % 2
                    out[128 * i : 128 * (i + 1), :] = part.astype(BF16)
                    mine, other = ins[-2], ins[-1]
                    row = mine[pl.ds(block, 1), :] + other[pl.ds(block, 1), :]
                    row = jnp.concatenate([row, jnp.zeros((15, 512), F32)], axis=0)
                    out[256 + 16 * i : 272 + 16 * i, :] = row.astype(BF16)


def grads(info, *bundles):
    plan, in_specs, out_specs, out_shape, args, at = [], [], [], [], [], 0

    def whole(rows):
        return pl.BlockSpec((rows, 2048), lambda i: (0, 0))

    for how, got, jobs, *gains in bundles:
        keep = got is not None
        width = 768 if jobs[0][1].shape[1] % 768 == 0 else 512
        first, starts, before = at, [], len(in_specs)

        def tile_of(start, count):
            return lambda i: (0, jnp.clip(i - start, 0, count - 1))

        for pieces, b in jobs:
            count = b.shape[1] // width
            starts.append(at)
            in_specs += [whole(128)] * 3 + [whole(64)] * 2
            in_specs.append(pl.BlockSpec((512, width), tile_of(at, count)))
            args += [*pieces, b]
            at += count
        tile, columns = tile_of(first, at - first), (at - first) * width
        if keep:
            in_specs.append(pl.BlockSpec((1024, width), tile))
            args.append(got)
            in_specs += [pl.BlockSpec(v.shape, lambda i: (0, 0)) for v in gains]
            args += gains
        count_out = 1
        if how == "y":
            out_shape.append(shape(4, 512, width))
            out_specs.append(pl.BlockSpec((4, 512, width), lambda i: (0, 0, 0)))
        elif how == "x":
            out_shape += [shape(288, width)] * 4
            out_specs += [pl.BlockSpec((288, width), lambda i: (0, 0))] * 4
            count_out = 4
        else:
            out_shape.append(shape(1024, columns))
            out_specs.append(pl.BlockSpec((1024, width), tile))
        plan.append((keep, how, tuple(starts), len(in_specs) - before, count_out))
    out = pl.pallas_call(
        functools.partial(grad_kernel, plan=tuple(plan)),
        grid=(at,),
        out_shape=out_shape,
        in_specs=[smem_spec()] + in_specs,
        out_specs=out_specs,
        scratch_shapes=[pltpu.VMEM((1024, 512), BF16)],
        compiler_params=params(),
        name="grads",
    )(info, *args)
    results, at = [], 0
    for *_, count_out in plan:
        results.append(out[at] if count_out == 1 else list(out[at : at + count_out]))
        at += count_out
    return results[0] if len(results) == 1 else results


def y_parts(quarter):
    c = quarter.shape[1] // 2
    return (
        quarter[:128, :c],
        swap(quarter[128:, :c], "ylo"),
        swap(quarter[:128, c:], "yhi"),
        cross(quarter[128:, c:]),
    )


def x_parts(parts):
    return parts[0], shift_x(parts[1], 1), shift_x(parts[2], 2), shift_x(parts[3], -1)


def y_split_kernel(oq, k0, k1, k2, k3, mine, to_ylo, to_yhi, to_cross, kv):
    kv[...] = add_up((k0, k1, k2, k3))
    for i, out in enumerate((mine, to_ylo, to_yhi, to_cross)):
        other, par = i % 2, i // 2
        rows = slice(128 * other, 128 * (other + 1))
        out[:128, :256] = oq[rows, 256 * par : 256 * par + 256].astype(out.dtype)
        out[:128, 256:512] = oq[rows, 512 + 256 * par : 768 + 256 * par].astype(out.dtype)
        out[:128, 512:] = kv[rows, 256 * par : 256 * par + 256].astype(out.dtype)
        out[128:, :512] = kv[256 + 16 * other : 272 + 16 * other, :].astype(out.dtype)
        out[128:, 512:] = jnp.zeros((16, 256), out.dtype)


def y_split(oq, kv):
    return pl.pallas_call(
        y_split_kernel,
        out_shape=[shape(144, 768, kind=F32)] + [shape(144, 768)] * 3,
        in_specs=[vmem_spec()] * 5,
        out_specs=[vmem_spec()] * 4,
        scratch_shapes=[pltpu.VMEM((288, 512), F32)],
        compiler_params=params(),
        name="y_split",
    )(oq, *kv)


def last_sum_kernel(info, *refs):
    out, q, k, v, gate, up, down, block, pre, mid, qgain, kgain = refs[16:]
    total = add_up(refs[:4])
    out[...] = total[:128, :256].T
    q[...] = total[:128, 256:512]
    k[...] = total[:128, 512:640]
    v[...] = total[:128, 640:]
    pre[...] = total[128:129, :128]
    mid[...] = total[128:129, 128:256]
    w = (info[1] * 2 + info[4]) * 2 + info[0]
    back = (128 - 8 * w) & 127
    qgain[...] = pltpu.roll(total[128:136, 256:384], back, 1)[:1, :8]
    kgain[...] = pltpu.roll(total[128:136, 384:512], back, 1)[:1, :8]
    total = add_up(refs[4:8])
    gate[...] = total[:, :768]
    up[...] = total[:, 768:]
    down[...] = add_up(refs[8:12]).T
    block[...] = add_up(refs[12:16]).astype(BF16)


def last_sum(info, parts, gu_parts, down_parts, mixed, hidden):
    dims = ((256, 128), (128, 256), (128, 128), (128, 128), (128, 768), (128, 768), (768, 128))
    gains = ((1, 128), (1, 128), (1, 8), (1, 8))
    return pl.pallas_call(
        last_sum_kernel,
        out_shape=[shape(*d, kind=F32) for d in dims]
        + [shape(128, 2048)]
        + [shape(*d, kind=F32) for d in gains],
        in_specs=[smem_spec()] + [vmem_spec()] * 16,
        out_specs=[vmem_spec()] * 12,
        compiler_params=params(),
        name="last_sum",
    )(info, *parts, *gu_parts, *down_parts, hidden, *mixed)


def first_norm_back(got, tokens, dhidden, gain):
    return pl.pallas_call(
        first_norm_back_kernel,
        out_shape=shape(128, 2048),
        in_specs=[vmem_spec()] * 6,
        out_specs=vmem_spec(),
        compiler_params=params(),
        name="first_norm_back",
    )(*got, tokens, dhidden, gain)


def rope(v, cosine, sine):
    return v * cosine + pltpu.roll(v, 64, 1) * sine


def rope_back(v, cosine, sine):
    return v * cosine - pltpu.roll(v, 64, 1) * sine


def place_keys(y, kv_ref, other_ref, k_all, v_all):
    for g in range(2):
        for z in range(4):
            rows = slice(128 * z, 128 * (z + 1))
            at = pl.ds(pl.multiple_of(256 * z + 128 * y, 128), 128)
            bt = pl.ds(pl.multiple_of(256 * z + 128 * (1 - y), 128), 128)
            k_all[g, at, :] = kv_ref[rows, 256 * g : 256 * g + 128]
            v_all[g, at, :] = kv_ref[rows, 256 * g + 128 : 256 * g + 256]
            og = 256 * (1 - g)
            k_all[g, bt, :] = other_ref[rows, og : og + 128]
            v_all[g, bt, :] = other_ref[rows, og + 128 : og + 256]


def seen_by(y, z, begin):
    rows = 256 * (z + 1)
    key = lax.broadcasted_iota(jnp.int32, (rows, 256), 0)
    query = (lax.broadcasted_iota(jnp.int32, (rows, 256), 1) & 127) + (256 * z + 128 * y)
    return (key <= query) & (key >= begin)


def stacked(ref, z, g):
    rows = slice(128 * z, 128 * (z + 1))
    return jnp.concatenate(
        [ref[rows, 256 * g : 256 * g + 128], ref[rows, 256 * g + 128 : 256 * g + 256]], axis=0
    )


def attention_kernel(y_ref, q_ref, kv_ref, other_ref, begin_ref, ctx_ref, lse_ref, k_all, v_all):
    scale2 = 128**-0.5 * LOG2E
    y = y_ref[0]
    place_keys(y, kv_ref, other_ref, k_all, v_all)
    for g in range(2):
        v_t = v_all[g].T
        for z in range(4):
            rows = 256 * (z + 1)
            begin = begin_ref[:, 128 * z : 128 * (z + 1)]
            begin = jnp.concatenate([begin, begin], axis=1)
            s = dot(k_all[g, :rows, :], stacked(q_ref, z, g), 1, 1) * scale2
            s = jnp.where(seen_by(y, z, begin), s, -1e30)
            peak = jnp.max(s, axis=0, keepdims=True)
            expo = jnp.exp2(s - peak)
            total = jnp.sum(expo, axis=0, keepdims=True)
            weights = (expo * (1.0 / total)).astype(BF16)
            ctx = dot(v_t[:, :rows], weights, 1, 0).T.astype(BF16)
            for h in range(2):
                ctx_ref[
                    128 * z : 128 * (z + 1), 256 * g + 128 * h : 256 * g + 128 * (h + 1)
                ] = ctx[128 * h : 128 * (h + 1), :]
            lse_ref[4 * g + z : 4 * g + z + 1, :] = peak + jnp.log2(total)


def attention(y, q, kv, other, begin_row):
    return pl.pallas_call(
        attention_kernel,
        out_shape=(
            jax.ShapeDtypeStruct((512, 512), BF16),
            jax.ShapeDtypeStruct((8, 256), F32),
        ),
        in_specs=[smem_spec()] + [vmem_spec()] * 4,
        out_specs=[vmem_spec()] * 2,
        scratch_shapes=[pltpu.VMEM((2, 1024, 128), BF16), pltpu.VMEM((2, 1024, 128), BF16)],
        compiler_params=params(),
        name="attention",
    )(y, q, kv, other, begin_row)


def head_back(d, raw, gain, cosine, sine):
    dn = rope_back(d, cosine, sine)
    inverse = lax.rsqrt(jnp.mean(raw * raw, axis=1, keepdims=True) + EPS)
    n = raw * inverse
    dgain = jnp.sum(dn * n, axis=0, keepdims=True)
    dn = dn * gain
    draw = inverse * (dn - n * jnp.mean(dn * n, axis=1, keepdims=True))
    return draw.astype(BF16), dgain


def attention_back_kernel(
    y_ref, q_ref, kv_ref, other_ref, begin_ref, lse_ref, dctx_ref, raw_ref, cos_ref, sin_ref,
    qgain_ref, dq_ref, mine_ref, send_ref, dqgain_ref, k_all, v_all, dk_acc, dv_acc, dq_acc,
):
    scale = 128**-0.5
    scale2 = scale * LOG2E
    y = y_ref[0]
    place_keys(y, kv_ref, other_ref, k_all, v_all)
    dk_acc[...] = jnp.zeros_like(dk_acc)
    dv_acc[...] = jnp.zeros_like(dv_acc)
    for g in range(2):
        k_t = k_all[g].T
        for z in range(4):
            rows = 256 * (z + 1)
            begin = begin_ref[:, 128 * z : 128 * (z + 1)]
            begin = jnp.concatenate([begin, begin], axis=1)
            q = stacked(q_ref, z, g)
            dctx = stacked(dctx_ref, z, g)
            s = dot(k_all[g, :rows, :], q, 1, 1) * scale2
            s = s - lse_ref[4 * g + z : 4 * g + z + 1, :]
            probs = jnp.where(seen_by(y, z, begin), jnp.exp2(s), 0.0)
            dprobs = dot(v_all[g, :rows, :], dctx, 1, 1)
            inner = jnp.sum(probs * dprobs, axis=0, keepdims=True)
            dscores = (probs * (dprobs - inner) * scale).astype(BF16)
            dv_acc[g, :rows, :] += dot(probs.astype(BF16), dctx, 1, 0)
            dk_acc[g, :rows, :] += dot(dscores, q, 1, 0)
            dq = dot(k_t[:, :rows], dscores, 1, 0).T
            for h in range(2):
                dq_acc[
                    128 * z : 128 * (z + 1), 256 * g + 128 * h : 256 * g + 128 * (h + 1)
                ] = dq[128 * h : 128 * (h + 1), :]
    dgain = jnp.zeros((1, 128), F32)
    for g in range(2):
        for h in range(2):
            lanes = slice(256 * g + 128 * h, 256 * g + 128 * (h + 1))
            raw = raw_ref[:, lanes].astype(F32)
            d, part = head_back(
                dq_acc[:, lanes], raw, qgain_ref[...], cos_ref[...], sin_ref[...]
            )
            dq_ref[:, lanes] = d
            dgain = dgain + part
        for z in range(4):
            rows = slice(128 * z, 128 * (z + 1))
            at = pl.ds(pl.multiple_of(256 * z + 128 * y, 128), 128)
            bt = pl.ds(pl.multiple_of(256 * z + 128 * (1 - y), 128), 128)
            mine_ref[rows, 256 * g : 256 * g + 128] = dk_acc[g, at, :]
            mine_ref[rows, 256 * g + 128 : 256 * g + 256] = dv_acc[g, at, :]
            send_ref[rows, 256 * g : 256 * g + 128] = dk_acc[g, bt, :].astype(BF16)
            send_ref[rows, 256 * g + 128 : 256 * g + 256] = dv_acc[g, bt, :].astype(BF16)
    dqgain_ref[...] = dgain


def attention_back(y, q, kv, other, begin_row, lse, dctx, raw, cosine, sine, qgain):
    return pl.pallas_call(
        attention_back_kernel,
        out_shape=(
            jax.ShapeDtypeStruct((512, 512), BF16),
            jax.ShapeDtypeStruct((512, 512), F32),
            jax.ShapeDtypeStruct((512, 512), BF16),
            jax.ShapeDtypeStruct((1, 128), F32),
        ),
        in_specs=[smem_spec()] + [vmem_spec()] * 10,
        out_specs=[vmem_spec()] * 4,
        scratch_shapes=[
            pltpu.VMEM((2, 1024, 128), BF16),
            pltpu.VMEM((2, 1024, 128), BF16),
            pltpu.VMEM((2, 1024, 128), F32),
            pltpu.VMEM((2, 1024, 128), F32),
            pltpu.VMEM((512, 512), F32),
        ],
        compiler_params=params(),
        name="attention_back",
    )(y, q, kv, other, begin_row, lse, dctx, raw, cosine, sine, qgain)


def row_tables(lengths):
    ends = jnp.cumsum(lengths)
    starts = ends - lengths
    at = jnp.arange(512, dtype=jnp.int32)
    places = (at // 128) * 256 + at % 128 + lax.axis_index("yhi") * 128
    begin = jnp.max(jnp.where(starts[None, :] <= places[:, None], starts[None, :], 0), axis=1)
    offset = (places - begin).astype(F32)
    freq = jnp.exp(jnp.arange(64, dtype=F32) * (-2.0 * math.log(ROPE_BASE) / 128))
    angle = offset[:, None] * freq[None, :]
    cosine, sine = jnp.cos(angle), jnp.sin(angle)
    return (
        begin,
        jnp.concatenate([cosine, cosine], axis=1),
        jnp.concatenate([-sine, sine], axis=1),
    )


def body(
    tokens, cotangent, doc_lengths, pre_gain, mid_gain, query_gain, key_gain,
    query_weight, key_matrix, value_matrix, output_weight, gate_weight, up_weight, down_weight,
):
    info = jnp.stack([lax.axis_index(name) for name in ("core", "x", "yhi", "z", "ylo")])
    info = info.astype(jnp.int32)
    y = info[2:3]
    pre_row, mid_row = pre_gain[None, :], mid_gain[None, :]
    qg, kg = query_gain[None, :], key_gain[None, :]

    qkv_piece, out_piece = pieces_of(
        small_pieces_kernel,
        "small_pieces",
        info,
        (query_weight, key_matrix, value_matrix),
        output_weight,
        (512, 256),
    )
    normed = first_norm(tokens, pre_row)
    normed, qkv_piece, out_piece = together(normed, qkv_piece, out_piece)
    gu_piece, down_piece = pieces_of(
        large_pieces_kernel, "large_pieces", info, (gate_weight, up_weight), down_weight, (1536, 768)
    )
    normed = gather_z(normed)
    tile, out_tile, gu_piece, down_piece = together(
        cross(qkv_piece), cross(out_piece), gu_piece, down_piece
    )

    def x_tiles(tile):
        return [tile, shift_x(tile, -1), shift_x(tile, -2), shift_x(tile, 1)]

    begin, cosine, sine = row_tables(doc_lengths[0])
    begin_row = begin[None, :]
    *parts, cosine, sine, gu_piece, down_piece = together(
        *x_tiles(tile), *normed, cosine, sine, cross(gu_piece), down_piece
    )
    tiles, normed = parts[:4], tuple(parts[4:])
    qkv_0 = jnp.stack(tiles)
    qkv_0, qkv_1, out_tile = together(qkv_0, swap(qkv_0, "core"), out_tile)

    qkv = (query_weight, key_matrix, value_matrix, qkv_0, qkv_1)
    rawq, rawk, q, kv = project(info, normed, *qkv, cosine, sine, qg, kg)
    kv, down_piece, out_tile, left, right = together(
        kv, cross(down_piece), out_tile, *neighbours_z(cotangent)
    )
    mlp_0 = lax.all_gather(
        jnp.concatenate([gu_piece, down_piece], axis=1), "x", axis=0, tiled=False
    )
    kv_other, far, *tiles = together(
        swap(kv, "yhi"), shift(cotangent, "z", 2), *x_tiles(out_tile)
    )
    cot = (cotangent, left, right, far[:64], far[64:])
    out_0 = jnp.stack(tiles)
    out_1 = swap(out_0, "core")
    ctx, lse = attention(y, q, kv, kv_other, begin_row)
    terms = attended_partial(info, ctx, output_weight, out_0, out_1)
    got = scatter_near(info, terms, together(*scatter_far(terms)))
    g0, g1, g2, mlp_0 = together(*got, mlp_0)
    hidden, mid = mid_norm((g0, g1, g2), tokens, mid_row)
    left, right, mlp_1 = together(*neighbours_z(mid), swap(mlp_0, "core"))
    mid = (mid, left, right, *far_z(left, right))
    product, dgu, *terms = mlp(info, mid, cot, gate_weight, up_weight, down_weight, mlp_0, mlp_1)
    product, dgu, *terms = together(product, dgu, *terms)
    gu_jobs, down_jobs = [(mid, dgu)], [(cot, product)]
    far_0, far_1, gu_send = together(*scatter_far(terms), grads(info, (None, None, gu_jobs)))
    gu_got = swap(gu_send, "core")
    got = scatter_near(info, terms, (far_0, far_1))
    gu_half = grads(info, ("s", gu_got, gu_jobs))
    g0, g1, g2, gu_half = together(*got, gu_half)
    gu_quarter = lax.psum_scatter(gu_half, "x", scatter_dimension=0, tiled=True)
    dhidden, datt, mid_part = mid_norm_back((g0, g1, g2), cotangent, hidden, mid_row)
    mixed = mixed_partial(info, product, down_weight, mlp_0, mlp_1)
    left, right, *mixed = together(*neighbours_z(datt), *mixed)
    far_0, far_1, down_send = together(
        *far_z(left, right), grads(info, (None, None, down_jobs))
    )
    datt = (datt, left, right, far_0, far_1)
    dctx = dcontext(info, datt, output_weight, out_0, out_1)
    down_got = swap(down_send, "core")
    dq, dkv_mine, dkv_send, dqgain = attention_back(
        y, q, kv, kv_other, begin_row, lse, dctx, rawq, cosine, sine, qg
    )
    dq, dkv_mine, dkv_send, down_got = together(dq, dkv_mine, dkv_send, down_got)
    oq_jobs = [(datt, ctx), (normed, dq)]
    down_half, oq_send = grads(info, ("s", down_got, down_jobs), (None, None, oq_jobs))
    dkv_got, mixed_far_0, mixed_far_1, oq_send, down_half = together(
        swap(dkv_send, "yhi"), *scatter_far(mixed), oq_send, down_half
    )
    down_quarter = lax.psum_scatter(down_half, "x", scatter_dimension=0, tiled=True)
    dkv, gains, *terms = dpre_partial(
        info, dkv_mine, dkv_got, dq, rawk, cosine, sine, kg, *qkv, normed, pre_row, mid_part, dqgain
    )
    dkv, gains, oq_got, gu_quarter, *terms = together(
        dkv, gains, swap(oq_send, "core"), gu_quarter, *terms
    )
    kv_jobs = [(normed, dkv)]
    oq, kv_send = grads(info, ("s", oq_got, oq_jobs), (None, None, kv_jobs))
    far_0, far_1, kv_send, oq, gains, *others = together(
        *scatter_far(terms), kv_send, oq, gains, *(shift(gains, "z", i) for i in (1, -1, 2))
    )
    oq = lax.psum_scatter(oq, "x", scatter_dimension=0, tiled=True)
    gains = (gains + others[0]) + (others[1] + others[2])
    got = scatter_near(info, terms, (far_0, far_1))
    kv = grads(info, ("x", swap(kv_send, "core"), kv_jobs, gains[0], swap(gains[1], "core")))
    *kv, down_quarter = together(*kv, down_quarter)
    to_right, to_left = relay(info, mixed, (mixed_far_0, mixed_far_1))
    oq, to_right, to_left, *parts = together(
        oq,
        to_right,
        to_left,
        *x_parts(kv),
        *got,
        *y_parts(gu_quarter),
        *y_parts(down_quarter),
    )
    kv, got, gu_parts, down_parts = parts[:4], parts[4:7], parts[7:11], parts[11:]
    mixed = (mixed[0], shift(to_right, "z", 1), shift(to_left, "z", -1))
    own, to_ylo, to_yhi, to_cross = y_split(oq, kv)
    tokens_grad = first_norm_back(got, tokens, dhidden, pre_row)
    tokens_grad, *parts = together(
        tokens_grad, own, swap(to_ylo, "ylo"), swap(to_yhi, "yhi"), cross(to_cross), *mixed
    )
    parts, mixed = parts[:4], parts[4:]
    *grads_out, block_output, pre, mid, heads_q, heads_k = last_sum(
        info, parts, gu_parts, down_parts, mixed, hidden
    )
    out_grad, q_grad, k_grad, v_grad, gate_grad, up_grad, down_grad = grads_out
    return (
        block_output,
        tokens_grad,
        pre[0],
        mid[0],
        heads_q[0],
        heads_k[0],
        q_grad,
        k_grad,
        v_grad,
        out_grad,
        gate_grad,
        up_grad,
        down_grad,
    )


def solution(mesh):
    torus = Mesh(mesh.devices.reshape(4, 2, 2, 4, 2), ("x", "ylo", "core", "z", "yhi"))
    return jax.shard_map(
        body,
        mesh=torus,
        in_specs=(
            P(ALL, None),
            P(ALL, None),
            P(WIDE, None),
            P(),
            P(),
            P(),
            P(),
            P(None, NARROW),
            P(None, NARROW),
            P(None, NARROW),
            P(NARROW, None),
            P(None, NARROW),
            P(None, NARROW),
            P(NARROW, None),
        ),
        out_specs=(
            P(ALL, None),
            P(ALL, None),
            P(WIDE),
            P(WIDE),
            P(WIDE),
            P(WIDE),
            P(WIDE, NARROW),
            P(WIDE, NARROW),
            P(WIDE, NARROW),
            P(NARROW, WIDE),
            P(WIDE, NARROW),
            P(WIDE, NARROW),
            P(NARROW, WIDE),
        ),
        check_vma=False,
    )
```

```python
import functools
import math

import jax
import jax.numpy as jnp
from jax import lax
from jax.experimental import pallas as pl
from jax.experimental.pallas import tpu as pltpu
from jax.sharding import Mesh
from jax.sharding import PartitionSpec as P

NARROW = ("z", "yhi")
WIDE = ("x", "ylo", "core")
ALL = WIDE + NARROW

EPS = 1e-06
ROPE_BASE = 1000000.0
LOG2E = math.log2(math.e)
F32 = jnp.float32
BF16 = jnp.bfloat16


def dot(a, b, ca, cb):
    return lax.dot_general(a, b, (((ca,), (cb,)), ((), ())), preferred_element_type=F32)


def swap(v, axis):
    return lax.ppermute(v, axis, [(0, 1), (1, 0)])


def cross(v):
    return lax.ppermute(v, ("ylo", "yhi"), [(0, 3), (3, 0), (1, 2), (2, 1)])


def shift(v, axis, by):
    return lax.ppermute(v, axis, [(i, (i + by) % 4) for i in range(4)])


def shift_x(v, by):
    return shift(v, "x", by)


def neighbours_z(piece):
    return shift(piece, "z", 1), shift(piece, "z", -1)


def far_z(left, right):
    return shift(left[:64], "z", 1), shift(right[64:], "z", -1)


def gather_z(piece):
    left, right = neighbours_z(piece)
    return piece, left, right, *far_z(left, right)


def gather_z_directly(piece):
    far = shift(piece, "z", 2)
    return piece, shift(piece, "z", 1), shift(piece, "z", -1), far


def scatter_far(terms):
    return shift(terms[3], "z", 1), shift(terms[4], "z", -1)


def scatter_near(info, terms, far):
    to_right, to_left = relay(info, terms, far)
    return terms[0], shift(to_right, "z", 1), shift(to_left, "z", -1)


def together(*values):
    return lax.optimization_barrier(values)


def vmem_spec():
    return pl.BlockSpec()


def smem_spec():
    return pl.BlockSpec(memory_space=pltpu.SMEM)


def params():
    return pltpu.CompilerParams(vmem_limit_bytes=58 * 2**20)


def shape(*dims, kind=BF16):
    return jax.ShapeDtypeStruct(dims, kind)


def features_of(info, c, t, ylo, turned):
    core = info[0] if c == 0 else 1 - info[0]
    tile = (info[1] + t) & 3 if turned else t
    return pl.ds(pl.multiple_of(((tile * 2 + ylo) * 2 + core) * 128, 128), 128)


def piece_moves(info, pieces, dst):
    own, left, right, *rest = pieces
    far = ((info[3] + 2) & 3) * 128
    if len(rest) == 1:
        halves = [(rest[0], dst.at[at_z(info, 2)])]
    else:
        halves = [
            (part, dst.at[pl.ds(pl.multiple_of(far + 64 * i, 64), 64)])
            for i, part in enumerate(rest)
        ]
    return halves + [
        (own, dst.at[at_z(info, 0)]),
        (left, dst.at[at_z(info, 3)]),
        (right, dst.at[at_z(info, 1)]),
    ]


def tile_moves(info, tiles, lanes, dst, turned):
    moves = []
    for c, tile in enumerate(tiles):
        for t in range(4):
            for ylo in range(2):
                rows = slice(128 * ylo, 128 * (ylo + 1))
                moves.append((tile.at[t, rows, lanes], dst.at[features_of(info, c, t, ylo, turned)]))
    return moves


def start(moves, sems, first):
    copies = [
        pltpu.make_async_copy(a, b, sems.at[first + i]) for i, (a, b) in enumerate(moves)
    ]
    for copy in copies:
        copy.start()
    return copies


def wait(copies):
    for copy in copies:
        copy.wait()


def any_spec():
    return pl.BlockSpec(memory_space=pl.ANY)


def place(info, pieces, dst):
    z = info[3]

    def rows(by, first, count):
        return pl.ds(pl.multiple_of(((z + by) & 3) * 128 + first, 64), count)

    own, left, right, far_0, far_1 = pieces
    dst[rows(0, 0, 128), :] = own[...]
    dst[rows(3, 0, 128), :] = left[...]
    dst[rows(1, 0, 128), :] = right[...]
    dst[rows(2, 0, 64), :] = far_0[...]
    dst[rows(2, 64, 64), :] = far_1[...]


def block_of(info, j, how):
    if how != "s" and how != "x":
        return j
    x = (info[1] + j // 2) & 3 if how == "x" else j // 2
    return x * 2 + (info[4] if j % 2 == 0 else 1 - info[4])


def turned_rows(info, pieces, core, how, dst):
    own, left, right, *rest = pieces
    z = info[3]
    for j in range(8):
        block = 2 * block_of(info, j, how) + core
        lanes = pl.ds(pl.multiple_of(block * 128, 128), 128)
        far = [part[:, lanes] for part in rest]
        far = far[0] if len(far) == 1 else jnp.concatenate(far, axis=0)
        for by, block in ((0, own[:, lanes]), (3, left[:, lanes]), (1, right[:, lanes]), (2, far)):
            at = pl.ds(pl.multiple_of(((z + by) & 3) * 128, 128), 128)
            dst[128 * j : 128 * (j + 1), at] = block.T


def take_tiles(info, src, dst, turned):
    for c in range(2):
        for t in range(4):
            for ylo in range(2):
                at = (c * 4 + t) * 256 + ylo * 128
                dst[:, at : at + 128] = src[:, features_of(info, c, t, ylo, turned)]


def add_tile(info, acc, c, t, value, turned):
    for ylo in range(2):
        acc[:, features_of(info, c, t, ylo, turned)] += value[:, ylo * 128 : (ylo + 1) * 128]


def inverse_rms(v):
    return lax.rsqrt(jnp.mean(v * v, axis=1, keepdims=True) + EPS)


def norm_back(d, v, inverse, gain):
    n = v * inverse
    dn = d * gain
    return inverse * (dn - n * jnp.mean(dn * n, axis=1, keepdims=True))


def add_up(refs):
    total = refs[0][...].astype(F32)
    for ref in refs[1:]:
        total = total + ref[...].astype(F32)
    return total


def write_terms(info, value, outs):
    for by, out in ((0, outs[0]), (1, outs[1]), (3, outs[2])):
        out[...] = value(at_z(info, by))
    far = value(at_z(info, 2))
    outs[3][...] = far[:64, :]
    outs[4][...] = far[64:, :]


def terms_shape():
    return [shape(128, 2048)] * 3 + [shape(64, 2048)] * 2


def relay_kernel(right_ref, left_ref, far_0, far_1, to_right, to_left):
    to_right[:64, :] = (right_ref[:64, :].astype(F32) + far_0[...].astype(F32)).astype(BF16)
    to_right[64:, :] = right_ref[64:, :]
    to_left[:64, :] = left_ref[:64, :]
    to_left[64:, :] = (left_ref[64:, :].astype(F32) + far_1[...].astype(F32)).astype(BF16)


def relay(info, terms, far):
    return pl.pallas_call(
        relay_kernel,
        out_shape=[shape(128, 2048)] * 2,
        in_specs=[vmem_spec()] * 4,
        out_specs=[vmem_spec()] * 2,
        compiler_params=params(),
        name="relay",
    )(terms[1], terms[2], *far)


def at_z(info, by):
    return pl.ds(pl.multiple_of(((info[3] + by) & 3) * 128, 128), 128)


def small_pieces_kernel(info, q_ref, k_ref, v_ref, o_ref, qkv_ref, out_ref):
    qkv_ref[:, :256] = q_ref[...]
    qkv_ref[:, 256:384] = k_ref[...]
    qkv_ref[:, 384:] = v_ref[...]
    out_ref[...] = o_ref[...].T


def large_pieces_kernel(info, g_ref, u_ref, d_ref, gu_ref, down_ref):
    gu_ref[:, :768] = g_ref[...]
    gu_ref[:, 768:] = u_ref[...]
    down_ref[...] = d_ref[...].T


def pieces_of(kernel, name, info, weights, turned, widths):
    def at(i, info):
        return (2 * info[1] + i) * 2 + info[0]

    def rows(i, info):
        return at(i, info), 0

    def columns(i, info):
        return 0, at(i, info)

    def out(i, info):
        return i, 0

    return pl.pallas_call(
        kernel,
        grid_spec=pltpu.PrefetchScalarGridSpec(
            num_scalar_prefetch=1,
            grid=(2,),
            in_specs=[pl.BlockSpec((128, w.shape[1]), rows) for w in weights]
            + [pl.BlockSpec((turned.shape[0], 128), columns)],
            out_specs=[pl.BlockSpec((128, w), out) for w in widths],
        ),
        out_shape=[shape(256, w) for w in widths],
        compiler_params=params(),
        name=name,
    )(info, *weights, turned)


def first_norm_kernel(tokens_ref, gain_ref, out_ref):
    x = tokens_ref[...].astype(F32)
    normed = (x * inverse_rms(x) * gain_ref[...]).astype(BF16)
    out_ref[...] = normed


def first_norm(tokens, gain):
    return pl.pallas_call(
        first_norm_kernel,
        out_shape=shape(128, 2048),
        in_specs=[vmem_spec()] * 2,
        out_specs=vmem_spec(),
        compiler_params=params(),
        name="first_norm",
    )(tokens, gain)


def mid_norm_kernel(g0, g1, g2, tokens_ref, gain_ref, hidden_ref, out_ref):
    hidden = tokens_ref[...].astype(F32) + add_up((g0, g1, g2))
    hidden_ref[...] = hidden
    normed = (hidden * inverse_rms(hidden) * gain_ref[...]).astype(BF16)
    out_ref[...] = normed


def mid_norm(got, tokens, gain):
    return pl.pallas_call(
        mid_norm_kernel,
        out_shape=(shape(128, 2048, kind=F32), shape(128, 2048)),
        in_specs=[vmem_spec()] * 5,
        out_specs=[vmem_spec()] * 2,
        compiler_params=params(),
        name="mid_norm",
    )(*got, tokens, gain)


def mid_norm_back_kernel(g0, g1, g2, cot_ref, hidden_ref, gain_ref, dhidden_ref, out_ref, dgain_ref):
    hidden = hidden_ref[...]
    inverse = inverse_rms(hidden)
    dmid = add_up((g0, g1, g2))
    dgain_ref[...] = jnp.sum(dmid * (hidden * inverse), axis=0, keepdims=True)
    dhidden = cot_ref[...].astype(F32) + norm_back(dmid, hidden, inverse, gain_ref[...])
    dhidden_ref[...] = dhidden
    out_ref[...] = dhidden.astype(BF16)


def mid_norm_back(got, cot, hidden, gain):
    return pl.pallas_call(
        mid_norm_back_kernel,
        out_shape=(
            shape(128, 2048, kind=F32),
            shape(128, 2048),
            shape(1, 2048, kind=F32),
        ),
        in_specs=[vmem_spec()] * 6,
        out_specs=[vmem_spec()] * 3,
        compiler_params=params(),
        name="mid_norm_back",
    )(*got, cot, hidden, gain)


def first_norm_back_kernel(g0, g1, g2, tokens_ref, dhidden_ref, gain_ref, out_ref):
    x = tokens_ref[...].astype(F32)
    d = norm_back(add_up((g0, g1, g2)), x, inverse_rms(x), gain_ref[...])
    out_ref[...] = (dhidden_ref[...] + d).astype(BF16)


def project_kernel(
    info, a0, a1, a2, a3, a4, wq, wk, wv, p0, p1, cos_ref, sin_ref, qgain_ref, kgain_ref,
    rawq_ref, rawk_ref, q_ref, kv_ref, normed, w, raw, sems,
):
    moves = piece_moves(info, (a0, a1, a2, a3, a4), normed)
    moves += [(wq, w.at[:, :256]), (wk, w.at[:, 256:384]), (wv, w.at[:, 384:512])]
    copies = start(moves, sems, 0)
    more = start(tile_moves(info, (p0, p1), slice(None), w.at[:, 512:], True), sems, 8)
    wait(copies)
    raw[:, :512] = dot(normed[...], w[:, :512], 1, 0)
    wait(more)
    raw[:, 512:] = dot(normed[...], w[:, 512:], 1, 0)
    cosine, sine = cos_ref[...], sin_ref[...]

    def prep(v, gain):
        return rope(v * inverse_rms(v) * gain, cosine, sine).astype(BF16)

    for g in range(2):
        at, bt = 512 * g, 256 * g
        for h in range(2):
            v = raw[:, at + 128 * h : at + 128 * (h + 1)]
            rawq_ref[:, bt + 128 * h : bt + 128 * (h + 1)] = v.astype(BF16)
            q_ref[:, bt + 128 * h : bt + 128 * (h + 1)] = prep(v, qgain_ref[...])
        v = raw[:, at + 256 : at + 384]
        rawk_ref[:, 128 * g : 128 * (g + 1)] = v.astype(BF16)
        kv_ref[:, bt : bt + 128] = prep(v, kgain_ref[...])
        kv_ref[:, bt + 128 : bt + 256] = raw[:, at + 384 : at + 512].astype(BF16)


def project(info, pieces, wq, wk, wv, p0, p1, cosine, sine, qgain, kgain):
    return pl.pallas_call(
        project_kernel,
        out_shape=(shape(512, 512), shape(512, 256), shape(512, 512), shape(512, 512)),
        in_specs=[smem_spec()] + [any_spec()] * 10 + [vmem_spec()] * 4,
        out_specs=[vmem_spec()] * 4,
        scratch_shapes=[
            pltpu.VMEM((512, 2048), BF16),
            pltpu.VMEM((2048, 1024), BF16),
            pltpu.VMEM((512, 1024), F32),
            pltpu.SemaphoreType.DMA((24,)),
        ],
        compiler_params=params(),
        name="project",
    )(info, *pieces, wq, wk, wv, p0, p1, cosine, sine, qgain, kgain)


def attended_kernel(info, ctx_ref, own_ref, p0_ref, p1_ref, o0, o1, o2, o3, o4, acc):
    acc[...] = dot(ctx_ref[:, :256], own_ref[...], 1, 0)
    par = ctx_ref[:, 256:]
    for c, p in enumerate((p0_ref, p1_ref)):
        for t in range(4):
            add_tile(info, acc, c, t, dot(par, p[t], 1, 1), True)
    write_terms(info, lambda rows: acc[rows, :].astype(BF16), (o0, o1, o2, o3, o4))


def attended_partial(info, ctx, own, p0, p1):
    return pl.pallas_call(
        attended_kernel,
        out_shape=terms_shape(),
        in_specs=[smem_spec()] + [vmem_spec()] * 4,
        out_specs=[vmem_spec()] * 5,
        scratch_shapes=[pltpu.VMEM((512, 2048), F32)],
        compiler_params=params(),
        name="attended",
    )(info, ctx, own, p0, p1)


def dcontext_kernel(info, d0, d1, d2, d3, d4, own_ref, p0_ref, p1_ref, out_ref, datt, tiles):
    place(info, (d0, d1, d2, d3, d4), datt)
    take_tiles(info, datt, tiles, True)
    out_ref[:, :256] = dot(datt[...], own_ref[...], 1, 1).astype(BF16)
    par = None
    for c, p in enumerate((p0_ref, p1_ref)):
        for t in range(4):
            at = (c * 4 + t) * 256
            part = dot(tiles[:, at : at + 256], p[t], 1, 0)
            par = part if par is None else par + part
    out_ref[:, 256:] = par.astype(BF16)


def dcontext(info, pieces, own, p0, p1):
    return pl.pallas_call(
        dcontext_kernel,
        out_shape=shape(512, 512),
        in_specs=[smem_spec()] + [vmem_spec()] * 8,
        out_specs=vmem_spec(),
        scratch_shapes=[pltpu.VMEM((512, 2048), BF16), pltpu.VMEM((512, 2048), BF16)],
        compiler_params=params(),
        name="dcontext",
    )(info, *pieces, own, p0, p1)


def mlp_kernel(
    info, m0, m1, m2, m3, m4, c0, c1, c2, c3, gate_any, up_any, down_any, p0, p1,
    product_ref, dgu_ref, o0, o1, o2, o3, o4, mid, cot, acc, w, d, par, sems,
):
    moves = piece_moves(info, (m0, m1, m2, m3, m4), mid)
    moves += [(gate_any, w.at[:, :768]), (up_any, w.at[:, 768:])]
    first = start(moves, sems, 0)
    moves = piece_moves(info, (c0, c1, c2, c3), cot) + [(down_any, d)]
    second = start(moves, sems, 7)
    third = start(tile_moves(info, (p0, p1), slice(None), par, False), sems, 13)

    def middle(gu, dproduct, at):
        gate, up = gu[:, :768], gu[:, 768:]
        sig = jax.nn.sigmoid(gate)
        silu = gate * sig
        product_ref[:, at : at + 768] = (silu * up).astype(BF16)
        dgate = (dproduct * up * sig * (1.0 + gate * (1.0 - sig))).astype(BF16)
        dgu_ref[:, 2 * at : 2 * at + 768] = dgate
        dgu_ref[:, 2 * at + 768 : 2 * at + 1536] = (dproduct * silu).astype(BF16)

    wait(first)
    gu = dot(mid[...], w[...], 1, 0)
    wait(second)
    middle(gu, dot(cot[...], d[...], 1, 1), 0)
    acc[...] = dot(w[...], dgu_ref[:, :1536], 1, 1)
    wait(third)
    gu = dot(mid[...], par[:, :1536], 1, 0)
    middle(gu, dot(cot[...], par[:, 1536:], 1, 0), 768)
    acc[...] += dot(par[:, :1536], dgu_ref[:, 1536:], 1, 1)
    write_terms(info, lambda rows: acc[:, rows].astype(BF16).T, (o0, o1, o2, o3, o4))


def mlp(info, mid, cot, gate, up, down, p0, p1):
    return pl.pallas_call(
        mlp_kernel,
        out_shape=[shape(512, 1536), shape(512, 3072)] + terms_shape(),
        in_specs=[smem_spec()] + [any_spec()] * 14,
        out_specs=[vmem_spec()] * 7,
        scratch_shapes=[
            pltpu.VMEM((512, 2048), BF16),
            pltpu.VMEM((512, 2048), BF16),
            pltpu.VMEM((2048, 512), F32),
            pltpu.VMEM((2048, 1536), BF16),
            pltpu.VMEM((768, 2048), BF16),
            pltpu.VMEM((2048, 2304), BF16),
            pltpu.SemaphoreType.DMA((29,)),
        ],
        compiler_params=params(),
        name="mlp",
    )(info, *mid, *cot, gate, up, down, p0, p1)


def mixed_kernel(info, own, p0, p1, product_ref, o0, o1, o2, o3, o4, acc, w, par, sems):
    copies = start([(own, w)], sems, 0)
    lanes = slice(1536, 2304)
    more = start(tile_moves(info, (p0, p1), lanes, par, False), sems, 1)
    wait(copies)
    acc[...] = dot(product_ref[:, :768], w[...], 1, 0)
    wait(more)
    acc[...] += dot(product_ref[:, 768:], par[...], 1, 1)
    write_terms(info, lambda rows: acc[rows, :].astype(BF16), (o0, o1, o2, o3, o4))


def mixed_partial(info, product, own, p0, p1):
    return pl.pallas_call(
        mixed_kernel,
        out_shape=terms_shape(),
        in_specs=[smem_spec()] + [any_spec()] * 3 + [vmem_spec()],
        out_specs=[vmem_spec()] * 5,
        scratch_shapes=[
            pltpu.VMEM((512, 2048), F32),
            pltpu.VMEM((768, 2048), BF16),
            pltpu.VMEM((2048, 768), BF16),
            pltpu.SemaphoreType.DMA((17,)),
        ],
        compiler_params=params(),
        name="mixed",
    )(info, own, p0, p1, product)


def dpre_kernel(
    info, wq, wk, wv, p0, p1, a0, a1, a2, a3, a4, mine_ref, got_ref, dq_ref, rawk_ref, cos_ref,
    sin_ref, kgain_ref, gain_ref, mid_ref, dqgain_ref, dkv_ref, gains_ref, o0, o1, o2, o3, o4,
    acc, normed, low, w, d_all, sems,
):
    copies = start([(wq, w.at[:, :256]), (wk, w.at[:, 256:384]), (wv, w.at[:, 384:512])], sems, 0)
    copies += start(tile_moves(info, (p0, p1), slice(None), w.at[:, 512:], True), sems, 3)
    more = start(piece_moves(info, (a0, a1, a2, a3, a4), normed), sems, 19)
    dgain = jnp.zeros((1, 128), F32)
    for g in range(2):
        at, bt, og = 256 * g, 256 * g + 128, 256 * (1 - g)
        dk = mine_ref[:, at:bt] + got_ref[:, og : og + 128].astype(F32)
        raw = rawk_ref[:, 128 * g : 128 * (g + 1)].astype(F32)
        d, part = head_back(dk, raw, kgain_ref[...], cos_ref[...], sin_ref[...])
        dkv_ref[:, at:bt] = d
        dgain = dgain + part
        dv = mine_ref[:, bt : bt + 128] + got_ref[:, og + 128 : og + 256].astype(F32)
        dkv_ref[:, bt : bt + 128] = dv.astype(BF16)
        d_all[:, 512 * g : 512 * g + 256] = dq_ref[:, at : at + 256]
        d_all[:, 512 * g + 256 : 512 * g + 512] = dkv_ref[:, at : at + 256]
    wait(copies)
    acc[...] = dot(w[...], d_all[...], 1, 1)
    wait(more)
    total = jnp.zeros((1, 2048), F32)
    for i in range(4):
        turned = acc[:, 128 * i : 128 * (i + 1)].astype(BF16).T
        part = turned.astype(F32) * normed[128 * i : 128 * (i + 1), :].astype(F32)
        total = total + jnp.sum(part, axis=0, keepdims=True)
        low[128 * i : 128 * (i + 1), :] = turned
    total = total / gain_ref[...]
    for i in range(16):
        row, lanes = slice(i // 2, i // 2 + 1), slice(128 * i, 128 * (i + 1))
        ref = gains_ref.at[jnp.where(info[0] == i % 2, 0, 1)]
        ref[row, :128] = total[:, lanes]
        ref[row, 128:256] = mid_ref[:, lanes]
        ref[row, 256:384] = dqgain_ref[...]
        ref[row, 384:] = dgain
    write_terms(info, lambda rows: low[rows, :], (o0, o1, o2, o3, o4))


def dpre_partial(
    info, mine, got, dq, rawk, cosine, sine, kgain, wq, wk, wv, p0, p1, pieces, *gains
):
    return pl.pallas_call(
        dpre_kernel,
        out_shape=(shape(512, 512), shape(2, 8, 512, kind=F32), *terms_shape()),
        in_specs=[smem_spec()] + [any_spec()] * 10 + [vmem_spec()] * 10,
        out_specs=[vmem_spec()] * 7,
        scratch_shapes=[
            pltpu.VMEM((2048, 512), F32),
            pltpu.VMEM((512, 2048), BF16),
            pltpu.VMEM((512, 2048), BF16),
            pltpu.VMEM((2048, 1024), BF16),
            pltpu.VMEM((512, 1024), BF16),
            pltpu.SemaphoreType.DMA((24,)),
        ],
        compiler_params=params(),
        name="dpre",
    )(info, wq, wk, wv, p0, p1, *pieces, mine, got, dq, rawk, cosine, sine, kgain, *gains)


def grad_kernel(info, *refs, plan):
    step = pl.program_id(0)
    turned = refs[-1]
    at_in, at_out = 0, sum(p[3] for p in plan)
    for n, (keep, how, starts, count_in, count_out, after) in enumerate(plan):
        ins = refs[at_in : at_in + count_in]
        outs = refs[at_out : at_out + count_out]
        at_in, at_out = at_in + count_in, at_out + count_out
        core = info[0] if keep else 1 - info[0]
        ends = starts[1:] + ((plan[n + 1][2][0],) if n + 1 < len(plan) else (None,))
        for job, (start, end) in enumerate(zip(starts, ends)):
            count = (len(ins) - after) // len(starts)
            job_ins = ins[count * job : count * (job + 1)]
            pieces, b = job_ins[:-1], job_ins[-1]

            @pl.when(step == start)
            def turn(pieces=pieces, core=core, how=how):
                turned_rows(info, pieces, core, how, turned)

            inside = step >= start if end is None else (step >= start) & (step < end)

            @pl.when(inside)
            def multiply(
                b=b, keep=keep, how=how, ins=ins, outs=outs, starts=starts, after=after
            ):
                total = dot(turned[...], b[...], 1, 0)
                if not keep:
                    outs[0][...] = total.astype(BF16)
                    return
                got = ins[len(ins) - after]
                if how == "y":
                    total = (total + got[...].astype(F32)).astype(BF16)
                    for par in range(2):

                        @pl.when(step == starts[0] + par)
                        def write(par=par):
                            yhi = info[2] if par == 0 else 1 - info[2]
                            for j in range(8):
                                rows = slice(128 * (j // 2), 128 * (j // 2 + 1))
                                out = outs[0].at[2 * (j % 2) + yhi]
                                out[rows, :] = total[128 * j : 128 * (j + 1), :]

                    return
                for j in range(8):
                    block = block_of(info, j, how)
                    rows = pl.ds(pl.multiple_of(block * 128, 128), 128)
                    part = total[128 * j : 128 * (j + 1), :] + got[rows, :].astype(F32)
                    if how == "s":
                        outs[0][128 * j : 128 * (j + 1), :] = part.astype(BF16)
                        continue
                    out, i = outs[j // 2], j % 2
                    out[128 * i : 128 * (i + 1), :] = part.astype(BF16)
                    mine, other = ins[-2], ins[-1]
                    row = mine[pl.ds(block, 1), :] + other[pl.ds(block, 1), :]
                    row = jnp.concatenate([row, jnp.zeros((15, 512), F32)], axis=0)
                    out[256 + 16 * i : 272 + 16 * i, :] = row.astype(BF16)


def grads(info, *bundles):
    plan, in_specs, out_specs, out_shape, args, at = [], [], [], [], [], 0

    def whole(rows):
        return pl.BlockSpec((rows, 2048), lambda i: (0, 0))

    for how, got, jobs, *gains in bundles:
        keep = got is not None
        width = 768 if jobs[0][1].shape[1] % 768 == 0 else 512
        first, starts, before = at, [], len(in_specs)

        def tile_of(start, count):
            return lambda i: (0, jnp.clip(i - start, 0, count - 1))

        for pieces, b in jobs:
            count = b.shape[1] // width
            starts.append(at)
            in_specs += [whole(piece.shape[0]) for piece in pieces]
            in_specs.append(pl.BlockSpec((512, width), tile_of(at, count)))
            args += [*pieces, b]
            at += count
        tile, columns = tile_of(first, at - first), (at - first) * width
        if keep:
            in_specs.append(pl.BlockSpec((1024, width), tile))
            args.append(got)
            in_specs += [pl.BlockSpec(v.shape, lambda i: (0, 0)) for v in gains]
            args += gains
        count_out = 1
        if how == "y":
            out_shape.append(shape(4, 512, width))
            out_specs.append(pl.BlockSpec((4, 512, width), lambda i: (0, 0, 0)))
        elif how == "x":
            out_shape += [shape(288, width)] * 4
            out_specs += [pl.BlockSpec((288, width), lambda i: (0, 0))] * 4
            count_out = 4
        else:
            out_shape.append(shape(1024, columns))
            out_specs.append(pl.BlockSpec((1024, width), tile))
        plan.append((keep, how, tuple(starts), len(in_specs) - before, count_out, keep + len(gains)))
    out = pl.pallas_call(
        functools.partial(grad_kernel, plan=tuple(plan)),
        grid=(at,),
        out_shape=out_shape,
        in_specs=[smem_spec()] + in_specs,
        out_specs=out_specs,
        scratch_shapes=[pltpu.VMEM((1024, 512), BF16)],
        compiler_params=params(),
        name="grads",
    )(info, *args)
    results, at = [], 0
    for _, _, _, _, count_out, _ in plan:
        results.append(out[at] if count_out == 1 else list(out[at : at + count_out]))
        at += count_out
    return results[0] if len(results) == 1 else results


def y_parts(quarter):
    c = quarter.shape[1] // 2
    return (
        quarter[:128, :c],
        swap(quarter[128:, :c], "ylo"),
        swap(quarter[:128, c:], "yhi"),
        cross(quarter[128:, c:]),
    )


def x_parts(parts):
    return parts[0], shift_x(parts[1], 1), shift_x(parts[2], 2), shift_x(parts[3], -1)


def y_split_kernel(oq_ref, k0, k1, k2, k3, mine, to_ylo, to_yhi, to_cross, kv, oq):
    kv[...] = add_up((k0, k1, k2, k3))
    oq[...] = add_up([oq_ref.at[i] for i in range(4)])
    for i, out in enumerate((mine, to_ylo, to_yhi, to_cross)):
        other, par = i % 2, i // 2
        rows = slice(128 * other, 128 * (other + 1))
        out[:128, :256] = oq[rows, 256 * par : 256 * par + 256].astype(out.dtype)
        out[:128, 256:512] = oq[rows, 512 + 256 * par : 768 + 256 * par].astype(out.dtype)
        out[:128, 512:] = kv[rows, 256 * par : 256 * par + 256].astype(out.dtype)
        out[128:, :512] = kv[256 + 16 * other : 272 + 16 * other, :].astype(out.dtype)
        out[128:, 512:] = jnp.zeros((16, 256), out.dtype)


def y_split(oq, kv):
    return pl.pallas_call(
        y_split_kernel,
        out_shape=[shape(144, 768, kind=F32)] + [shape(144, 768)] * 3,
        in_specs=[vmem_spec()] * 5,
        out_specs=[vmem_spec()] * 4,
        scratch_shapes=[pltpu.VMEM((288, 512), F32), pltpu.VMEM((256, 1024), F32)],
        compiler_params=params(),
        name="y_split",
    )(oq, *kv)


def last_sum_kernel(info, *refs):
    out, q, k, v, block, pre, mid, qgain, kgain = refs[8:]
    total = add_up(refs[:4])
    out[...] = total[:128, :256].T
    q[...] = total[:128, 256:512]
    k[...] = total[:128, 512:640]
    v[...] = total[:128, 640:]
    pre[...] = total[128:129, :128]
    mid[...] = total[128:129, 128:256]
    w = (info[1] * 2 + info[4]) * 2 + info[0]
    back = (128 - 8 * w) & 127
    qgain[...] = pltpu.roll(total[128:136, 256:384], back, 1)[:1, :8]
    kgain[...] = pltpu.roll(total[128:136, 384:512], back, 1)[:1, :8]
    block[...] = add_up(refs[4:8]).astype(BF16)


def last_sum(info, parts, mixed, hidden):
    dims = ((256, 128), (128, 256), (128, 128), (128, 128))
    gains = ((1, 128), (1, 128), (1, 8), (1, 8))
    return pl.pallas_call(
        last_sum_kernel,
        out_shape=[shape(*d, kind=F32) for d in dims]
        + [shape(128, 2048)]
        + [shape(*d, kind=F32) for d in gains],
        in_specs=[smem_spec()] + [vmem_spec()] * 8,
        out_specs=[vmem_spec()] * 9,
        compiler_params=params(),
        name="last_sum",
    )(info, *parts, hidden, *mixed)


def inner_kernel(*refs):
    first_norm_back_kernel(*refs[:6], refs[14])
    gate, up, down = refs[15:]
    total = add_up(refs[6:10])
    gate[...] = total[:, :768]
    up[...] = total[:, 768:]
    down[...] = add_up(refs[10:14]).T


def inner(got, tokens, dhidden, gain, gu_parts, down_parts):
    dims = ((128, 768), (128, 768), (768, 128))
    return pl.pallas_call(
        inner_kernel,
        out_shape=[shape(128, 2048)] + [shape(*d, kind=F32) for d in dims],
        in_specs=[vmem_spec()] * 14,
        out_specs=[vmem_spec()] * 4,
        compiler_params=params(),
        name="inner",
    )(*got, tokens, dhidden, gain, *gu_parts, *down_parts)


def rope(v, cosine, sine):
    return v * cosine + pltpu.roll(v, 64, 1) * sine


def rope_back(v, cosine, sine):
    return v * cosine - pltpu.roll(v, 64, 1) * sine


def place_keys(y, kv_ref, other_ref, k_all, v_all):
    for g in range(2):
        for z in range(4):
            rows = slice(128 * z, 128 * (z + 1))
            at = pl.ds(pl.multiple_of(256 * z + 128 * y, 128), 128)
            bt = pl.ds(pl.multiple_of(256 * z + 128 * (1 - y), 128), 128)
            k_all[g, at, :] = kv_ref[rows, 256 * g : 256 * g + 128]
            v_all[g, at, :] = kv_ref[rows, 256 * g + 128 : 256 * g + 256]
            og = 256 * (1 - g)
            k_all[g, bt, :] = other_ref[rows, og : og + 128]
            v_all[g, bt, :] = other_ref[rows, og + 128 : og + 256]


def seen_by(y, z, begin):
    rows = 256 * (z + 1)
    key = lax.broadcasted_iota(jnp.int32, (rows, 256), 0)
    query = (lax.broadcasted_iota(jnp.int32, (rows, 256), 1) & 127) + (256 * z + 128 * y)
    return (key <= query) & (key >= begin)


def stacked(ref, z, g):
    rows = slice(128 * z, 128 * (z + 1))
    return jnp.concatenate(
        [ref[rows, 256 * g : 256 * g + 128], ref[rows, 256 * g + 128 : 256 * g + 256]], axis=0
    )


def attention_kernel(y_ref, q_ref, kv_ref, other_ref, begin_ref, ctx_ref, lse_ref, k_all, v_all):
    scale2 = 128**-0.5 * LOG2E
    y = y_ref[0]
    place_keys(y, kv_ref, other_ref, k_all, v_all)
    for g in range(2):
        v_t = v_all[g].T
        for z in range(4):
            rows = 256 * (z + 1)
            begin = begin_ref[:, 128 * z : 128 * (z + 1)]
            begin = jnp.concatenate([begin, begin], axis=1)
            s = dot(k_all[g, :rows, :], stacked(q_ref, z, g), 1, 1) * scale2
            s = jnp.where(seen_by(y, z, begin), s, -1e30)
            peak = jnp.max(s, axis=0, keepdims=True)
            expo = jnp.exp2(s - peak)
            total = jnp.sum(expo, axis=0, keepdims=True)
            weights = (expo * (1.0 / total)).astype(BF16)
            ctx = dot(v_t[:, :rows], weights, 1, 0).T.astype(BF16)
            for h in range(2):
                ctx_ref[
                    128 * z : 128 * (z + 1), 256 * g + 128 * h : 256 * g + 128 * (h + 1)
                ] = ctx[128 * h : 128 * (h + 1), :]
            lse_ref[4 * g + z : 4 * g + z + 1, :] = peak + jnp.log2(total)


def attention(y, q, kv, other, begin_row):
    return pl.pallas_call(
        attention_kernel,
        out_shape=(
            jax.ShapeDtypeStruct((512, 512), BF16),
            jax.ShapeDtypeStruct((8, 256), F32),
        ),
        in_specs=[smem_spec()] + [vmem_spec()] * 4,
        out_specs=[vmem_spec()] * 2,
        scratch_shapes=[pltpu.VMEM((2, 1024, 128), BF16), pltpu.VMEM((2, 1024, 128), BF16)],
        compiler_params=params(),
        name="attention",
    )(y, q, kv, other, begin_row)


def head_back(d, raw, gain, cosine, sine):
    dn = rope_back(d, cosine, sine)
    inverse = lax.rsqrt(jnp.mean(raw * raw, axis=1, keepdims=True) + EPS)
    n = raw * inverse
    dgain = jnp.sum(dn * n, axis=0, keepdims=True)
    dn = dn * gain
    draw = inverse * (dn - n * jnp.mean(dn * n, axis=1, keepdims=True))
    return draw.astype(BF16), dgain


def attention_back_kernel(
    y_ref, q_ref, kv_ref, other_ref, begin_ref, lse_ref, dctx_ref, raw_ref, cos_ref, sin_ref,
    qgain_ref, dq_ref, mine_ref, send_ref, dqgain_ref, k_all, v_all, dk_acc, dv_acc, dq_acc,
):
    scale = 128**-0.5
    scale2 = scale * LOG2E
    y = y_ref[0]
    place_keys(y, kv_ref, other_ref, k_all, v_all)
    dk_acc[...] = jnp.zeros_like(dk_acc)
    dv_acc[...] = jnp.zeros_like(dv_acc)
    for g in range(2):
        k_t = k_all[g].T
        for z in range(4):
            rows = 256 * (z + 1)
            begin = begin_ref[:, 128 * z : 128 * (z + 1)]
            begin = jnp.concatenate([begin, begin], axis=1)
            q = stacked(q_ref, z, g)
            dctx = stacked(dctx_ref, z, g)
            s = dot(k_all[g, :rows, :], q, 1, 1) * scale2
            s = s - lse_ref[4 * g + z : 4 * g + z + 1, :]
            probs = jnp.where(seen_by(y, z, begin), jnp.exp2(s), 0.0)
            dprobs = dot(v_all[g, :rows, :], dctx, 1, 1)
            inner = jnp.sum(probs * dprobs, axis=0, keepdims=True)
            dscores = (probs * (dprobs - inner) * scale).astype(BF16)
            dv_acc[g, :rows, :] += dot(probs.astype(BF16), dctx, 1, 0)
            dk_acc[g, :rows, :] += dot(dscores, q, 1, 0)
            dq = dot(k_t[:, :rows], dscores, 1, 0).T
            for h in range(2):
                dq_acc[
                    128 * z : 128 * (z + 1), 256 * g + 128 * h : 256 * g + 128 * (h + 1)
                ] = dq[128 * h : 128 * (h + 1), :]
    dgain = jnp.zeros((1, 128), F32)
    for g in range(2):
        for h in range(2):
            lanes = slice(256 * g + 128 * h, 256 * g + 128 * (h + 1))
            raw = raw_ref[:, lanes].astype(F32)
            d, part = head_back(
                dq_acc[:, lanes], raw, qgain_ref[...], cos_ref[...], sin_ref[...]
            )
            dq_ref[:, lanes] = d
            dgain = dgain + part
        for z in range(4):
            rows = slice(128 * z, 128 * (z + 1))
            at = pl.ds(pl.multiple_of(256 * z + 128 * y, 128), 128)
            bt = pl.ds(pl.multiple_of(256 * z + 128 * (1 - y), 128), 128)
            mine_ref[rows, 256 * g : 256 * g + 128] = dk_acc[g, at, :]
            mine_ref[rows, 256 * g + 128 : 256 * g + 256] = dv_acc[g, at, :]
            send_ref[rows, 256 * g : 256 * g + 128] = dk_acc[g, bt, :].astype(BF16)
            send_ref[rows, 256 * g + 128 : 256 * g + 256] = dv_acc[g, bt, :].astype(BF16)
    dqgain_ref[...] = dgain


def attention_back(y, q, kv, other, begin_row, lse, dctx, raw, cosine, sine, qgain):
    return pl.pallas_call(
        attention_back_kernel,
        out_shape=(
            jax.ShapeDtypeStruct((512, 512), BF16),
            jax.ShapeDtypeStruct((512, 512), F32),
            jax.ShapeDtypeStruct((512, 512), BF16),
            jax.ShapeDtypeStruct((1, 128), F32),
        ),
        in_specs=[smem_spec()] + [vmem_spec()] * 10,
        out_specs=[vmem_spec()] * 4,
        scratch_shapes=[
            pltpu.VMEM((2, 1024, 128), BF16),
            pltpu.VMEM((2, 1024, 128), BF16),
            pltpu.VMEM((2, 1024, 128), F32),
            pltpu.VMEM((2, 1024, 128), F32),
            pltpu.VMEM((512, 512), F32),
        ],
        compiler_params=params(),
        name="attention_back",
    )(y, q, kv, other, begin_row, lse, dctx, raw, cosine, sine, qgain)


def row_tables(lengths):
    ends = jnp.cumsum(lengths)
    starts = ends - lengths
    at = jnp.arange(512, dtype=jnp.int32)
    places = (at // 128) * 256 + at % 128 + lax.axis_index("yhi") * 128
    begin = jnp.max(jnp.where(starts[None, :] <= places[:, None], starts[None, :], 0), axis=1)
    offset = (places - begin).astype(F32)
    freq = jnp.exp(jnp.arange(64, dtype=F32) * (-2.0 * math.log(ROPE_BASE) / 128))
    angle = offset[:, None] * freq[None, :]
    cosine, sine = jnp.cos(angle), jnp.sin(angle)
    return (
        begin,
        jnp.concatenate([cosine, cosine], axis=1),
        jnp.concatenate([-sine, sine], axis=1),
    )


def body(
    tokens, cotangent, doc_lengths, pre_gain, mid_gain, query_gain, key_gain,
    query_weight, key_matrix, value_matrix, output_weight, gate_weight, up_weight, down_weight,
):
    info = jnp.stack([lax.axis_index(name) for name in ("core", "x", "yhi", "z", "ylo")])
    info = info.astype(jnp.int32)
    y = info[2:3]
    pre_row, mid_row = pre_gain[None, :], mid_gain[None, :]
    qg, kg = query_gain[None, :], key_gain[None, :]

    qkv_piece, out_piece = pieces_of(
        small_pieces_kernel,
        "small_pieces",
        info,
        (query_weight, key_matrix, value_matrix),
        output_weight,
        (512, 256),
    )
    normed = first_norm(tokens, pre_row)
    normed, qkv_piece, out_piece = together(normed, qkv_piece, out_piece)
    gu_piece, down_piece = pieces_of(
        large_pieces_kernel, "large_pieces", info, (gate_weight, up_weight), down_weight, (1536, 768)
    )
    normed = gather_z(normed)
    tile, out_tile, gu_piece, down_piece = together(
        cross(qkv_piece), cross(out_piece), gu_piece, down_piece
    )

    def x_tiles(tile):
        return [tile, shift_x(tile, -1), shift_x(tile, -2), shift_x(tile, 1)]

    begin, cosine, sine = row_tables(doc_lengths[0])
    begin_row = begin[None, :]
    *parts, cosine, sine, gu_piece, down_piece = together(
        *x_tiles(tile), *normed, cosine, sine, cross(gu_piece), down_piece
    )
    tiles, normed = parts[:4], tuple(parts[4:])
    qkv_0 = jnp.stack(tiles)
    qkv_0, qkv_1, out_tile = together(qkv_0, swap(qkv_0, "core"), out_tile)

    qkv = (query_weight, key_matrix, value_matrix, qkv_0, qkv_1)
    rawq, rawk, q, kv = project(info, normed, *qkv, cosine, sine, qg, kg)
    kv, down_piece, out_tile, left, right = together(
        kv, cross(down_piece), out_tile, *neighbours_z(cotangent)
    )
    mlp_0 = lax.all_gather(
        jnp.concatenate([gu_piece, down_piece], axis=1), "x", axis=0, tiled=False
    )
    kv_other, far, *tiles = together(
        swap(kv, "yhi"), shift(cotangent, "z", 2), *x_tiles(out_tile)
    )
    cot = (cotangent, left, right, far)
    out_0 = jnp.stack(tiles)
    out_1 = swap(out_0, "core")
    ctx, lse = attention(y, q, kv, kv_other, begin_row)
    terms = attended_partial(info, ctx, output_weight, out_0, out_1)
    got = scatter_near(info, terms, together(*scatter_far(terms)))
    g0, g1, g2, mlp_0 = together(*got, mlp_0)
    hidden, mid = mid_norm((g0, g1, g2), tokens, mid_row)
    left, right, mlp_1 = together(*neighbours_z(mid), swap(mlp_0, "core"))
    mid = (mid, left, right, *far_z(left, right))
    product, dgu, *terms = mlp(info, mid, cot, gate_weight, up_weight, down_weight, mlp_0, mlp_1)
    product, dgu, *terms = together(product, dgu, *terms)
    gu_jobs, down_jobs = [(mid, dgu)], [(cot, product)]
    far_0, far_1, gu_send = together(*scatter_far(terms), grads(info, (None, None, gu_jobs)))
    gu_got = swap(gu_send, "core")
    got = scatter_near(info, terms, (far_0, far_1))
    gu_half = grads(info, ("s", gu_got, gu_jobs))
    g0, g1, g2, gu_half = together(*got, gu_half)
    gu_quarter = lax.psum_scatter(gu_half, "x", scatter_dimension=0, tiled=True)
    dhidden, datt, mid_part = mid_norm_back((g0, g1, g2), cotangent, hidden, mid_row)
    mixed = mixed_partial(info, product, down_weight, mlp_0, mlp_1)
    left, right, *mixed = together(*neighbours_z(datt), *mixed)
    far_0, far_1, down_send = together(
        *far_z(left, right), grads(info, (None, None, down_jobs))
    )
    datt = (datt, left, right, far_0, far_1)
    dctx = dcontext(info, datt, output_weight, out_0, out_1)
    down_got = swap(down_send, "core")
    dq, dkv_mine, dkv_send, dqgain = attention_back(
        y, q, kv, kv_other, begin_row, lse, dctx, rawq, cosine, sine, qg
    )
    dq, dkv_mine, dkv_send, down_got = together(dq, dkv_mine, dkv_send, down_got)
    oq_jobs = [(datt, ctx), (normed, dq)]
    down_half, oq_send = grads(info, ("s", down_got, down_jobs), (None, None, oq_jobs))
    dkv_got, mixed_far_0, mixed_far_1, oq_send, down_half = together(
        swap(dkv_send, "yhi"), *scatter_far(mixed), oq_send, down_half
    )
    down_quarter = lax.psum_scatter(down_half, "x", scatter_dimension=0, tiled=True)
    dkv, gains, *terms = dpre_partial(
        info, dkv_mine, dkv_got, dq, rawk, cosine, sine, kg, *qkv, normed, pre_row, mid_part, dqgain
    )
    dkv, gains, oq_got, gu_quarter, *terms = together(
        dkv, gains, swap(oq_send, "core"), gu_quarter, *terms
    )
    kv_jobs = [(normed, dkv)]
    oq, kv_send = grads(info, ("s", oq_got, oq_jobs), (None, None, kv_jobs))
    far_0, far_1, kv_send, oq, gains, *others = together(
        *scatter_far(terms), kv_send, oq, gains, *(shift(gains, "z", i) for i in (1, -1, 2))
    )
    oq = lax.all_to_all(
        oq.reshape(4, 256, 1024), "x", split_axis=0, concat_axis=0, tiled=True
    )
    gains = (gains + others[0]) + (others[1] + others[2])
    got = scatter_near(info, terms, (far_0, far_1))
    kv = grads(info, ("x", swap(kv_send, "core"), kv_jobs, gains[0], swap(gains[1], "core")))
    *kv, down_quarter = together(*kv, down_quarter)
    to_right, to_left = relay(info, mixed, (mixed_far_0, mixed_far_1))
    oq, to_right, to_left, *parts = together(
        oq,
        to_right,
        to_left,
        *x_parts(kv),
        *got,
        *y_parts(gu_quarter),
        *y_parts(down_quarter),
    )
    kv, got, gu_parts, down_parts = parts[:4], parts[4:7], parts[7:11], parts[11:]
    mixed = (mixed[0], shift(to_right, "z", 1), shift(to_left, "z", -1))
    own, to_ylo, to_yhi, to_cross = y_split(oq, kv)
    tokens_grad, gate_grad, up_grad, down_grad = inner(
        got, tokens, dhidden, pre_row, gu_parts, down_parts
    )
    tokens_grad, *parts = together(
        tokens_grad, own, swap(to_ylo, "ylo"), swap(to_yhi, "yhi"), cross(to_cross), *mixed
    )
    parts, mixed = parts[:4], parts[4:]
    out_grad, q_grad, k_grad, v_grad, block_output, pre, mid, heads_q, heads_k = last_sum(
        info, parts, mixed, hidden
    )
    return (
        block_output,
        tokens_grad,
        pre[0],
        mid[0],
        heads_q[0],
        heads_k[0],
        q_grad,
        k_grad,
        v_grad,
        out_grad,
        gate_grad,
        up_grad,
        down_grad,
    )


def solution(mesh):
    torus = Mesh(mesh.devices.reshape(4, 2, 2, 4, 2), ("x", "ylo", "core", "z", "yhi"))
    return jax.shard_map(
        body,
        mesh=torus,
        in_specs=(
            P(ALL, None),
            P(ALL, None),
            P(WIDE, None),
            P(),
            P(),
            P(),
            P(),
            P(None, NARROW),
            P(None, NARROW),
            P(None, NARROW),
            P(NARROW, None),
            P(None, NARROW),
            P(None, NARROW),
            P(NARROW, None),
        ),
        out_specs=(
            P(ALL, None),
            P(ALL, None),
            P(WIDE),
            P(WIDE),
            P(WIDE),
            P(WIDE),
            P(WIDE, NARROW),
            P(WIDE, NARROW),
            P(WIDE, NARROW),
            P(NARROW, WIDE),
            P(WIDE, NARROW),
            P(WIDE, NARROW),
            P(NARROW, WIDE),
        ),
        check_vma=False,
    )
```

```python
import functools
import math

import jax
import jax.numpy as jnp
from jax import lax
from jax.experimental import pallas as pl
from jax.experimental.pallas import tpu as pltpu
from jax.sharding import Mesh
from jax.sharding import PartitionSpec as P

NARROW = ("z", "yhi")
WIDE = ("x", "ylo", "core")
ALL = WIDE + NARROW

EPS = 1e-06
ROPE_BASE = 1000000.0
LOG2E = math.log2(math.e)
F32 = jnp.float32
BF16 = jnp.bfloat16


def dot(a, b, ca, cb):
    return lax.dot_general(a, b, (((ca,), (cb,)), ((), ())), preferred_element_type=F32)


def swap(v, axis):
    return lax.ppermute(v, axis, [(0, 1), (1, 0)])


def cross(v):
    return lax.ppermute(v, ("ylo", "yhi"), [(0, 3), (3, 0), (1, 2), (2, 1)])


def shift(v, axis, by):
    return lax.ppermute(v, axis, [(i, (i + by) % 4) for i in range(4)])


def shift_x(v, by):
    return shift(v, "x", by)


def neighbours_z(piece):
    return shift(piece, "z", 1), shift(piece, "z", -1)


def far_z(left, right):
    return shift(left[:64], "z", 1), shift(right[64:], "z", -1)


def gather_z(piece):
    left, right = neighbours_z(piece)
    return piece, left, right, *far_z(left, right)


def gather_z_directly(piece):
    far = shift(piece, "z", 2)
    return piece, shift(piece, "z", 1), shift(piece, "z", -1), far


def scatter_far(terms):
    return shift(terms[3], "z", 1), shift(terms[4], "z", -1)


def scatter_near(info, terms, far):
    to_right, to_left = relay(info, terms, far)
    return terms[0], shift(to_right, "z", 1), shift(to_left, "z", -1)


def together(*values):
    return lax.optimization_barrier(values)


def vmem_spec():
    return pl.BlockSpec()


def smem_spec():
    return pl.BlockSpec(memory_space=pltpu.SMEM)


def params():
    return pltpu.CompilerParams(vmem_limit_bytes=58 * 2**20)


def shape(*dims, kind=BF16):
    return jax.ShapeDtypeStruct(dims, kind)


def features_of(info, c, t, ylo, turned):
    core = info[0] if c == 0 else 1 - info[0]
    tile = (info[1] + t) & 3 if turned else t
    return pl.ds(pl.multiple_of(((tile * 2 + ylo) * 2 + core) * 128, 128), 128)


def piece_moves(info, pieces, dst):
    own, left, right, *rest = pieces
    far = ((info[3] + 2) & 3) * 128
    if len(rest) == 1:
        halves = [(rest[0], dst.at[at_z(info, 2)])]
    else:
        halves = [
            (part, dst.at[pl.ds(pl.multiple_of(far + 64 * i, 64), 64)])
            for i, part in enumerate(rest)
        ]
    return halves + [
        (own, dst.at[at_z(info, 0)]),
        (left, dst.at[at_z(info, 3)]),
        (right, dst.at[at_z(info, 1)]),
    ]


def tile_moves(info, tiles, lanes, dst, turned):
    moves = []
    for c, tile in enumerate(tiles):
        for t in range(4):
            for ylo in range(2):
                rows = slice(128 * ylo, 128 * (ylo + 1))
                moves.append((tile.at[t, rows, lanes], dst.at[features_of(info, c, t, ylo, turned)]))
    return moves


def start(moves, sems, first):
    copies = [
        pltpu.make_async_copy(a, b, sems.at[first + i]) for i, (a, b) in enumerate(moves)
    ]
    for copy in copies:
        copy.start()
    return copies


def wait(copies):
    for copy in copies:
        copy.wait()


def any_spec():
    return pl.BlockSpec(memory_space=pl.ANY)


def place(info, pieces, dst):
    z = info[3]

    def rows(by, first, count):
        return pl.ds(pl.multiple_of(((z + by) & 3) * 128 + first, 64), count)

    own, left, right, far_0, far_1 = pieces
    dst[rows(0, 0, 128), :] = own[...]
    dst[rows(3, 0, 128), :] = left[...]
    dst[rows(1, 0, 128), :] = right[...]
    dst[rows(2, 0, 64), :] = far_0[...]
    dst[rows(2, 64, 64), :] = far_1[...]


def block_of(info, j, how):
    if how != "s" and how != "x":
        return j
    x = (info[1] + j // 2) & 3 if how == "x" else j // 2
    return x * 2 + (info[4] if j % 2 == 0 else 1 - info[4])


def turned_rows(info, pieces, core, how, dst):
    own, left, right, *rest = pieces
    z = info[3]
    for j in range(8):
        block = 2 * block_of(info, j, how) + core
        lanes = pl.ds(pl.multiple_of(block * 128, 128), 128)
        far = [part[:, lanes] for part in rest]
        far = far[0] if len(far) == 1 else jnp.concatenate(far, axis=0)
        for by, block in ((0, own[:, lanes]), (3, left[:, lanes]), (1, right[:, lanes]), (2, far)):
            at = pl.ds(pl.multiple_of(((z + by) & 3) * 128, 128), 128)
            dst[128 * j : 128 * (j + 1), at] = block.T


def take_tiles(info, src, dst, turned):
    for c in range(2):
        for t in range(4):
            for ylo in range(2):
                at = (c * 4 + t) * 256 + ylo * 128
                dst[:, at : at + 128] = src[:, features_of(info, c, t, ylo, turned)]


def add_tile(info, acc, c, t, value, turned):
    for ylo in range(2):
        acc[:, features_of(info, c, t, ylo, turned)] += value[:, ylo * 128 : (ylo + 1) * 128]


def inverse_rms(v):
    return lax.rsqrt(jnp.mean(v * v, axis=1, keepdims=True) + EPS)


def norm_back(d, v, inverse, gain):
    n = v * inverse
    dn = d * gain
    return inverse * (dn - n * jnp.mean(dn * n, axis=1, keepdims=True))


def add_up(refs):
    total = refs[0][...].astype(F32)
    for ref in refs[1:]:
        total = total + ref[...].astype(F32)
    return total


def write_terms(info, value, outs):
    for by, out in ((0, outs[0]), (1, outs[1]), (3, outs[2])):
        out[...] = value(at_z(info, by))
    far = value(at_z(info, 2))
    outs[3][...] = far[:64, :]
    outs[4][...] = far[64:, :]


def terms_shape():
    return [shape(128, 2048)] * 3 + [shape(64, 2048)] * 2


def relay_kernel(right_ref, left_ref, far_0, far_1, to_right, to_left):
    to_right[:64, :] = (right_ref[:64, :].astype(F32) + far_0[...].astype(F32)).astype(BF16)
    to_right[64:, :] = right_ref[64:, :]
    to_left[:64, :] = left_ref[:64, :]
    to_left[64:, :] = (left_ref[64:, :].astype(F32) + far_1[...].astype(F32)).astype(BF16)


def relay(info, terms, far):
    return pl.pallas_call(
        relay_kernel,
        out_shape=[shape(128, 2048)] * 2,
        in_specs=[vmem_spec()] * 4,
        out_specs=[vmem_spec()] * 2,
        compiler_params=params(),
        name="relay",
    )(terms[1], terms[2], *far)


def at_z(info, by):
    return pl.ds(pl.multiple_of(((info[3] + by) & 3) * 128, 128), 128)


def small_pieces_kernel(info, q_ref, k_ref, v_ref, o_ref, qkv_ref, out_ref):
    qkv_ref[:, :256] = q_ref[...]
    qkv_ref[:, 256:384] = k_ref[...]
    qkv_ref[:, 384:] = v_ref[...]
    out_ref[...] = o_ref[...].T


def large_pieces_kernel(info, g_ref, u_ref, d_ref, gu_ref, down_ref):
    gu_ref[:, :768] = g_ref[...]
    gu_ref[:, 768:] = u_ref[...]
    down_ref[...] = d_ref[...].T


def pieces_of(kernel, name, info, weights, turned, widths):
    def at(i, info):
        return (2 * info[1] + i) * 2 + info[0]

    def rows(i, info):
        return at(i, info), 0

    def columns(i, info):
        return 0, at(i, info)

    def out(i, info):
        return i, 0

    return pl.pallas_call(
        kernel,
        grid_spec=pltpu.PrefetchScalarGridSpec(
            num_scalar_prefetch=1,
            grid=(2,),
            in_specs=[pl.BlockSpec((128, w.shape[1]), rows) for w in weights]
            + [pl.BlockSpec((turned.shape[0], 128), columns)],
            out_specs=[pl.BlockSpec((128, w), out) for w in widths],
        ),
        out_shape=[shape(256, w) for w in widths],
        compiler_params=params(),
        name=name,
    )(info, *weights, turned)


def first_norm_kernel(tokens_ref, gain_ref, out_ref):
    x = tokens_ref[...].astype(F32)
    normed = (x * inverse_rms(x) * gain_ref[...]).astype(BF16)
    out_ref[...] = normed


def first_norm(tokens, gain):
    return pl.pallas_call(
        first_norm_kernel,
        out_shape=shape(128, 2048),
        in_specs=[vmem_spec()] * 2,
        out_specs=vmem_spec(),
        compiler_params=params(),
        name="first_norm",
    )(tokens, gain)


def mid_norm_kernel(g0, g1, g2, tokens_ref, gain_ref, hidden_ref, out_ref):
    hidden = tokens_ref[...].astype(F32) + add_up((g0, g1, g2))
    hidden_ref[...] = hidden
    normed = (hidden * inverse_rms(hidden) * gain_ref[...]).astype(BF16)
    out_ref[...] = normed


def mid_norm(got, tokens, gain):
    return pl.pallas_call(
        mid_norm_kernel,
        out_shape=(shape(128, 2048, kind=F32), shape(128, 2048)),
        in_specs=[vmem_spec()] * 5,
        out_specs=[vmem_spec()] * 2,
        compiler_params=params(),
        name="mid_norm",
    )(*got, tokens, gain)


def mid_norm_back_kernel(g0, g1, g2, cot_ref, hidden_ref, gain_ref, dhidden_ref, out_ref, dgain_ref):
    hidden = hidden_ref[...]
    inverse = inverse_rms(hidden)
    dmid = add_up((g0, g1, g2))
    dgain_ref[...] = jnp.sum(dmid * (hidden * inverse), axis=0, keepdims=True)
    dhidden = cot_ref[...].astype(F32) + norm_back(dmid, hidden, inverse, gain_ref[...])
    dhidden_ref[...] = dhidden
    out_ref[...] = dhidden.astype(BF16)


def mid_norm_back(got, cot, hidden, gain):
    return pl.pallas_call(
        mid_norm_back_kernel,
        out_shape=(
            shape(128, 2048, kind=F32),
            shape(128, 2048),
            shape(1, 2048, kind=F32),
        ),
        in_specs=[vmem_spec()] * 6,
        out_specs=[vmem_spec()] * 3,
        compiler_params=params(),
        name="mid_norm_back",
    )(*got, cot, hidden, gain)


def first_norm_back_kernel(g0, g1, g2, tokens_ref, dhidden_ref, gain_ref, out_ref):
    x = tokens_ref[...].astype(F32)
    d = norm_back(add_up((g0, g1, g2)), x, inverse_rms(x), gain_ref[...])
    out_ref[...] = (dhidden_ref[...] + d).astype(BF16)


def project_kernel(
    info, a0, a1, a2, a3, a4, wq, wk, wv, p0, p1, cos_ref, sin_ref, qgain_ref, kgain_ref,
    rawq_ref, rawk_ref, q_ref, kv_ref, normed, w, raw, sems,
):
    moves = piece_moves(info, (a0, a1, a2, a3, a4), normed)
    moves += [(wq, w.at[:, :256]), (wk, w.at[:, 256:384]), (wv, w.at[:, 384:512])]
    copies = start(moves, sems, 0)
    more = start(tile_moves(info, (p0, p1), slice(None), w.at[:, 512:], True), sems, 8)
    wait(copies)
    raw[:, :512] = dot(normed[...], w[:, :512], 1, 0)
    wait(more)
    raw[:, 512:] = dot(normed[...], w[:, 512:], 1, 0)
    cosine, sine = cos_ref[...], sin_ref[...]

    def prep(v, gain):
        return rope(v * inverse_rms(v) * gain, cosine, sine).astype(BF16)

    for g in range(2):
        at, bt = 512 * g, 256 * g
        for h in range(2):
            v = raw[:, at + 128 * h : at + 128 * (h + 1)]
            rawq_ref[:, bt + 128 * h : bt + 128 * (h + 1)] = v.astype(BF16)
            q_ref[:, bt + 128 * h : bt + 128 * (h + 1)] = prep(v, qgain_ref[...])
        v = raw[:, at + 256 : at + 384]
        rawk_ref[:, 128 * g : 128 * (g + 1)] = v.astype(BF16)
        kv_ref[:, bt : bt + 128] = prep(v, kgain_ref[...])
        kv_ref[:, bt + 128 : bt + 256] = raw[:, at + 384 : at + 512].astype(BF16)


def project(info, pieces, wq, wk, wv, p0, p1, cosine, sine, qgain, kgain):
    return pl.pallas_call(
        project_kernel,
        out_shape=(shape(512, 512), shape(512, 256), shape(512, 512), shape(512, 512)),
        in_specs=[smem_spec()] + [any_spec()] * 10 + [vmem_spec()] * 4,
        out_specs=[vmem_spec()] * 4,
        scratch_shapes=[
            pltpu.VMEM((512, 2048), BF16),
            pltpu.VMEM((2048, 1024), BF16),
            pltpu.VMEM((512, 1024), F32),
            pltpu.SemaphoreType.DMA((24,)),
        ],
        compiler_params=params(),
        name="project",
    )(info, *pieces, wq, wk, wv, p0, p1, cosine, sine, qgain, kgain)


def attended_kernel(info, ctx_ref, own_ref, p0_ref, p1_ref, o0, o1, o2, o3, o4, acc):
    acc[...] = dot(ctx_ref[:, :256], own_ref[...], 1, 0)
    par = ctx_ref[:, 256:]
    for c, p in enumerate((p0_ref, p1_ref)):
        for t in range(4):
            add_tile(info, acc, c, t, dot(par, p[t], 1, 1), True)
    write_terms(info, lambda rows: acc[rows, :].astype(BF16), (o0, o1, o2, o3, o4))


def attended_partial(info, ctx, own, p0, p1):
    return pl.pallas_call(
        attended_kernel,
        out_shape=terms_shape(),
        in_specs=[smem_spec()] + [vmem_spec()] * 4,
        out_specs=[vmem_spec()] * 5,
        scratch_shapes=[pltpu.VMEM((512, 2048), F32)],
        compiler_params=params(),
        name="attended",
    )(info, ctx, own, p0, p1)


def dcontext_kernel(info, d0, d1, d2, d3, d4, own_ref, p0_ref, p1_ref, out_ref, datt, tiles):
    place(info, (d0, d1, d2, d3, d4), datt)
    take_tiles(info, datt, tiles, True)
    out_ref[:, :256] = dot(datt[...], own_ref[...], 1, 1).astype(BF16)
    par = None
    for c, p in enumerate((p0_ref, p1_ref)):
        for t in range(4):
            at = (c * 4 + t) * 256
            part = dot(tiles[:, at : at + 256], p[t], 1, 0)
            par = part if par is None else par + part
    out_ref[:, 256:] = par.astype(BF16)


def dcontext(info, pieces, own, p0, p1):
    return pl.pallas_call(
        dcontext_kernel,
        out_shape=shape(512, 512),
        in_specs=[smem_spec()] + [vmem_spec()] * 8,
        out_specs=vmem_spec(),
        scratch_shapes=[pltpu.VMEM((512, 2048), BF16), pltpu.VMEM((512, 2048), BF16)],
        compiler_params=params(),
        name="dcontext",
    )(info, *pieces, own, p0, p1)


def mlp_kernel(
    info, m0, m1, m2, m3, m4, c0, c1, c2, c3, gate_any, up_any, down_any, p0, p1,
    product_ref, dgu_ref, o0, o1, o2, o3, o4, mid, cot, acc, w, d, par, sems,
):
    moves = piece_moves(info, (m0, m1, m2, m3, m4), mid)
    moves += [(gate_any, w.at[:, :768]), (up_any, w.at[:, 768:])]
    first = start(moves, sems, 0)
    moves = piece_moves(info, (c0, c1, c2, c3), cot) + [(down_any, d)]
    second = start(moves, sems, 7)
    third = start(tile_moves(info, (p0, p1), slice(None), par, False), sems, 13)

    def middle(gu, dproduct, at):
        gate, up = gu[:, :768], gu[:, 768:]
        sig = jax.nn.sigmoid(gate)
        silu = gate * sig
        product_ref[:, at : at + 768] = (silu * up).astype(BF16)
        dgate = (dproduct * up * sig * (1.0 + gate * (1.0 - sig))).astype(BF16)
        dgu_ref[:, 2 * at : 2 * at + 768] = dgate
        dgu_ref[:, 2 * at + 768 : 2 * at + 1536] = (dproduct * silu).astype(BF16)

    wait(first)
    gu = dot(mid[...], w[...], 1, 0)
    wait(second)
    middle(gu, dot(cot[...], d[...], 1, 1), 0)
    acc[...] = dot(w[...], dgu_ref[:, :1536], 1, 1)
    wait(third)
    gu = dot(mid[...], par[:, :1536], 1, 0)
    middle(gu, dot(cot[...], par[:, 1536:], 1, 0), 768)
    acc[...] += dot(par[:, :1536], dgu_ref[:, 1536:], 1, 1)
    write_terms(info, lambda rows: acc[:, rows].astype(BF16).T, (o0, o1, o2, o3, o4))


def mlp(info, mid, cot, gate, up, down, p0, p1):
    return pl.pallas_call(
        mlp_kernel,
        out_shape=[shape(512, 1536), shape(512, 3072)] + terms_shape(),
        in_specs=[smem_spec()] + [any_spec()] * 14,
        out_specs=[vmem_spec()] * 7,
        scratch_shapes=[
            pltpu.VMEM((512, 2048), BF16),
            pltpu.VMEM((512, 2048), BF16),
            pltpu.VMEM((2048, 512), F32),
            pltpu.VMEM((2048, 1536), BF16),
            pltpu.VMEM((768, 2048), BF16),
            pltpu.VMEM((2048, 2304), BF16),
            pltpu.SemaphoreType.DMA((29,)),
        ],
        compiler_params=params(),
        name="mlp",
    )(info, *mid, *cot, gate, up, down, p0, p1)


def mixed_kernel(info, own, p0, p1, product_ref, o0, o1, o2, o3, o4, acc, w, par, sems):
    copies = start([(own, w)], sems, 0)
    lanes = slice(1536, 2304)
    more = start(tile_moves(info, (p0, p1), lanes, par, False), sems, 1)
    wait(copies)
    acc[...] = dot(product_ref[:, :768], w[...], 1, 0)
    wait(more)
    acc[...] += dot(product_ref[:, 768:], par[...], 1, 1)
    write_terms(info, lambda rows: acc[rows, :].astype(BF16), (o0, o1, o2, o3, o4))


def mixed_partial(info, product, own, p0, p1):
    return pl.pallas_call(
        mixed_kernel,
        out_shape=terms_shape(),
        in_specs=[smem_spec()] + [any_spec()] * 3 + [vmem_spec()],
        out_specs=[vmem_spec()] * 5,
        scratch_shapes=[
            pltpu.VMEM((512, 2048), F32),
            pltpu.VMEM((768, 2048), BF16),
            pltpu.VMEM((2048, 768), BF16),
            pltpu.SemaphoreType.DMA((17,)),
        ],
        compiler_params=params(),
        name="mixed",
    )(info, own, p0, p1, product)


def dpre_kernel(
    info, wq, wk, wv, p0, p1, a0, a1, a2, a3, a4, mine_ref, got_ref, dq_ref, rawk_ref, cos_ref,
    sin_ref, kgain_ref, gain_ref, mid_ref, dqgain_ref, dkv_ref, gains_ref, o0, o1, o2, o3, o4,
    acc, normed, low, w, d_all, sems,
):
    copies = start([(wq, w.at[:, :256]), (wk, w.at[:, 256:384]), (wv, w.at[:, 384:512])], sems, 0)
    copies += start(tile_moves(info, (p0, p1), slice(None), w.at[:, 512:], True), sems, 3)
    more = start(piece_moves(info, (a0, a1, a2, a3, a4), normed), sems, 19)
    dgain = jnp.zeros((1, 128), F32)
    for g in range(2):
        at, bt, og = 256 * g, 256 * g + 128, 256 * (1 - g)
        dk = mine_ref[:, at:bt] + got_ref[:, og : og + 128].astype(F32)
        raw = rawk_ref[:, 128 * g : 128 * (g + 1)].astype(F32)
        d, part = head_back(dk, raw, kgain_ref[...], cos_ref[...], sin_ref[...])
        dkv_ref[:, at:bt] = d
        dgain = dgain + part
        dv = mine_ref[:, bt : bt + 128] + got_ref[:, og + 128 : og + 256].astype(F32)
        dkv_ref[:, bt : bt + 128] = dv.astype(BF16)
        d_all[:, 512 * g : 512 * g + 256] = dq_ref[:, at : at + 256]
        d_all[:, 512 * g + 256 : 512 * g + 512] = dkv_ref[:, at : at + 256]
    wait(copies)
    acc[...] = dot(w[...], d_all[...], 1, 1)
    wait(more)
    total = jnp.zeros((1, 2048), F32)
    for i in range(4):
        turned = acc[:, 128 * i : 128 * (i + 1)].astype(BF16).T
        part = turned.astype(F32) * normed[128 * i : 128 * (i + 1), :].astype(F32)
        total = total + jnp.sum(part, axis=0, keepdims=True)
        low[128 * i : 128 * (i + 1), :] = turned
    total = total / gain_ref[...]
    for i in range(16):
        row, lanes = slice(i // 2, i // 2 + 1), slice(128 * i, 128 * (i + 1))
        ref = gains_ref.at[jnp.where(info[0] == i % 2, 0, 1)]
        ref[row, :128] = total[:, lanes]
        ref[row, 128:256] = mid_ref[:, lanes]
        ref[row, 256:384] = dqgain_ref[...]
        ref[row, 384:] = dgain
    write_terms(info, lambda rows: low[rows, :], (o0, o1, o2, o3, o4))


def dpre_partial(
    info, mine, got, dq, rawk, cosine, sine, kgain, wq, wk, wv, p0, p1, pieces, *gains
):
    return pl.pallas_call(
        dpre_kernel,
        out_shape=(shape(512, 512), shape(2, 8, 512, kind=F32), *terms_shape()),
        in_specs=[smem_spec()] + [any_spec()] * 10 + [vmem_spec()] * 10,
        out_specs=[vmem_spec()] * 7,
        scratch_shapes=[
            pltpu.VMEM((2048, 512), F32),
            pltpu.VMEM((512, 2048), BF16),
            pltpu.VMEM((512, 2048), BF16),
            pltpu.VMEM((2048, 1024), BF16),
            pltpu.VMEM((512, 1024), BF16),
            pltpu.SemaphoreType.DMA((24,)),
        ],
        compiler_params=params(),
        name="dpre",
    )(info, wq, wk, wv, p0, p1, *pieces, mine, got, dq, rawk, cosine, sine, kgain, *gains)


def grad_kernel(info, *refs, plan):
    step = pl.program_id(0)
    turned = refs[-1]
    at_in, at_out = 0, sum(p[3] for p in plan)
    for n, (keep, how, starts, count_in, count_out, after) in enumerate(plan):
        ins = refs[at_in : at_in + count_in]
        outs = refs[at_out : at_out + count_out]
        at_in, at_out = at_in + count_in, at_out + count_out
        core = info[0] if keep else 1 - info[0]
        ends = starts[1:] + ((plan[n + 1][2][0],) if n + 1 < len(plan) else (None,))
        for job, (start, end) in enumerate(zip(starts, ends)):
            count = (len(ins) - after) // len(starts)
            job_ins = ins[count * job : count * (job + 1)]
            pieces, b = job_ins[:-1], job_ins[-1]

            @pl.when(step == start)
            def turn(pieces=pieces, core=core, how=how):
                turned_rows(info, pieces, core, how, turned)

            inside = step >= start if end is None else (step >= start) & (step < end)

            @pl.when(inside)
            def multiply(
                b=b, keep=keep, how=how, ins=ins, outs=outs, starts=starts, after=after
            ):
                total = dot(turned[...], b[...], 1, 0)
                if not keep:
                    outs[0][...] = total.astype(BF16)
                    return
                got = ins[len(ins) - after]
                if how == "y":
                    total = (total + got[...].astype(F32)).astype(BF16)
                    for par in range(2):

                        @pl.when(step == starts[0] + par)
                        def write(par=par):
                            yhi = info[2] if par == 0 else 1 - info[2]
                            for j in range(8):
                                rows = slice(128 * (j // 2), 128 * (j // 2 + 1))
                                out = outs[0].at[2 * (j % 2) + yhi]
                                out[rows, :] = total[128 * j : 128 * (j + 1), :]

                    return
                for j in range(8):
                    block = block_of(info, j, how)
                    rows = pl.ds(pl.multiple_of(block * 128, 128), 128)
                    part = total[128 * j : 128 * (j + 1), :] + got[rows, :].astype(F32)
                    if how == "s":
                        outs[0][128 * j : 128 * (j + 1), :] = part.astype(BF16)
                        continue
                    out, i = outs[j // 2], j % 2
                    out[128 * i : 128 * (i + 1), :] = part.astype(BF16)
                    mine, other = ins[-2], ins[-1]
                    row = mine[pl.ds(block, 1), :] + other[pl.ds(block, 1), :]
                    row = jnp.concatenate([row, jnp.zeros((15, 512), F32)], axis=0)
                    out[256 + 16 * i : 272 + 16 * i, :] = row.astype(BF16)


def grads(info, *bundles):
    plan, in_specs, out_specs, out_shape, args, at = [], [], [], [], [], 0

    def whole(rows):
        return pl.BlockSpec((rows, 2048), lambda i: (0, 0))

    for how, got, jobs, *gains in bundles:
        keep = got is not None
        width = 768 if jobs[0][1].shape[1] % 768 == 0 else 512
        first, starts, before = at, [], len(in_specs)

        def tile_of(start, count):
            return lambda i: (0, jnp.clip(i - start, 0, count - 1))

        for pieces, b in jobs:
            count = b.shape[1] // width
            starts.append(at)
            in_specs += [whole(piece.shape[0]) for piece in pieces]
            in_specs.append(pl.BlockSpec((512, width), tile_of(at, count)))
            args += [*pieces, b]
            at += count
        tile, columns = tile_of(first, at - first), (at - first) * width
        if keep:
            in_specs.append(pl.BlockSpec((1024, width), tile))
            args.append(got)
            in_specs += [pl.BlockSpec(v.shape, lambda i: (0, 0)) for v in gains]
            args += gains
        count_out = 1
        if how == "y":
            out_shape.append(shape(4, 512, width))
            out_specs.append(pl.BlockSpec((4, 512, width), lambda i: (0, 0, 0)))
        elif how == "x":
            out_shape += [shape(288, width)] * 4
            out_specs += [pl.BlockSpec((288, width), lambda i: (0, 0))] * 4
            count_out = 4
        else:
            out_shape.append(shape(1024, columns))
            out_specs.append(pl.BlockSpec((1024, width), tile))
        plan.append((keep, how, tuple(starts), len(in_specs) - before, count_out, keep + len(gains)))
    out = pl.pallas_call(
        functools.partial(grad_kernel, plan=tuple(plan)),
        grid=(at,),
        out_shape=out_shape,
        in_specs=[smem_spec()] + in_specs,
        out_specs=out_specs,
        scratch_shapes=[pltpu.VMEM((1024, 512), BF16)],
        compiler_params=params(),
        name="grads",
    )(info, *args)
    results, at = [], 0
    for _, _, _, _, count_out, _ in plan:
        results.append(out[at] if count_out == 1 else list(out[at : at + count_out]))
        at += count_out
    return results[0] if len(results) == 1 else results


def y_parts(quarter):
    c = quarter.shape[1] // 2
    return (
        quarter[:128, :c],
        swap(quarter[128:, :c], "ylo"),
        swap(quarter[:128, c:], "yhi"),
        cross(quarter[128:, c:]),
    )


def x_parts(parts):
    return parts[0], shift_x(parts[1], 1), shift_x(parts[2], 2), shift_x(parts[3], -1)


def y_split_kernel(oq_ref, k0, k1, k2, k3, mine, to_ylo, to_yhi, to_cross, kv, oq):
    kv[...] = add_up((k0, k1, k2, k3))
    oq[...] = add_up([oq_ref.at[i] for i in range(4)])
    for i, out in enumerate((mine, to_ylo, to_yhi, to_cross)):
        other, par = i % 2, i // 2
        rows = slice(128 * other, 128 * (other + 1))
        out[:128, :256] = oq[rows, 256 * par : 256 * par + 256].astype(out.dtype)
        out[:128, 256:512] = oq[rows, 512 + 256 * par : 768 + 256 * par].astype(out.dtype)
        out[:128, 512:] = kv[rows, 256 * par : 256 * par + 256].astype(out.dtype)
        out[128:, :512] = kv[256 + 16 * other : 272 + 16 * other, :].astype(out.dtype)
        out[128:, 512:] = jnp.zeros((16, 256), out.dtype)


def y_split(oq, kv):
    return pl.pallas_call(
        y_split_kernel,
        out_shape=[shape(144, 768, kind=F32)] + [shape(144, 768)] * 3,
        in_specs=[vmem_spec()] * 5,
        out_specs=[vmem_spec()] * 4,
        scratch_shapes=[pltpu.VMEM((288, 512), F32), pltpu.VMEM((256, 1024), F32)],
        compiler_params=params(),
        name="y_split",
    )(oq, *kv)


def last_sum_kernel(info, *refs):
    out, q, k, v, block, pre, mid, qgain, kgain = refs[8:]
    total = add_up(refs[:4])
    out[...] = total[:128, :256].T
    q[...] = total[:128, 256:512]
    k[...] = total[:128, 512:640]
    v[...] = total[:128, 640:]
    pre[...] = total[128:129, :128]
    mid[...] = total[128:129, 128:256]
    w = (info[1] * 2 + info[4]) * 2 + info[0]
    back = (128 - 8 * w) & 127
    qgain[...] = pltpu.roll(total[128:136, 256:384], back, 1)[:1, :8]
    kgain[...] = pltpu.roll(total[128:136, 384:512], back, 1)[:1, :8]
    block[...] = add_up(refs[4:8]).astype(BF16)


def last_sum(info, parts, mixed, hidden):
    dims = ((256, 128), (128, 256), (128, 128), (128, 128))
    gains = ((1, 128), (1, 128), (1, 8), (1, 8))
    return pl.pallas_call(
        last_sum_kernel,
        out_shape=[shape(*d, kind=F32) for d in dims]
        + [shape(128, 2048)]
        + [shape(*d, kind=F32) for d in gains],
        in_specs=[smem_spec()] + [vmem_spec()] * 8,
        out_specs=[vmem_spec()] * 9,
        compiler_params=params(),
        name="last_sum",
    )(info, *parts, hidden, *mixed)


def inner_kernel(*refs):
    first_norm_back_kernel(*refs[:6], refs[14])
    gate, up, down = refs[15:]
    total = add_up(refs[6:10])
    gate[...] = total[:, :768]
    up[...] = total[:, 768:]
    down[...] = add_up(refs[10:14]).T


def inner(got, tokens, dhidden, gain, gu_parts, down_parts):
    dims = ((128, 768), (128, 768), (768, 128))
    return pl.pallas_call(
        inner_kernel,
        out_shape=[shape(128, 2048)] + [shape(*d, kind=F32) for d in dims],
        in_specs=[vmem_spec()] * 14,
        out_specs=[vmem_spec()] * 4,
        compiler_params=params(),
        name="inner",
    )(*got, tokens, dhidden, gain, *gu_parts, *down_parts)


def rope(v, cosine, sine):
    return v * cosine + pltpu.roll(v, 64, 1) * sine


def rope_back(v, cosine, sine):
    return v * cosine - pltpu.roll(v, 64, 1) * sine


def place_keys(y, kv_ref, other_ref, k_all, v_all):
    for g in range(2):
        for z in range(4):
            rows = slice(128 * z, 128 * (z + 1))
            at = pl.ds(pl.multiple_of(256 * z + 128 * y, 128), 128)
            bt = pl.ds(pl.multiple_of(256 * z + 128 * (1 - y), 128), 128)
            k_all[g, at, :] = kv_ref[rows, 256 * g : 256 * g + 128]
            v_all[g, at, :] = kv_ref[rows, 256 * g + 128 : 256 * g + 256]
            og = 256 * (1 - g)
            k_all[g, bt, :] = other_ref[rows, og : og + 128]
            v_all[g, bt, :] = other_ref[rows, og + 128 : og + 256]


def seen_by(y, z, begin):
    rows = 256 * (z + 1)
    key = lax.broadcasted_iota(jnp.int32, (rows, 256), 0)
    query = (lax.broadcasted_iota(jnp.int32, (rows, 256), 1) & 127) + (256 * z + 128 * y)
    return (key <= query) & (key >= begin)


def stacked(ref, z, g):
    rows = slice(128 * z, 128 * (z + 1))
    return jnp.concatenate(
        [ref[rows, 256 * g : 256 * g + 128], ref[rows, 256 * g + 128 : 256 * g + 256]], axis=0
    )


def attention_kernel(y_ref, q_ref, kv_ref, other_ref, begin_ref, ctx_ref, lse_ref, k_all, v_all):
    scale2 = 128**-0.5 * LOG2E
    y = y_ref[0]
    place_keys(y, kv_ref, other_ref, k_all, v_all)
    for g in range(2):
        v_t = v_all[g].T
        for z in range(4):
            rows = 256 * (z + 1)
            begin = begin_ref[:, 128 * z : 128 * (z + 1)]
            begin = jnp.concatenate([begin, begin], axis=1)
            s = dot(k_all[g, :rows, :], stacked(q_ref, z, g), 1, 1) * scale2
            s = jnp.where(seen_by(y, z, begin), s, -1e30)
            peak = jnp.max(s, axis=0, keepdims=True)
            expo = jnp.exp2(s - peak)
            total = jnp.sum(expo, axis=0, keepdims=True)
            weights = (expo * (1.0 / total)).astype(BF16)
            ctx = dot(v_t[:, :rows], weights, 1, 0).T.astype(BF16)
            for h in range(2):
                ctx_ref[
                    128 * z : 128 * (z + 1), 256 * g + 128 * h : 256 * g + 128 * (h + 1)
                ] = ctx[128 * h : 128 * (h + 1), :]
            lse_ref[4 * g + z : 4 * g + z + 1, :] = peak + jnp.log2(total)


def attention(y, q, kv, other, begin_row):
    return pl.pallas_call(
        attention_kernel,
        out_shape=(
            jax.ShapeDtypeStruct((512, 512), BF16),
            jax.ShapeDtypeStruct((8, 256), F32),
        ),
        in_specs=[smem_spec()] + [vmem_spec()] * 4,
        out_specs=[vmem_spec()] * 2,
        scratch_shapes=[pltpu.VMEM((2, 1024, 128), BF16), pltpu.VMEM((2, 1024, 128), BF16)],
        compiler_params=params(),
        name="attention",
    )(y, q, kv, other, begin_row)


def head_back(d, raw, gain, cosine, sine):
    dn = rope_back(d, cosine, sine)
    inverse = lax.rsqrt(jnp.mean(raw * raw, axis=1, keepdims=True) + EPS)
    n = raw * inverse
    dgain = jnp.sum(dn * n, axis=0, keepdims=True)
    dn = dn * gain
    draw = inverse * (dn - n * jnp.mean(dn * n, axis=1, keepdims=True))
    return draw.astype(BF16), dgain


def attention_back_kernel(
    y_ref, q_ref, kv_ref, other_ref, begin_ref, lse_ref, dctx_ref, raw_ref, cos_ref, sin_ref,
    qgain_ref, dq_ref, mine_ref, send_ref, dqgain_ref, k_all, v_all, dk_acc, dv_acc, dq_acc,
):
    scale = 128**-0.5
    scale2 = scale * LOG2E
    y = y_ref[0]
    place_keys(y, kv_ref, other_ref, k_all, v_all)
    dk_acc[...] = jnp.zeros_like(dk_acc)
    dv_acc[...] = jnp.zeros_like(dv_acc)
    for g in range(2):
        k_t = k_all[g].T
        for z in range(4):
            rows = 256 * (z + 1)
            begin = begin_ref[:, 128 * z : 128 * (z + 1)]
            begin = jnp.concatenate([begin, begin], axis=1)
            q = stacked(q_ref, z, g)
            dctx = stacked(dctx_ref, z, g)
            s = dot(k_all[g, :rows, :], q, 1, 1) * scale2
            s = s - lse_ref[4 * g + z : 4 * g + z + 1, :]
            probs = jnp.where(seen_by(y, z, begin), jnp.exp2(s), 0.0)
            dprobs = dot(v_all[g, :rows, :], dctx, 1, 1)
            inner = jnp.sum(probs * dprobs, axis=0, keepdims=True)
            dscores = (probs * (dprobs - inner) * scale).astype(BF16)
            dv_acc[g, :rows, :] += dot(probs.astype(BF16), dctx, 1, 0)
            dk_acc[g, :rows, :] += dot(dscores, q, 1, 0)
            dq = dot(k_t[:, :rows], dscores, 1, 0).T
            for h in range(2):
                dq_acc[
                    128 * z : 128 * (z + 1), 256 * g + 128 * h : 256 * g + 128 * (h + 1)
                ] = dq[128 * h : 128 * (h + 1), :]
    dgain = jnp.zeros((1, 128), F32)
    for g in range(2):
        for h in range(2):
            lanes = slice(256 * g + 128 * h, 256 * g + 128 * (h + 1))
            raw = raw_ref[:, lanes].astype(F32)
            d, part = head_back(
                dq_acc[:, lanes], raw, qgain_ref[...], cos_ref[...], sin_ref[...]
            )
            dq_ref[:, lanes] = d
            dgain = dgain + part
        for z in range(4):
            rows = slice(128 * z, 128 * (z + 1))
            at = pl.ds(pl.multiple_of(256 * z + 128 * y, 128), 128)
            bt = pl.ds(pl.multiple_of(256 * z + 128 * (1 - y), 128), 128)
            mine_ref[rows, 256 * g : 256 * g + 128] = dk_acc[g, at, :]
            mine_ref[rows, 256 * g + 128 : 256 * g + 256] = dv_acc[g, at, :]
            send_ref[rows, 256 * g : 256 * g + 128] = dk_acc[g, bt, :].astype(BF16)
            send_ref[rows, 256 * g + 128 : 256 * g + 256] = dv_acc[g, bt, :].astype(BF16)
    dqgain_ref[...] = dgain


def attention_back(y, q, kv, other, begin_row, lse, dctx, raw, cosine, sine, qgain):
    return pl.pallas_call(
        attention_back_kernel,
        out_shape=(
            jax.ShapeDtypeStruct((512, 512), BF16),
            jax.ShapeDtypeStruct((512, 512), F32),
            jax.ShapeDtypeStruct((512, 512), BF16),
            jax.ShapeDtypeStruct((1, 128), F32),
        ),
        in_specs=[smem_spec()] + [vmem_spec()] * 10,
        out_specs=[vmem_spec()] * 4,
        scratch_shapes=[
            pltpu.VMEM((2, 1024, 128), BF16),
            pltpu.VMEM((2, 1024, 128), BF16),
            pltpu.VMEM((2, 1024, 128), F32),
            pltpu.VMEM((2, 1024, 128), F32),
            pltpu.VMEM((512, 512), F32),
        ],
        compiler_params=params(),
        name="attention_back",
    )(y, q, kv, other, begin_row, lse, dctx, raw, cosine, sine, qgain)


def row_tables(lengths):
    ends = jnp.cumsum(lengths)
    starts = ends - lengths
    at = jnp.arange(512, dtype=jnp.int32)
    places = (at // 128) * 256 + at % 128 + lax.axis_index("yhi") * 128
    begin = jnp.max(jnp.where(starts[None, :] <= places[:, None], starts[None, :], 0), axis=1)
    offset = (places - begin).astype(F32)
    freq = jnp.exp(jnp.arange(64, dtype=F32) * (-2.0 * math.log(ROPE_BASE) / 128))
    angle = offset[:, None] * freq[None, :]
    cosine, sine = jnp.cos(angle), jnp.sin(angle)
    return (
        begin,
        jnp.concatenate([cosine, cosine], axis=1),
        jnp.concatenate([-sine, sine], axis=1),
    )


def body(
    tokens, cotangent, doc_lengths, pre_gain, mid_gain, query_gain, key_gain,
    query_weight, key_matrix, value_matrix, output_weight, gate_weight, up_weight, down_weight,
):
    info = jnp.stack([lax.axis_index(name) for name in ("core", "x", "yhi", "z", "ylo")])
    info = info.astype(jnp.int32)
    y = info[2:3]
    pre_row, mid_row = pre_gain[None, :], mid_gain[None, :]
    qg, kg = query_gain[None, :], key_gain[None, :]

    qkv_piece, out_piece = pieces_of(
        small_pieces_kernel,
        "small_pieces",
        info,
        (query_weight, key_matrix, value_matrix),
        output_weight,
        (512, 256),
    )
    normed = first_norm(tokens, pre_row)
    gu_piece, down_piece = pieces_of(
        large_pieces_kernel, "large_pieces", info, (gate_weight, up_weight), down_weight, (1536, 768)
    )
    normed = gather_z(normed)
    tile, out_tile, gu_piece, down_piece = together(
        cross(qkv_piece), cross(out_piece), gu_piece, down_piece
    )

    def x_tiles(tile):
        return [tile, shift_x(tile, -1), shift_x(tile, -2), shift_x(tile, 1)]

    begin, cosine, sine = row_tables(doc_lengths[0])
    begin_row = begin[None, :]
    *parts, cosine, sine, gu_piece, down_piece = together(
        *x_tiles(tile), *normed, cosine, sine, cross(gu_piece), down_piece
    )
    tiles, normed = parts[:4], tuple(parts[4:])
    qkv_0 = jnp.stack(tiles)
    qkv_0, qkv_1, out_tile = together(qkv_0, swap(qkv_0, "core"), out_tile)

    qkv = (query_weight, key_matrix, value_matrix, qkv_0, qkv_1)
    rawq, rawk, q, kv = project(info, normed, *qkv, cosine, sine, qg, kg)
    kv, down_piece, out_tile, left, right = together(
        kv, cross(down_piece), out_tile, *neighbours_z(cotangent)
    )
    mlp_0 = lax.all_gather(
        jnp.concatenate([gu_piece, down_piece], axis=1), "x", axis=0, tiled=False
    )
    kv_other, far, *tiles = together(
        swap(kv, "yhi"), shift(cotangent, "z", 2), *x_tiles(out_tile)
    )
    cot = (cotangent, left, right, far)
    out_0 = jnp.stack(tiles)
    out_1 = swap(out_0, "core")
    ctx, lse = attention(y, q, kv, kv_other, begin_row)
    terms = attended_partial(info, ctx, output_weight, out_0, out_1)
    got = scatter_near(info, terms, together(*scatter_far(terms)))
    g0, g1, g2, mlp_0 = together(*got, mlp_0)
    hidden, mid = mid_norm((g0, g1, g2), tokens, mid_row)
    left, right, mlp_1 = together(*neighbours_z(mid), swap(mlp_0, "core"))
    mid = (mid, left, right, *far_z(left, right))
    product, dgu, *terms = mlp(info, mid, cot, gate_weight, up_weight, down_weight, mlp_0, mlp_1)
    product, dgu, *terms = together(product, dgu, *terms)
    gu_jobs, down_jobs = [(mid, dgu)], [(cot, product)]
    far_0, far_1, gu_send = together(*scatter_far(terms), grads(info, (None, None, gu_jobs)))
    gu_got = swap(gu_send, "core")
    got = scatter_near(info, terms, (far_0, far_1))
    gu_half = grads(info, ("s", gu_got, gu_jobs))
    g0, g1, g2, gu_half = together(*got, gu_half)
    gu_quarter = lax.psum_scatter(gu_half, "x", scatter_dimension=0, tiled=True)
    dhidden, datt, mid_part = mid_norm_back((g0, g1, g2), cotangent, hidden, mid_row)
    mixed = mixed_partial(info, product, down_weight, mlp_0, mlp_1)
    left, right, *mixed = together(*neighbours_z(datt), *mixed)
    far_0, far_1, down_send = together(
        *far_z(left, right), grads(info, (None, None, down_jobs))
    )
    datt = (datt, left, right, far_0, far_1)
    dctx = dcontext(info, datt, output_weight, out_0, out_1)
    down_got = swap(down_send, "core")
    dq, dkv_mine, dkv_send, dqgain = attention_back(
        y, q, kv, kv_other, begin_row, lse, dctx, rawq, cosine, sine, qg
    )
    dq, dkv_mine, dkv_send, down_got = together(dq, dkv_mine, dkv_send, down_got)
    oq_jobs = [(datt, ctx), (normed, dq)]
    down_half, oq_send = grads(info, ("s", down_got, down_jobs), (None, None, oq_jobs))
    dkv_got, mixed_far_0, mixed_far_1, oq_send, down_half = together(
        swap(dkv_send, "yhi"), *scatter_far(mixed), oq_send, down_half
    )
    down_quarter = lax.psum_scatter(down_half, "x", scatter_dimension=0, tiled=True)
    dkv, gains, *terms = dpre_partial(
        info, dkv_mine, dkv_got, dq, rawk, cosine, sine, kg, *qkv, normed, pre_row, mid_part, dqgain
    )
    dkv, gains, oq_got, gu_quarter, *terms = together(
        dkv, gains, swap(oq_send, "core"), gu_quarter, *terms
    )
    kv_jobs = [(normed, dkv)]
    oq, kv_send = grads(info, ("s", oq_got, oq_jobs), (None, None, kv_jobs))
    far_0, far_1, kv_send, oq, gains, *others = together(
        *scatter_far(terms), kv_send, oq, gains, *(shift(gains, "z", i) for i in (1, -1, 2))
    )
    oq = lax.all_to_all(
        oq.reshape(4, 256, 1024), "x", split_axis=0, concat_axis=0, tiled=True
    )
    gains = (gains + others[0]) + (others[1] + others[2])
    got = scatter_near(info, terms, (far_0, far_1))
    kv = grads(info, ("x", swap(kv_send, "core"), kv_jobs, gains[0], swap(gains[1], "core")))
    *kv, down_quarter = together(*kv, down_quarter)
    to_right, to_left = relay(info, mixed, (mixed_far_0, mixed_far_1))
    oq, to_right, to_left, *parts = together(
        oq,
        to_right,
        to_left,
        *x_parts(kv),
        *got,
        *y_parts(gu_quarter),
        *y_parts(down_quarter),
    )
    kv, got, gu_parts, down_parts = parts[:4], parts[4:7], parts[7:11], parts[11:]
    mixed = (mixed[0], shift(to_right, "z", 1), shift(to_left, "z", -1))
    own, to_ylo, to_yhi, to_cross = y_split(oq, kv)
    tokens_grad, gate_grad, up_grad, down_grad = inner(
        got, tokens, dhidden, pre_row, gu_parts, down_parts
    )
    tokens_grad, *parts = together(
        tokens_grad, own, swap(to_ylo, "ylo"), swap(to_yhi, "yhi"), cross(to_cross), *mixed
    )
    parts, mixed = parts[:4], parts[4:]
    out_grad, q_grad, k_grad, v_grad, block_output, pre, mid, heads_q, heads_k = last_sum(
        info, parts, mixed, hidden
    )
    return (
        block_output,
        tokens_grad,
        pre[0],
        mid[0],
        heads_q[0],
        heads_k[0],
        q_grad,
        k_grad,
        v_grad,
        out_grad,
        gate_grad,
        up_grad,
        down_grad,
    )


def solution(mesh):
    torus = Mesh(mesh.devices.reshape(4, 2, 2, 4, 2), ("x", "ylo", "core", "z", "yhi"))
    return jax.shard_map(
        body,
        mesh=torus,
        in_specs=(
            P(ALL, None),
            P(ALL, None),
            P(WIDE, None),
            P(),
            P(),
            P(),
            P(),
            P(None, NARROW),
            P(None, NARROW),
            P(None, NARROW),
            P(NARROW, None),
            P(None, NARROW),
            P(None, NARROW),
            P(NARROW, None),
        ),
        out_specs=(
            P(ALL, None),
            P(ALL, None),
            P(WIDE),
            P(WIDE),
            P(WIDE),
            P(WIDE),
            P(WIDE, NARROW),
            P(WIDE, NARROW),
            P(WIDE, NARROW),
            P(NARROW, WIDE),
            P(WIDE, NARROW),
            P(WIDE, NARROW),
            P(NARROW, WIDE),
        ),
        check_vma=False,
    )
```
